32 devices in a mesh: dp: 2 (over x), expert: 16 (over z, y, core).
Axes of the slice: x: 2, y: 2, z: 4, core: 2. Of those that a mesh axis runs over, the one named last changes fastest.
Arguments:
- queries: bfloat16 [2048, 2048], P('expert', 'dp'), may hold values from -160 to 160
- kv_pool: bfloat16 [2, 128, 64, 2048], P(None, 'expert', None, 'dp'), may hold values from -6 to 6
- page_table: int32 [32, 4], P('expert'), may hold values from 0 to 127, as said below
- ctx_lens: int32 [2048], P('expert'), may hold values from 2 to 256, as said below
- w_out: bfloat16 [2048, 2048], P('dp', 'expert'), may hold values from -0.59765625 to 0.59765625
- residual: bfloat16 [2048, 2048], P(('expert', 'dp')), may hold values from -3 to 3
- moe_gain: float32 [2048], replicated, may hold values from 0.25 to 1.75
- expert_ids: int32 [2048, 6], P(('expert', 'dp')), may hold values from 0 to 15, all different within a row; in each aligned block of 64 rows (0 to 63, 64 to 127, ...) at most 48 rows name the same one
- route_weights: float32 [2048, 6], P(('expert', 'dp')), may hold values from 0.05 to 0.4
- w_gate: bfloat16 [16, 2048, 1408], P('expert', 'dp'), may hold values from -0.125 to 0.125
- w_up: bfloat16 [16, 2048, 1408], P('expert', 'dp'), may hold values from -0.125 to 0.125
- w_down: bfloat16 [16, 1408, 2048], P('expert', 'dp'), may hold values from -0.15625 to 0.15625
- final_gain: float32 [2048], replicated, may hold values from 0.25 to 1.75
Outputs:
- layer_out: bfloat16 [2048, 2048], P(('expert', 'dp'))
The draws below stay inside these ranges and needn't reach their ends.
Inputs may be any that keep to these rules, and one draw needn't show every extreme that they name: `page_table`: the 4 pages of sequence s are distinct pages of group s // 2, which owns pages g * 8 to g * 8 + 7; every page belongs to exactly one sequence. `ctx_lens`: the first row of every sequence reads all 256 positions. `expert_ids`: each row names 6 distinct experts; among the 64 rows of one device (aligned blocks of 64 rows) no expert is named more than 48 times.
All inputs are finite; a program needn't handle non-finite values.
Results may differ from the reference program's by a relative error of at most 0.017.
Values may be sent and summed in bfloat16 or wider, within the bound.
No kernel may reach another device: no remote copies, remote signals or barrier semaphores. Data moves between devices by JAX's collectives and lax.ppermute only.
A program may use at most 128 MiB of HBM per device.

```python
import math
import jax
import jax.numpy as jnp
import numpy as np
from jax import lax

D = 2048
HEADS = 16
HD = 128
FF = 1408
TOP = 6
R = 64
SEQ_ROWS = 64
PPS = 4
PAGE = 64
EXPERTS = 16
CTX = 256
CAP = 48
ROWS = 2048
SEQS = 32
PAGES_GRP = 8
POOL = 128
BLOCKS = 32


def page_layout(key):
    groups = POOL // PAGES_GRP
    keys = jax.random.split(jax.random.fold_in(key, 101), groups)

    def one_group(group_key):
        return jax.random.permutation(group_key, PAGES_GRP)
    perms = jax.vmap(one_group)(keys).astype(jnp.int32)
    base = (jnp.arange(groups, dtype=jnp.int32) * PAGES_GRP)[:, None]
    return (perms + base).reshape(SEQS, PPS)


def cache_values(key):
    raw = jnp.clip(jax.random.normal(jax.random.fold_in(key, 202), (2, POOL, PAGE, D), jnp.float32), -5.0, 5.0)
    return raw


def draw_page_table(key, part):
    return page_layout(key)


def draw_kv_pool(key, part):
    return cache_values(key).astype(jnp.bfloat16)


def draw_ctx_lens(key, part):
    lens = jax.random.randint(jax.random.fold_in(key, 404), (ROWS,), 2, CTX + 1, jnp.int32)
    leading = jnp.arange(ROWS, dtype=jnp.int32) % SEQ_ROWS == 0
    return jnp.where(leading, CTX, lens).astype(jnp.int32)


def draw_queries(key, part):
    raw = jnp.clip(jax.random.normal(jax.random.fold_in(key, 303), (ROWS, D), jnp.float32), -5.0, 5.0)
    return raw.astype(jnp.bfloat16)


def levels(stream_key, shape, cuts, low, top_value):
    loudness = 1.0
    for axis_at, parts in cuts:
        steps = jax.random.uniform(jax.random.fold_in(jax.random.fold_in(stream_key, 6), axis_at), (parts,), jnp.float32, low / len(cuts), top_value / len(cuts))
        loudness = loudness * jnp.repeat(jnp.exp(steps), shape[axis_at] // parts).reshape((-1,) + (1,) * (len(shape) - 1 - axis_at))
    return loudness


def shared_out(own_key, own, number, rows, count, top, reach, lean):
    sequence = jax.random.permutation(own_key, count)
    packed, ordinary = load_shares(count, rows * top, reach, lean, True), load_shares(count, rows * top, reach, lean, False)
    places = jnp.arange(count)

    def named(tallies, rotation):
        used = int((tallies > 0).sum())
        fixed = max(1, used // 4)
        passed = fixed + (places - fixed + rotation * (used - fixed)) % max(1, count - fixed)
        return jnp.zeros((count,), jnp.int32).at[sequence[jnp.where(places < fixed, places, passed)]].set(jnp.asarray(tallies, jnp.int32))

    tallies = jnp.where(number % 4 == 0, named(packed, number // 4), named(ordinary, number - number // 4 - 1))
    mixed = jax.random.permutation(jax.random.fold_in(own, 3), count)
    giver, receiver = mixed[0:count // 2 * 2:2], mixed[1:count // 2 * 2:2]
    margin = jnp.minimum(tallies[giver] - 1, reach - tallies[receiver]) // 2
    margin = jnp.where((giver == sequence[0]) | (receiver == sequence[0]) | (tallies[receiver] == 0), 0, jnp.maximum(margin, 0))
    passed = jax.random.randint(jax.random.fold_in(own, 4), (count // 2,), 0, 1 << 20) % (margin + 1)
    tallies = tallies.at[giver].add(-passed).at[receiver].add(passed)
    members = jnp.searchsorted(jnp.cumsum(tallies), jnp.arange(rows * top), side="right").astype(jnp.int32)
    listing = members.reshape(top, rows).T
    listing = listing[jax.random.permutation(jax.random.fold_in(own, 1), rows)]
    rotation = jax.random.randint(jax.random.fold_in(own, 2), (rows, 1), 0, top)
    return jnp.take_along_axis(listing, (jnp.arange(top)[None, :] + rotation) % top, axis=1)


def load_shares(amount, total, bound, slope, full):
    loads = [(1 << 20) // math.isqrt(grade ** slope) + 1 for grade in range(1, amount + 1)]
    largest = bound if full else min(bound, max(-(-total // amount), total * loads[0] // sum(loads)))
    least = 1 if total - largest >= amount - 1 else 0
    holding, surplus = [largest] + [least] * (amount - 1), total - largest - least * (amount - 1)
    while surplus > 0:
        movable = [i for i in range(1, amount) if holding[i] < largest] or [i for i in range(1, amount) if holding[i] < bound]
        mass, left = sum([loads[i] for i in movable]), surplus
        for i in movable:
            addition = min(bound - holding[i], max(1, left * loads[i] // mass), surplus)
            holding[i] = holding[i] + addition
            surplus = surplus - addition
    return np.array(holding)


def centred(own_key, shape, width, most, pieces=(), held_as=jnp.bfloat16):
    result = jax.random.normal(own_key, shape, jnp.float32) * width
    if len(pieces) > 0:
        result = levels(own_key, shape, pieces, -0.22, 0.18) * result
    return jnp.clip(result, min=-most, max=most).astype(held_as)


def setup_inputs(seed: int = 0) -> dict:
    seeds = jax.random.split(jax.random.key(seed), 14)
    queries = draw_queries(jax.random.fold_in(seeds[13], 71), 0)
    kv_pool = draw_kv_pool(jax.random.fold_in(seeds[13], 71), 0)
    page_table = draw_page_table(jax.random.fold_in(seeds[13], 71), 0)
    ctx_lens = draw_ctx_lens(jax.random.fold_in(seeds[13], 71), 0)
    w_out = centred(seeds[4], (D, D), 0.1, 0.59765625, ((0, 2), (1, 16)))
    residual = centred(seeds[5], (ROWS, D), 0.5, 3.0, ((0, 32),))
    moe_gain = jnp.clip(1.0 + 0.15 * jax.random.normal(seeds[6], (D,), jnp.float32), 0.25, 1.75)
    expert_ids_keys = jax.random.split(jax.random.fold_in(seeds[7], 1), ROWS // R)
    expert_ids_turns = jax.random.permutation(jax.random.fold_in(seeds[7], 3), ROWS // R)
    expert_ids = jax.vmap(lambda own, number: shared_out(jax.random.fold_in(seeds[7], 2), own, number, R, EXPERTS, TOP, CAP, 2))(expert_ids_keys, expert_ids_turns).reshape((ROWS, TOP))
    route_weights = jnp.clip(0.05 + 0.35 * jax.random.uniform(seeds[8], (ROWS, TOP), jnp.float32) ** levels(seeds[8], (ROWS, TOP), ((0, 32),), -0.2, 0.2), 0.05, 0.4)
    w_gate = centred(seeds[9], (EXPERTS, D, FF), D ** -0.5, 0.125, ((0, 16), (1, 2)))
    w_up = centred(seeds[10], (EXPERTS, D, FF), D ** -0.5, 0.125, ((0, 16), (1, 2)))
    w_down = centred(seeds[11], (EXPERTS, FF, D), FF ** -0.5, 0.15625, ((0, 16), (1, 2)))
    final_gain = jnp.clip(1.0 + 0.15 * jax.random.normal(seeds[12], (D,), jnp.float32), 0.25, 1.75)
    return dict(queries=queries, kv_pool=kv_pool, page_table=page_table, ctx_lens=ctx_lens, w_out=w_out, residual=residual, moe_gain=moe_gain, expert_ids=expert_ids, route_weights=route_weights, w_gate=w_gate, w_up=w_up, w_down=w_down, final_gain=final_gain)


def normalize(values, gain):
    mean_sq = lax.optimization_barrier(jnp.mean(values * values, axis=-1, keepdims=True))
    return values * lax.rsqrt(mean_sq + 1e-06) * gain

def reference(queries, kv_pool, page_table, ctx_lens, w_out, residual, moe_gain, expert_ids, route_weights, w_gate, w_up, w_down, final_gain):
    scale = 1.0 / math.sqrt(HD)
    asked = queries.reshape(SEQS, SEQ_ROWS, HEADS, HD)
    lengths_all = ctx_lens.reshape(SEQS, SEQ_ROWS)

    def attend(inputs):
        query, pages, lengths = inputs
        keys = kv_pool[0][pages].reshape(CTX, HEADS, HD).astype(jnp.float32)
        values = kv_pool[1][pages].reshape(CTX, HEADS, HD).astype(jnp.float32)
        scores = jnp.einsum('qhd,khd->hqk', query.astype(jnp.float32), keys) * scale
        visible = (jnp.arange(CTX, dtype=jnp.int32)[None, :] < lengths[:, None])[None]
        scores = jnp.where(visible, scores, -1e+30)
        top_score = lax.optimization_barrier(jnp.max(scores, axis=-1, keepdims=True))
        expo = jnp.where(visible, jnp.exp(scores - top_score), 0.0)
        probs = (expo / lax.optimization_barrier(jnp.sum(expo, axis=-1, keepdims=True))).astype(jnp.bfloat16)
        mixed = jnp.einsum('hqk,khd->qhd', probs.astype(jnp.float32), values)
        return mixed.astype(jnp.bfloat16).reshape(SEQ_ROWS, D)
    context = lax.map(attend, (asked, page_table, lengths_all)).reshape(ROWS, D)
    projected = jnp.dot(context, w_out, preferred_element_type=jnp.float32)
    hidden_state = residual.astype(jnp.float32) + projected
    moe_input = normalize(hidden_state, moe_gain).astype(jnp.bfloat16)
    pairs = expert_ids.reshape(BLOCKS, R * TOP)
    marks = (pairs[:, :, None] == jnp.arange(EXPERTS, dtype=jnp.int32)[None, None, :]).astype(jnp.int32)
    before = lax.optimization_barrier(jnp.sum((jnp.cumsum(marks, axis=1) - 1) * marks, axis=2))
    block_ids = jnp.arange(BLOCKS, dtype=jnp.int32)[:, None]
    target = (pairs * BLOCKS + block_ids) * CAP + before
    owner = block_ids * R + (jnp.arange(R * TOP, dtype=jnp.int32) // TOP)[None, :]
    table = jnp.full((EXPERTS * BLOCKS * CAP,), ROWS, dtype=jnp.int32)
    table = table.at[target.reshape(-1)].set(owner.reshape(-1))
    padded = jnp.concatenate([moe_input, jnp.zeros((1, D), jnp.bfloat16)], axis=0)

    def run_expert(inputs):
        chosen, gate_w, up_w, down_w = inputs
        rows_in = padded[chosen]
        gate = jnp.dot(rows_in, gate_w, preferred_element_type=jnp.float32)
        up_part = jnp.dot(rows_in, up_w, preferred_element_type=jnp.float32)
        expert_mid = (jax.nn.silu(gate) * up_part).astype(jnp.bfloat16)
        return jnp.dot(expert_mid, down_w, preferred_element_type=jnp.float32).astype(jnp.bfloat16)
    outputs = lax.map(run_expert, (table.reshape(EXPERTS, BLOCKS * CAP), w_gate, w_up, w_down))
    outputs = outputs.reshape(EXPERTS * BLOCKS * CAP, D)
    answers = outputs[target.reshape(ROWS, TOP)]
    moe = lax.optimization_barrier(jnp.sum(route_weights[:, :, None] * answers.astype(jnp.float32), axis=1))
    combined = hidden_state + moe
    return normalize(combined, final_gain).astype(jnp.bfloat16)
```

```python
import functools
import math

import jax
import jax.numpy as jnp
from jax import lax
from jax.experimental import pallas as pl
from jax.experimental.pallas import tpu as pltpu
from jax.sharding import PartitionSpec as P

HD = 128
TOP = 6
CTX = 256
MIB = 1024 * 1024


def normalize(values, gain):
    mean_sq = jnp.mean(values * values, axis=-1, keepdims=True)
    return values * lax.rsqrt(mean_sq + 1e-06) * gain


def attend(queries, kv_pool, page_table, ctx_lens):
    scale = 1.0 / math.sqrt(HD)
    group_rows = queries.shape[0]
    local_feats = queries.shape[1]
    local_heads = local_feats // HD
    seq_count = page_table.shape[0]
    seq_rows = group_rows // seq_count
    pool_here = kv_pool.shape[1]
    local_pages = page_table - lax.axis_index("expert") * pool_here
    keys = kv_pool[0][local_pages].reshape(seq_count, CTX, local_heads, HD)
    values = kv_pool[1][local_pages].reshape(seq_count, CTX, local_heads, HD)
    asked = queries.reshape(seq_count, seq_rows, local_heads, HD)
    scores = jnp.einsum("sqhd,skhd->shqk", asked, keys, preferred_element_type=jnp.float32) * scale
    lengths = ctx_lens.reshape(seq_count, seq_rows)
    visible = (jnp.arange(CTX, dtype=jnp.int32)[None, None, :] < lengths[:, :, None])[:, None]
    scores = jnp.where(visible, scores, -1e30)
    top_score = jnp.max(scores, axis=-1, keepdims=True)
    expo = jnp.where(visible, jnp.exp(scores - top_score), 0.0)
    probs = (expo / jnp.sum(expo, axis=-1, keepdims=True)).astype(jnp.bfloat16)
    mixed = jnp.einsum("shqk,skhd->sqhd", probs, values, preferred_element_type=jnp.float32)
    return mixed.astype(jnp.bfloat16).reshape(group_rows, local_feats)


def dispatched(
    queries,
    kv_pool,
    page_table,
    ctx_lens,
    w_out,
    residual,
    moe_gain,
    expert_ids,
    route_weights,
    w_gate,
    w_up,
    w_down,
    final_gain,
):
    context = attend(queries, kv_pool, page_table, ctx_lens)
    columns = lax.all_gather(w_out, "expert", axis=1, tiled=True)
    projected = lax.psum_scatter(
        jnp.dot(context, columns, preferred_element_type=jnp.float32).astype(jnp.bfloat16),
        "dp",
        scatter_dimension=0,
        tiled=True,
    ).astype(jnp.float32)
    hidden_state = residual.astype(jnp.float32) + projected
    moe_input = normalize(hidden_state, moe_gain).astype(jnp.bfloat16)
    rows_here = moe_input.shape[0]
    experts = lax.axis_size("expert")
    slots = max(2, min(rows_here, 2 * rows_here * TOP // experts))
    flat_ids = expert_ids.reshape(-1)
    marks = (flat_ids[:, None] == jnp.arange(experts, dtype=jnp.int32)[None, :]).astype(jnp.int32)
    before = jnp.sum((jnp.cumsum(marks, axis=0) - 1) * marks, axis=1)
    target = (flat_ids * slots + before).reshape(rows_here, TOP)
    placing = jnp.any(
        jnp.arange(experts * slots, dtype=jnp.int32)[:, None, None] == target[None], axis=-1
    )
    outbound = jnp.dot(placing.astype(jnp.bfloat16), moe_input, preferred_element_type=jnp.float32)
    outbound = outbound.astype(jnp.bfloat16).reshape(experts, slots, moe_input.shape[1])
    gate_full = lax.all_gather(w_gate, "dp", axis=1, tiled=True)
    up_full = lax.all_gather(w_up, "dp", axis=1, tiled=True)
    down_full = lax.all_gather(w_down, "dp", axis=1, tiled=True)
    arrived = lax.all_to_all(outbound, "expert", split_axis=0, concat_axis=0, tiled=True)
    flat = arrived.reshape(-1, arrived.shape[2])
    gate = jnp.dot(flat, gate_full[0], preferred_element_type=jnp.float32)
    up_part = jnp.dot(flat, up_full[0], preferred_element_type=jnp.float32)
    expert_mid = (jax.nn.silu(gate) * up_part).astype(jnp.bfloat16)
    done = jnp.dot(expert_mid, down_full[0], preferred_element_type=jnp.float32).astype(
        jnp.bfloat16
    )
    done = done.reshape(arrived.shape[0], arrived.shape[1], arrived.shape[2])
    returned = lax.all_to_all(done, "expert", split_axis=0, concat_axis=0, tiled=True)
    answers = returned.reshape(experts * slots, returned.shape[2])[target]
    moe = jnp.sum(route_weights[:, :, None] * answers.astype(jnp.float32), axis=1)
    combined = hidden_state + moe
    return normalize(combined, final_gain).astype(jnp.bfloat16)


def place(z, y, c):
    return (z * 2 + y) * 2 + c


def shift_z(values, depth, step):
    pairs = [
        (place((z + step) % depth, y, c), place(z, y, c))
        for z in range(depth)
        for y in range(2)
        for c in range(2)
    ]
    return lax.ppermute(values, "expert", pairs)


def flip_y(values, depth):
    pairs = [
        (place(z, 1 - y, c), place(z, y, c))
        for z in range(depth)
        for y in range(2)
        for c in range(2)
    ]
    return lax.ppermute(values, "expert", pairs)


def flip_core(values, depth):
    pairs = [
        (place(z, y, 1 - c), place(z, y, c))
        for z in range(depth)
        for y in range(2)
        for c in range(2)
    ]
    return lax.ppermute(values, "expert", pairs)


def flip_x(values):
    return lax.ppermute(values, "dp", [(0, 1), (1, 0)])


def project_kernel(depth, ctx_ref, *refs):
    pieces, (own_ref, send_ref) = refs[:-2], refs[-2:]
    half = own_ref.shape[0]
    width = pieces[0].shape[2]
    chunk = pieces[0].shape[1]
    me = lax.axis_index("expert")
    x = lax.axis_index("dp")
    c = lax.rem(me, 2)
    y = lax.rem(lax.div(me, 2), 2)
    z = lax.div(me, 4)
    mine = ctx_ref[pl.ds(pl.multiple_of(x * half, half), half), :]
    theirs = ctx_ref[pl.ds(pl.multiple_of((1 - x) * half, half), half), :]
    rows = jnp.concatenate([mine, theirs], axis=0)
    for piece in range(4):
        flips = ((0, 0), (1, 0), (0, 1), (1, 1))[piece]
        at_y = y if flips[0] == 0 else 1 - y
        at_c = c if flips[1] == 0 else 1 - c
        for r in range(depth):
            total = None
            for k in range(2):
                part = jnp.dot(
                    rows[:, k * chunk : (k + 1) * chunk],
                    pieces[2 * piece + k][r],
                    preferred_element_type=jnp.float32,
                )
                total = part if total is None else total + part
            index = (lax.rem(z + r, depth) * 2 + at_y) * 2 + at_c
            columns = pl.ds(pl.multiple_of(index * width, width), width)
            own_ref[:, columns] = total[:half]
            send_ref[:, columns] = total[half:].astype(send_ref.dtype)


def project(context, pieces, depth):
    rows, feats = context.shape
    width = pieces[0].shape[2]
    columns = width * 4 * depth
    return pl.pallas_call(
        functools.partial(project_kernel, depth),
        out_shape=(
            jax.ShapeDtypeStruct((rows // 2, columns), jnp.float32),
            jax.ShapeDtypeStruct((rows // 2, columns), jnp.bfloat16),
        ),
        compiler_params=pltpu.CompilerParams(vmem_limit_bytes=24 * MIB),
        cost_estimate=pl.CostEstimate(
            flops=2 * rows * feats * columns,
            bytes_accessed=2 * feats * columns + 4 * rows * columns,
            transcendentals=0,
        ),
        name="project",
    )(context, *pieces)


def experts_kernel(
    tile, out_tile, a8, ya, b8, xb, share, *refs
):
    weights, refs = refs[:10], refs[10:]
    outs, (rows, gate, up, down, mid, row_sem, weight_sem, down_sem) = refs[:4], refs[4:]
    x = lax.axis_index("dp")
    feats = rows.shape[1]
    half = feats // 2
    width = gate.shape[2]
    tiles = width // tile
    part = a8.shape[0]
    near = pl.ds(pl.multiple_of(x * half, half), half)
    far = pl.ds(pl.multiple_of((1 - x) * half, half), half)

    row_copies = []
    for i, piece in enumerate((a8, ya, b8, xb)):
        for s, lanes in enumerate((near, far)):
            copy = pltpu.make_async_copy(
                piece.at[:, lanes],
                rows.at[pl.ds(i * part, part), pl.ds(s * half, half)],
                row_sem.at[2 * i + s],
            )
            copy.start()
            row_copies.append(copy)
    weight_copies = []
    down_copies = []
    for e in range(2):
        gate_own, gate_far, up_own, up_far, down_e = weights[5 * e : 5 * e + 5]
        for j in range(tiles):
            group = []
            for n, (source, target, s) in enumerate(
                (
                    (gate_own, gate, 0),
                    (gate_far, gate, 1),
                    (up_own, up, 0),
                    (up_far, up, 1),
                )
            ):
                copy = pltpu.make_async_copy(
                    source.at[:, pl.ds(j * tile, tile)],
                    target.at[e, pl.ds(s * half, half), pl.ds(j * tile, tile)],
                    weight_sem.at[(e * tiles + j) * 4 + n],
                )
                copy.start()
                group.append(copy)
            weight_copies.append(group)
    for e in range(2):
        copy = pltpu.make_async_copy(
            weights[5 * e + 4], down.at[pl.ds(e * width, width), :], down_sem.at[e]
        )
        copy.start()
        down_copies.append(copy)

    for copy in row_copies:
        copy.wait()
    for e in range(2):
        scale = share[:, e : e + 1]
        for j in range(tiles):
            for copy in weight_copies[e * tiles + j]:
                copy.wait()
            lanes = pl.ds(j * tile, tile)
            g = jnp.dot(rows[...], gate[e, :, lanes], preferred_element_type=jnp.float32)
            u = jnp.dot(rows[...], up[e, :, lanes], preferred_element_type=jnp.float32)
            h = g / (1.0 + jnp.exp(-g)) * u * scale
            mid[:, pl.ds(e * width + j * tile, tile)] = h.astype(mid.dtype)
    for copy in down_copies:
        copy.wait()
    for n in range(feats // out_tile):
        lanes = pl.ds(n * out_tile, out_tile)
        total = jnp.dot(mid[...], down[:, lanes], preferred_element_type=jnp.float32)
        for i, out in enumerate(outs):
            out[:, lanes] = total[i * part : (i + 1) * part].astype(out.dtype)


def run_experts(pieces, share, weights):
    part, feats = pieces[0].shape
    half, width = weights[0].shape
    total = 4 * part
    tile = 256
    any_spec = pl.BlockSpec(memory_space=pl.ANY)
    vmem_spec = pl.BlockSpec(memory_space=pltpu.VMEM)
    return pl.pallas_call(
        functools.partial(experts_kernel, tile, 512),
        out_shape=tuple(
            jax.ShapeDtypeStruct((part, feats), kind)
            for kind in (jnp.float32, jnp.bfloat16, jnp.float32, jnp.bfloat16)
        ),
        in_specs=[any_spec] * 4 + [vmem_spec] + [any_spec] * 10,
        out_specs=(vmem_spec,) * 4,
        scratch_shapes=[
            pltpu.VMEM((total, feats), jnp.bfloat16),
            pltpu.VMEM((2, feats, width), jnp.bfloat16),
            pltpu.VMEM((2, feats, width), jnp.bfloat16),
            pltpu.VMEM((2 * width, feats), jnp.bfloat16),
            pltpu.VMEM((total, 2 * width), jnp.bfloat16),
            pltpu.SemaphoreType.DMA((8,)),
            pltpu.SemaphoreType.DMA((8 * (width // tile),)),
            pltpu.SemaphoreType.DMA((2,)),
        ],
        compiler_params=pltpu.CompilerParams(vmem_limit_bytes=40 * MIB),
        cost_estimate=pl.CostEstimate(
            flops=2 * total * feats * width * 6,
            bytes_accessed=12 * feats * width + 12 * total * feats,
            transcendentals=total * width * 2,
        ),
        name="experts",
    )(*pieces, share, *weights)


def gathered(
    queries,
    kv_pool,
    page_table,
    ctx_lens,
    w_out,
    residual,
    moe_gain,
    expert_ids,
    route_weights,
    w_gate,
    w_up,
    w_down,
    final_gain,
):
    experts = lax.axis_size("expert")
    depth = experts // 4
    me = lax.axis_index("expert")
    x = lax.axis_index("dp")
    c = me % 2
    y = (me // 2) % 2
    z = me // 4
    first = x == 0
    feats = residual.shape[1]
    block = residual.shape[0]
    units = w_gate.shape[2]
    units_here = w_down.shape[1]
    width = -(-units_here // 256) * 256

    def halves(weights):
        low, high = weights[:, :width], weights[:, units - width :]
        return jnp.where(first, low, high), jnp.where(first, high, low)

    gate_own, gate_sent = halves(w_gate[0])
    up_own, up_sent = halves(w_up[0])
    gate_far = flip_x(gate_sent)
    up_far = flip_x(up_sent)
    blank = jnp.zeros((width - units_here, feats), w_down.dtype)
    down_own = jnp.where(
        first,
        jnp.concatenate([w_down[0], blank], axis=0),
        jnp.concatenate([blank, w_down[0]], axis=0),
    )
    here = [gate_own, gate_far, up_own, up_far, down_own]
    weights = here + [flip_core(array, depth) for array in here]

    near, across, near_core, across_core = [], [], [], []
    chunk = w_out.shape[0] // 2
    for k in range(2):
        own = w_out[k * chunk : (k + 1) * chunk]
        line = jnp.stack([own] + [shift_z(own, depth, s) for s in range(1, depth)])
        near.append(line)
        near_core.append(flip_core(line, depth))
        other = flip_y(line, depth)
        across.append(other)
        across_core.append(flip_core(other, depth))

    named = expert_ids[:, :, None] == jnp.arange(experts, dtype=jnp.int32)[None, None, :]
    share = jnp.sum(jnp.where(named, route_weights[:, :, None], 0.0), axis=1)
    share = lax.all_gather(share, ("expert", "dp"), axis=0, tiled=True)
    both = jnp.stack([me, me + 1 - 2 * c])
    pick = (jnp.arange(experts, dtype=jnp.int32)[:, None] == both[None, :]).astype(jnp.float32)
    share = jnp.dot(share, pick, precision=lax.Precision.HIGHEST)
    share = share.reshape(experts * 2, 2, 2, block // 4, 2)
    line_z = (z + jnp.arange(depth, dtype=jnp.int32)) % depth

    def blocks(dx, dy):
        at_x = x if dx == 0 else 1 - x
        at_y = y if dy == 0 else 1 - y
        return place(line_z, at_y, c) * 2 + at_x

    order_a = jnp.concatenate([blocks(0, 0), blocks(1, 0), blocks(0, 1), blocks(1, 1)])
    order_b = jnp.concatenate([blocks(0, 0), blocks(0, 1), blocks(1, 0), blocks(1, 1)])
    share_a = jnp.take(share[:, :, 0], order_a, axis=0)
    share_b = jnp.take(share[:, :, 1], order_b, axis=0)

    context = attend(queries, kv_pool, page_table, ctx_lens)
    own, sent = project(context, near + across + near_core + across_core, depth)
    projected = own + flip_x(sent).astype(jnp.float32)
    hidden_state = residual.astype(jnp.float32) + projected
    moe_input = normalize(hidden_state, moe_gain).astype(jnp.bfloat16)

    quarter = block // 4
    part = depth * quarter
    moe = []
    for k in range(2):
        mine = moe_input[2 * quarter * k : 2 * quarter * (k + 1)]
        line = jnp.stack([mine] + [shift_z(mine, depth, s) for s in range(1, depth)])
        line_a, line_b = line[:, :quarter], line[:, quarter:]
        line_a = line_a.reshape(part, feats)
        line_b = line_b.reshape(part, feats)
        a8 = jnp.concatenate([line_a, flip_x(line_a)], axis=0)
        b8 = jnp.concatenate([line_b, flip_y(line_b, depth)], axis=0)
        ya = flip_y(a8, depth)
        xb = flip_x(b8)
        shares = jnp.concatenate(
            [share_a[:, k].reshape(4 * part, 2), share_b[:, k].reshape(4 * part, 2)], axis=0
        )
        out_a, out_ya, out_b, out_xb = run_experts([a8, ya, b8, xb], shares, weights)
        back_a = flip_y(out_ya, depth).astype(jnp.float32)
        back_b = flip_x(out_xb).astype(jnp.float32)
        sum_a = out_a + back_a
        sum_b = out_b + back_b
        last_a = flip_x(sum_a[part:].astype(jnp.bfloat16)).astype(jnp.float32)
        last_b = flip_y(sum_b[part:].astype(jnp.bfloat16), depth).astype(jnp.float32)
        full_a = (sum_a[:part] + last_a).reshape(depth, quarter, feats)
        full_b = (sum_b[:part] + last_b).reshape(depth, quarter, feats)
        full = jnp.concatenate([full_a, full_b], axis=1)
        total = full[0]
        for s in range(1, depth):
            total = total + shift_z(full[s].astype(jnp.bfloat16), depth, depth - s).astype(
                jnp.float32
            )
        moe.append(total)
    combined = hidden_state + jnp.concatenate(moe, axis=0)
    return normalize(combined, final_gain).astype(jnp.bfloat16)


def solution(mesh):
    few = mesh.shape["dp"] == 2 and mesh.shape["expert"] == 16
    return jax.shard_map(
        gathered if few else dispatched,
        mesh=mesh,
        in_specs=(
            P("expert", "dp"),
            P(None, "expert", None, "dp"),
            P("expert", None),
            P("expert"),
            P("dp", "expert"),
            P(("expert", "dp"), None),
            P(),
            P(("expert", "dp"), None),
            P(("expert", "dp"), None),
            P("expert", "dp", None),
            P("expert", "dp", None),
            P("expert", "dp", None),
            P(),
        ),
        out_specs=P(("expert", "dp"), None),
        check_vma=False,
    )
```

```python
import functools
import math

import jax
import jax.numpy as jnp
from jax import lax
from jax.experimental import pallas as pl
from jax.experimental.pallas import tpu as pltpu
from jax.sharding import PartitionSpec as P

HD = 128
TOP = 6
CTX = 256
MIB = 1024 * 1024


def normalize(values, gain):
    mean_sq = jnp.mean(values * values, axis=-1, keepdims=True)
    return values * lax.rsqrt(mean_sq + 1e-06) * gain


def attend(queries, kv_pool, page_table, ctx_lens):
    scale = 1.0 / math.sqrt(HD)
    group_rows = queries.shape[0]
    local_feats = queries.shape[1]
    local_heads = local_feats // HD
    seq_count = page_table.shape[0]
    seq_rows = group_rows // seq_count
    pool_here = kv_pool.shape[1]
    local_pages = page_table - lax.axis_index("expert") * pool_here
    keys = kv_pool[0][local_pages].reshape(seq_count, CTX, local_heads, HD)
    values = kv_pool[1][local_pages].reshape(seq_count, CTX, local_heads, HD)
    asked = queries.reshape(seq_count, seq_rows, local_heads, HD)
    scores = jnp.einsum("sqhd,skhd->shqk", asked, keys, preferred_element_type=jnp.float32) * scale
    lengths = ctx_lens.reshape(seq_count, seq_rows)
    visible = (jnp.arange(CTX, dtype=jnp.int32)[None, None, :] < lengths[:, :, None])[:, None]
    scores = jnp.where(visible, scores, -1e30)
    top_score = jnp.max(scores, axis=-1, keepdims=True)
    expo = jnp.where(visible, jnp.exp(scores - top_score), 0.0)
    probs = (expo / jnp.sum(expo, axis=-1, keepdims=True)).astype(jnp.bfloat16)
    mixed = jnp.einsum("shqk,skhd->sqhd", probs, values, preferred_element_type=jnp.float32)
    return mixed.astype(jnp.bfloat16).reshape(group_rows, local_feats)


def dispatched(
    queries,
    kv_pool,
    page_table,
    ctx_lens,
    w_out,
    residual,
    moe_gain,
    expert_ids,
    route_weights,
    w_gate,
    w_up,
    w_down,
    final_gain,
):
    context = attend(queries, kv_pool, page_table, ctx_lens)
    columns = lax.all_gather(w_out, "expert", axis=1, tiled=True)
    projected = lax.psum_scatter(
        jnp.dot(context, columns, preferred_element_type=jnp.float32).astype(jnp.bfloat16),
        "dp",
        scatter_dimension=0,
        tiled=True,
    ).astype(jnp.float32)
    hidden_state = residual.astype(jnp.float32) + projected
    moe_input = normalize(hidden_state, moe_gain).astype(jnp.bfloat16)
    rows_here = moe_input.shape[0]
    experts = lax.axis_size("expert")
    slots = max(2, min(rows_here, 2 * rows_here * TOP // experts))
    flat_ids = expert_ids.reshape(-1)
    marks = (flat_ids[:, None] == jnp.arange(experts, dtype=jnp.int32)[None, :]).astype(jnp.int32)
    before = jnp.sum((jnp.cumsum(marks, axis=0) - 1) * marks, axis=1)
    target = (flat_ids * slots + before).reshape(rows_here, TOP)
    placing = jnp.any(
        jnp.arange(experts * slots, dtype=jnp.int32)[:, None, None] == target[None], axis=-1
    )
    outbound = jnp.dot(placing.astype(jnp.bfloat16), moe_input, preferred_element_type=jnp.float32)
    outbound = outbound.astype(jnp.bfloat16).reshape(experts, slots, moe_input.shape[1])
    gate_full = lax.all_gather(w_gate, "dp", axis=1, tiled=True)
    up_full = lax.all_gather(w_up, "dp", axis=1, tiled=True)
    down_full = lax.all_gather(w_down, "dp", axis=1, tiled=True)
    arrived = lax.all_to_all(outbound, "expert", split_axis=0, concat_axis=0, tiled=True)
    flat = arrived.reshape(-1, arrived.shape[2])
    gate = jnp.dot(flat, gate_full[0], preferred_element_type=jnp.float32)
    up_part = jnp.dot(flat, up_full[0], preferred_element_type=jnp.float32)
    expert_mid = (jax.nn.silu(gate) * up_part).astype(jnp.bfloat16)
    done = jnp.dot(expert_mid, down_full[0], preferred_element_type=jnp.float32).astype(
        jnp.bfloat16
    )
    done = done.reshape(arrived.shape[0], arrived.shape[1], arrived.shape[2])
    returned = lax.all_to_all(done, "expert", split_axis=0, concat_axis=0, tiled=True)
    answers = returned.reshape(experts * slots, returned.shape[2])[target]
    moe = jnp.sum(route_weights[:, :, None] * answers.astype(jnp.float32), axis=1)
    combined = hidden_state + moe
    return normalize(combined, final_gain).astype(jnp.bfloat16)


def place(z, y, c):
    return (z * 2 + y) * 2 + c


def shift_z(values, depth, step):
    pairs = [
        (place((z + step) % depth, y, c), place(z, y, c))
        for z in range(depth)
        for y in range(2)
        for c in range(2)
    ]
    return lax.ppermute(values, "expert", pairs)


def flip_y(values, depth):
    pairs = [
        (place(z, 1 - y, c), place(z, y, c))
        for z in range(depth)
        for y in range(2)
        for c in range(2)
    ]
    return lax.ppermute(values, "expert", pairs)


def flip_core(values, depth):
    pairs = [
        (place(z, y, 1 - c), place(z, y, c))
        for z in range(depth)
        for y in range(2)
        for c in range(2)
    ]
    return lax.ppermute(values, "expert", pairs)


def flip_x(values):
    return lax.ppermute(values, "dp", [(0, 1), (1, 0)])


def project_kernel(depth, ctx_ref, *refs):
    pieces, (own_ref, send_ref) = refs[:-2], refs[-2:]
    half = own_ref.shape[0]
    width = pieces[0].shape[1]
    me = lax.axis_index("expert")
    x = lax.axis_index("dp")
    c = lax.rem(me, 2)
    y = lax.rem(lax.div(me, 2), 2)
    z = lax.div(me, 4)
    mine = ctx_ref[pl.ds(pl.multiple_of(x * half, half), half), :]
    theirs = ctx_ref[pl.ds(pl.multiple_of((1 - x) * half, half), half), :]
    rows = jnp.concatenate([mine, theirs], axis=0)
    for flips in range(4):
        at_y = y if flips % 2 == 0 else 1 - y
        at_c = c if flips < 2 else 1 - c
        for r in range(depth):
            total = jnp.dot(
                rows, pieces[flips * depth + r][...], preferred_element_type=jnp.float32
            )
            index = (lax.rem(z + r, depth) * 2 + at_y) * 2 + at_c
            columns = pl.ds(pl.multiple_of(index * width, width), width)
            own_ref[:, columns] = total[:half]
            send_ref[:, columns] = total[half:].astype(send_ref.dtype)


def project(context, pieces, depth):
    rows, feats = context.shape
    columns = pieces[0].shape[1] * 4 * depth
    return pl.pallas_call(
        functools.partial(project_kernel, depth),
        out_shape=(
            jax.ShapeDtypeStruct((rows // 2, columns), jnp.float32),
            jax.ShapeDtypeStruct((rows // 2, columns), jnp.bfloat16),
        ),
        compiler_params=pltpu.CompilerParams(vmem_limit_bytes=24 * MIB),
        cost_estimate=pl.CostEstimate(
            flops=2 * rows * feats * columns,
            bytes_accessed=2 * feats * columns + 4 * rows * columns,
            transcendentals=0,
        ),
        name="project",
    )(context, *pieces)


def experts_kernel(
    tile, out_tile, count, *refs
):
    pieces, share, weights = refs[:count], refs[count], refs[count + 1 : count + 11]
    outs, refs = refs[count + 11 : 2 * count + 11], refs[2 * count + 11 :]
    rows, gate, up, down, mid, row_sem, weight_sem, down_sem = refs
    x = lax.axis_index("dp")
    feats = rows.shape[1]
    half = feats // 2
    width = gate.shape[2]
    tiles = width // tile
    near = pl.ds(pl.multiple_of(x * half, half), half)
    far = pl.ds(pl.multiple_of((1 - x) * half, half), half)

    row_copies = []
    offsets = []
    at = 0
    for i, piece in enumerate(pieces):
        part = piece.shape[0]
        offsets.append((at, part))
        for s, lanes in enumerate((near, far)):
            copy = pltpu.make_async_copy(
                piece.at[:, lanes],
                rows.at[pl.ds(at, part), pl.ds(s * half, half)],
                row_sem.at[2 * i + s],
            )
            copy.start()
            row_copies.append(copy)
        at += part
    weight_copies = []
    down_copies = []
    for e in range(2):
        gate_own, gate_far, up_own, up_far, down_e = weights[5 * e : 5 * e + 5]
        for j in range(tiles):
            group = []
            for n, (source, target, s) in enumerate(
                (
                    (gate_own, gate, 0),
                    (gate_far, gate, 1),
                    (up_own, up, 0),
                    (up_far, up, 1),
                )
            ):
                copy = pltpu.make_async_copy(
                    source.at[:, pl.ds(j * tile, tile)],
                    target.at[e, pl.ds(s * half, half), pl.ds(j * tile, tile)],
                    weight_sem.at[(e * tiles + j) * 4 + n],
                )
                copy.start()
                group.append(copy)
            weight_copies.append(group)
    for e in range(2):
        copy = pltpu.make_async_copy(
            weights[5 * e + 4], down.at[pl.ds(e * width, width), :], down_sem.at[e]
        )
        copy.start()
        down_copies.append(copy)

    for copy in row_copies:
        copy.wait()
    for e in range(2):
        scale = share[:, e : e + 1]
        for j in range(tiles):
            for copy in weight_copies[e * tiles + j]:
                copy.wait()
            lanes = pl.ds(j * tile, tile)
            g = jnp.dot(rows[...], gate[e, :, lanes], preferred_element_type=jnp.float32)
            u = jnp.dot(rows[...], up[e, :, lanes], preferred_element_type=jnp.float32)
            h = g / (1.0 + jnp.exp(-g)) * u * scale
            mid[:, pl.ds(e * width + j * tile, tile)] = h.astype(mid.dtype)
    for copy in down_copies:
        copy.wait()
    for n in range(feats // out_tile):
        lanes = pl.ds(n * out_tile, out_tile)
        total = jnp.dot(mid[...], down[:, lanes], preferred_element_type=jnp.float32)
        for (first, part), out in zip(offsets, outs):
            out[:, lanes] = total[first : first + part].astype(out.dtype)


def run_experts(pieces, kinds, share, weights):
    feats = pieces[0].shape[1]
    half, width = weights[0].shape
    count = len(pieces)
    total = sum(piece.shape[0] for piece in pieces)
    tile = 256
    any_spec = pl.BlockSpec(memory_space=pl.ANY)
    vmem_spec = pl.BlockSpec(memory_space=pltpu.VMEM)
    return pl.pallas_call(
        functools.partial(experts_kernel, tile, 512, count),
        out_shape=tuple(
            jax.ShapeDtypeStruct(piece.shape, kind) for piece, kind in zip(pieces, kinds)
        ),
        in_specs=[any_spec] * count + [vmem_spec] + [any_spec] * 10,
        out_specs=(vmem_spec,) * count,
        scratch_shapes=[
            pltpu.VMEM((total, feats), jnp.bfloat16),
            pltpu.VMEM((2, feats, width), jnp.bfloat16),
            pltpu.VMEM((2, feats, width), jnp.bfloat16),
            pltpu.VMEM((2 * width, feats), jnp.bfloat16),
            pltpu.VMEM((total, 2 * width), jnp.bfloat16),
            pltpu.SemaphoreType.DMA((2 * count,)),
            pltpu.SemaphoreType.DMA((8 * (width // tile),)),
            pltpu.SemaphoreType.DMA((2,)),
        ],
        compiler_params=pltpu.CompilerParams(vmem_limit_bytes=40 * MIB),
        cost_estimate=pl.CostEstimate(
            flops=2 * total * feats * width * 6,
            bytes_accessed=12 * feats * width + 12 * total * feats,
            transcendentals=total * width * 2,
        ),
        name="experts",
    )(*pieces, share, *weights)


def gathered(
    queries,
    kv_pool,
    page_table,
    ctx_lens,
    w_out,
    residual,
    moe_gain,
    expert_ids,
    route_weights,
    w_gate,
    w_up,
    w_down,
    final_gain,
):
    experts = lax.axis_size("expert")
    depth = experts // 4
    me = lax.axis_index("expert")
    x = lax.axis_index("dp")
    c = me % 2
    first = x == 0
    feats = residual.shape[1]
    block = residual.shape[0]
    units = w_gate.shape[2]
    units_here = w_down.shape[1]
    width = -(-units_here // 256) * 256

    def halves(weights):
        low, high = weights[:, :width], weights[:, units - width :]
        return jnp.where(first, low, high), jnp.where(first, high, low)

    gate_own, gate_sent = halves(w_gate[0])
    up_own, up_sent = halves(w_up[0])
    gate_far = flip_x(gate_sent)
    blank = jnp.zeros((width - units_here, feats), w_down.dtype)
    down_own = jnp.where(
        first,
        jnp.concatenate([w_down[0], blank], axis=0),
        jnp.concatenate([blank, w_down[0]], axis=0),
    )
    gate_own_core = flip_core(gate_own, depth)
    up_own_core = flip_core(up_own, depth)
    down_own_core = flip_core(down_own, depth)

    near = [w_out] + [shift_z(w_out, depth, s) for s in range(1, depth)]
    across = [flip_y(piece, depth) for piece in near]
    columns = near + across
    columns = columns + [flip_core(piece, depth) for piece in columns]

    named = expert_ids[:, :, None] == jnp.arange(experts, dtype=jnp.int32)[None, None, :]
    share = jnp.sum(jnp.where(named, route_weights[:, :, None], 0.0), axis=1)
    both = jnp.stack([me, me + 1 - 2 * c])
    pick = both[None, :] == jnp.arange(experts, dtype=jnp.int32)[:, None]
    share_l = jnp.stack([share] + [shift_z(share, depth, s) for s in range(1, depth)])
    share_x = flip_x(share_l)
    share_y = flip_y(share_l, depth)
    share_d = flip_y(share_x, depth)
    shares = jnp.stack([share_l, share_x, share_y, share_d])
    shares = jnp.sum(jnp.where(pick[:, None, :].swapaxes(0, 1), shares[..., None], 0.0), axis=-2)

    context = attend(queries, kv_pool, page_table, ctx_lens)
    own, sent = project(context, columns, depth)
    own, sent, gate_far, shares, gate_own_core, up_own_core, down_own_core = lax.optimization_barrier(
        (own, sent, gate_far, shares, gate_own_core, up_own_core, down_own_core)
    )
    received, up_sent = lax.optimization_barrier((flip_x(sent), up_sent))
    up_far = flip_x(up_sent)
    weights = [gate_own, gate_far, up_own, up_far, down_own]
    weights += [
        gate_own_core,
        flip_core(gate_far, depth),
        up_own_core,
        flip_core(up_far, depth),
        down_own_core,
    ]
    hidden_state = residual.astype(jnp.float32) + (own + received.astype(jnp.float32))
    moe_input = normalize(hidden_state, moe_gain).astype(jnp.bfloat16)

    chunks = 2
    rows = block // chunks
    part = rows // 2
    moe = []
    for k in range(chunks):
        mine = moe_input[rows * k : rows * (k + 1)]
        line = jnp.stack([mine] + [shift_z(mine, depth, s) for s in range(1, depth)])
        line_x = flip_x(line)
        line_y = flip_y(line, depth)
        low = flip_y(line_x[:, :part], depth)
        high = flip_x(line_y[:, part:])
        share = shares[:, :, rows * k : rows * (k + 1)]
        share = jnp.concatenate(
            [
                share[:3].reshape(3 * depth * rows, 2),
                share[3, :, :part].reshape(depth * part, 2),
                share[3, :, part:].reshape(depth * part, 2),
            ],
            axis=0,
        )
        out_l, out_x, out_y, out_low, out_high = run_experts(
            [piece.reshape(-1, feats) for piece in (line, line_x, line_y, low, high)],
            (jnp.float32, jnp.float32, jnp.float32, jnp.bfloat16, jnp.bfloat16),
            share,
            weights,
        )
        out_l = out_l.reshape(line.shape)
        out_x = out_x.reshape(line.shape)
        out_y = out_y.reshape(line.shape)
        back_low = flip_y(out_low, depth).reshape(low.shape).astype(jnp.float32)
        back_high = flip_x(out_high).reshape(high.shape).astype(jnp.float32)
        sum_x = jnp.concatenate([out_x[:, :part] + back_low, out_x[:, part:]], axis=1)
        sum_y = jnp.concatenate([out_y[:, :part], out_y[:, part:] + back_high], axis=1)
        back_x = flip_x(sum_x.astype(jnp.bfloat16)).astype(jnp.float32)
        back_y = flip_y(sum_y.astype(jnp.bfloat16), depth).astype(jnp.float32)
        full = out_l + back_x + back_y
        total = full[0]
        for s in range(1, depth):
            total = total + shift_z(full[s].astype(jnp.bfloat16), depth, depth - s).astype(
                jnp.float32
            )
        moe.append(total)
    combined = hidden_state + jnp.concatenate(moe, axis=0)
    return normalize(combined, final_gain).astype(jnp.bfloat16)


def solution(mesh):
    few = mesh.shape["dp"] == 2 and mesh.shape["expert"] == 16
    return jax.shard_map(
        gathered if few else dispatched,
        mesh=mesh,
        in_specs=(
            P("expert", "dp"),
            P(None, "expert", None, "dp"),
            P("expert", None),
            P("expert"),
            P("dp", "expert"),
            P(("expert", "dp"), None),
            P(),
            P(("expert", "dp"), None),
            P(("expert", "dp"), None),
            P("expert", "dp", None),
            P("expert", "dp", None),
            P("expert", "dp", None),
            P(),
        ),
        out_specs=P(("expert", "dp"), None),
        check_vma=False,
    )
```

```python
import functools
import math

import jax
import jax.numpy as jnp
from jax import lax
from jax.experimental import pallas as pl
from jax.experimental.pallas import tpu as pltpu
from jax.sharding import PartitionSpec as P

HD = 128
TOP = 6
CTX = 256
MIB = 1024 * 1024


def normalize(values, gain):
    mean_sq = jnp.mean(values * values, axis=-1, keepdims=True)
    return values * lax.rsqrt(mean_sq + 1e-06) * gain


def attend(queries, kv_pool, page_table, ctx_lens):
    scale = 1.0 / math.sqrt(HD)
    group_rows = queries.shape[0]
    local_feats = queries.shape[1]
    local_heads = local_feats // HD
    seq_count = page_table.shape[0]
    seq_rows = group_rows // seq_count
    pool_here = kv_pool.shape[1]
    local_pages = page_table - lax.axis_index("expert") * pool_here
    keys = kv_pool[0][local_pages].reshape(seq_count, CTX, local_heads, HD)
    values = kv_pool[1][local_pages].reshape(seq_count, CTX, local_heads, HD)
    asked = queries.reshape(seq_count, seq_rows, local_heads, HD)
    scores = jnp.einsum("sqhd,skhd->shqk", asked, keys, preferred_element_type=jnp.float32) * scale
    lengths = ctx_lens.reshape(seq_count, seq_rows)
    visible = (jnp.arange(CTX, dtype=jnp.int32)[None, None, :] < lengths[:, :, None])[:, None]
    scores = jnp.where(visible, scores, -1e30)
    top_score = jnp.max(scores, axis=-1, keepdims=True)
    expo = jnp.where(visible, jnp.exp(scores - top_score), 0.0)
    probs = (expo / jnp.sum(expo, axis=-1, keepdims=True)).astype(jnp.bfloat16)
    mixed = jnp.einsum("shqk,skhd->sqhd", probs, values, preferred_element_type=jnp.float32)
    return mixed.astype(jnp.bfloat16).reshape(group_rows, local_feats)


def dispatched(
    queries,
    kv_pool,
    page_table,
    ctx_lens,
    w_out,
    residual,
    moe_gain,
    expert_ids,
    route_weights,
    w_gate,
    w_up,
    w_down,
    final_gain,
):
    context = attend(queries, kv_pool, page_table, ctx_lens)
    columns = lax.all_gather(w_out, "expert", axis=1, tiled=True)
    projected = lax.psum_scatter(
        jnp.dot(context, columns, preferred_element_type=jnp.float32).astype(jnp.bfloat16),
        "dp",
        scatter_dimension=0,
        tiled=True,
    ).astype(jnp.float32)
    hidden_state = residual.astype(jnp.float32) + projected
    moe_input = normalize(hidden_state, moe_gain).astype(jnp.bfloat16)
    rows_here = moe_input.shape[0]
    experts = lax.axis_size("expert")
    slots = max(2, min(rows_here, 2 * rows_here * TOP // experts))
    flat_ids = expert_ids.reshape(-1)
    marks = (flat_ids[:, None] == jnp.arange(experts, dtype=jnp.int32)[None, :]).astype(jnp.int32)
    before = jnp.sum((jnp.cumsum(marks, axis=0) - 1) * marks, axis=1)
    target = (flat_ids * slots + before).reshape(rows_here, TOP)
    placing = jnp.any(
        jnp.arange(experts * slots, dtype=jnp.int32)[:, None, None] == target[None], axis=-1
    )
    outbound = jnp.dot(placing.astype(jnp.bfloat16), moe_input, preferred_element_type=jnp.float32)
    outbound = outbound.astype(jnp.bfloat16).reshape(experts, slots, moe_input.shape[1])
    gate_full = lax.all_gather(w_gate, "dp", axis=1, tiled=True)
    up_full = lax.all_gather(w_up, "dp", axis=1, tiled=True)
    down_full = lax.all_gather(w_down, "dp", axis=1, tiled=True)
    arrived = lax.all_to_all(outbound, "expert", split_axis=0, concat_axis=0, tiled=True)
    flat = arrived.reshape(-1, arrived.shape[2])
    gate = jnp.dot(flat, gate_full[0], preferred_element_type=jnp.float32)
    up_part = jnp.dot(flat, up_full[0], preferred_element_type=jnp.float32)
    expert_mid = (jax.nn.silu(gate) * up_part).astype(jnp.bfloat16)
    done = jnp.dot(expert_mid, down_full[0], preferred_element_type=jnp.float32).astype(
        jnp.bfloat16
    )
    done = done.reshape(arrived.shape[0], arrived.shape[1], arrived.shape[2])
    returned = lax.all_to_all(done, "expert", split_axis=0, concat_axis=0, tiled=True)
    answers = returned.reshape(experts * slots, returned.shape[2])[target]
    moe = jnp.sum(route_weights[:, :, None] * answers.astype(jnp.float32), axis=1)
    combined = hidden_state + moe
    return normalize(combined, final_gain).astype(jnp.bfloat16)


def place(z, y, c):
    return (z * 2 + y) * 2 + c


def shift_z(values, depth, step):
    pairs = [
        (place((z + step) % depth, y, c), place(z, y, c))
        for z in range(depth)
        for y in range(2)
        for c in range(2)
    ]
    return lax.ppermute(values, "expert", pairs)


def flip_y(values, depth):
    pairs = [
        (place(z, 1 - y, c), place(z, y, c))
        for z in range(depth)
        for y in range(2)
        for c in range(2)
    ]
    return lax.ppermute(values, "expert", pairs)


def flip_core(values, depth):
    pairs = [
        (place(z, y, 1 - c), place(z, y, c))
        for z in range(depth)
        for y in range(2)
        for c in range(2)
    ]
    return lax.ppermute(values, "expert", pairs)


def flip_x(values):
    return lax.ppermute(values, "dp", [(0, 1), (1, 0)])


def project_kernel(depth, ctx_ref, *refs):
    pieces, (own_ref, send_ref) = refs[:-2], refs[-2:]
    half = own_ref.shape[0]
    width = pieces[0].shape[1]
    me = lax.axis_index("expert")
    x = lax.axis_index("dp")
    c = lax.rem(me, 2)
    y = lax.rem(lax.div(me, 2), 2)
    z = lax.div(me, 4)
    mine = ctx_ref[pl.ds(pl.multiple_of(x * half, half), half), :]
    theirs = ctx_ref[pl.ds(pl.multiple_of((1 - x) * half, half), half), :]
    rows = jnp.concatenate([mine, theirs], axis=0)
    for flips in range(4):
        at_y = y if flips % 2 == 0 else 1 - y
        at_c = c if flips < 2 else 1 - c
        for r in range(depth):
            total = jnp.dot(
                rows, pieces[flips * depth + r][...], preferred_element_type=jnp.float32
            )
            index = (lax.rem(z + r, depth) * 2 + at_y) * 2 + at_c
            columns = pl.ds(pl.multiple_of(index * width, width), width)
            own_ref[:, columns] = total[:half]
            send_ref[:, columns] = total[half:].astype(send_ref.dtype)


def project(context, pieces, depth):
    rows, feats = context.shape
    columns = pieces[0].shape[1] * 4 * depth
    return pl.pallas_call(
        functools.partial(project_kernel, depth),
        out_shape=(
            jax.ShapeDtypeStruct((rows // 2, columns), jnp.float32),
            jax.ShapeDtypeStruct((rows // 2, columns), jnp.bfloat16),
        ),
        compiler_params=pltpu.CompilerParams(vmem_limit_bytes=24 * MIB),
        cost_estimate=pl.CostEstimate(
            flops=2 * rows * feats * columns,
            bytes_accessed=2 * feats * columns + 4 * rows * columns,
            transcendentals=0,
        ),
        name="project",
    )(context, *pieces)


def experts_kernel(tile, out_tile, count, n_gate, n_up, *refs):
    per_expert = n_gate + n_up + 1
    pieces, refs = refs[:count], refs[count:]
    share, weights, refs = refs[0], refs[1 : 1 + 2 * per_expert], refs[1 + 2 * per_expert :]
    outs, refs = refs[:count], refs[count:]
    rows, gate, up, down, mid, row_sem, weight_sem, down_sem = refs
    x = lax.axis_index("dp")
    feats = rows.shape[1]
    half = feats // 2
    width = gate.shape[2]
    tiles = width // tile
    near = pl.ds(pl.multiple_of(x * half, half), half)
    far = pl.ds(pl.multiple_of((1 - x) * half, half), half)

    row_copies = []
    offsets = []
    at = 0
    for i, piece in enumerate(pieces):
        part = piece.shape[0]
        offsets.append((at, part))
        for s, lanes in enumerate((near, far)):
            copy = pltpu.make_async_copy(
                piece.at[:, lanes],
                rows.at[pl.ds(at, part), pl.ds(s * half, half)],
                row_sem.at[2 * i + s],
            )
            copy.start()
            row_copies.append(copy)
        at += part
    weight_copies = []
    down_copies = []
    sem = 0
    for e in range(2):
        mine = weights[e * per_expert : (e + 1) * per_expert]
        for j in range(tiles):
            group = []
            for sources, target in ((mine[:n_gate], gate), (mine[n_gate:-1], up)):
                depth_at = 0
                for source in sources:
                    copy = pltpu.make_async_copy(
                        source.at[:, pl.ds(j * tile, tile)],
                        target.at[e, pl.ds(depth_at, source.shape[0]), pl.ds(j * tile, tile)],
                        weight_sem.at[sem],
                    )
                    copy.start()
                    group.append(copy)
                    depth_at += source.shape[0]
                    sem += 1
            weight_copies.append(group)
    units = weights[-1].shape[0]
    spare = width - units
    for e in range(2):
        start = pl.multiple_of(e * width + x * spare, 16)
        copy = pltpu.make_async_copy(
            weights[(e + 1) * per_expert - 1], down.at[pl.ds(start, units), :], down_sem.at[e]
        )
        copy.start()
        down_copies.append(copy)
        if spare:
            blank = pl.multiple_of(e * width + (1 - x) * units, 16)
            down[pl.ds(blank, spare), :] = jnp.zeros((spare, feats), down.dtype)

    for copy in row_copies:
        copy.wait()
    for e in range(2):
        scale = share[:, e : e + 1]
        for j in range(tiles):
            for copy in weight_copies[e * tiles + j]:
                copy.wait()
            lanes = pl.ds(j * tile, tile)
            g = jnp.dot(rows[...], gate[e, :, lanes], preferred_element_type=jnp.float32)
            u = jnp.dot(rows[...], up[e, :, lanes], preferred_element_type=jnp.float32)
            h = g / (1.0 + jnp.exp(-g)) * u * scale
            mid[:, pl.ds(e * width + j * tile, tile)] = h.astype(mid.dtype)
    for copy in down_copies:
        copy.wait()
    for n in range(feats // out_tile):
        lanes = pl.ds(n * out_tile, out_tile)
        total = jnp.dot(mid[...], down[:, lanes], preferred_element_type=jnp.float32)
        for (first, part), out in zip(offsets, outs):
            out[:, lanes] = total[first : first + part].astype(out.dtype)


def run_experts(pieces, kinds, share, experts_weights):
    feats = pieces[0].shape[1]
    width = experts_weights[0][0][0].shape[1]
    n_gate, n_up = len(experts_weights[0][0]), len(experts_weights[0][1])
    weights = [
        array for gate, up, down in experts_weights for array in list(gate) + list(up) + [down]
    ]
    count = len(pieces)
    total = sum(piece.shape[0] for piece in pieces)
    tile = 256
    any_spec = pl.BlockSpec(memory_space=pl.ANY)
    vmem_spec = pl.BlockSpec(memory_space=pltpu.VMEM)
    return pl.pallas_call(
        functools.partial(experts_kernel, tile, 512, count, n_gate, n_up),
        out_shape=tuple(
            jax.ShapeDtypeStruct(piece.shape, kind) for piece, kind in zip(pieces, kinds)
        ),
        in_specs=[any_spec] * count + [vmem_spec] + [any_spec] * len(weights),
        out_specs=(vmem_spec,) * count,
        scratch_shapes=[
            pltpu.VMEM((total, feats), jnp.bfloat16),
            pltpu.VMEM((2, feats, width), jnp.bfloat16),
            pltpu.VMEM((2, feats, width), jnp.bfloat16),
            pltpu.VMEM((2 * width, feats), jnp.bfloat16),
            pltpu.VMEM((total, 2 * width), jnp.bfloat16),
            pltpu.SemaphoreType.DMA((2 * count,)),
            pltpu.SemaphoreType.DMA((2 * (n_gate + n_up) * (width // tile),)),
            pltpu.SemaphoreType.DMA((2,)),
        ],
        compiler_params=pltpu.CompilerParams(vmem_limit_bytes=34 * MIB),
        cost_estimate=pl.CostEstimate(
            flops=2 * total * feats * width * 6,
            bytes_accessed=12 * feats * width + 12 * total * feats,
            transcendentals=total * width * 2,
        ),
        name="experts",
    )(*pieces, share, *weights)


def gathered(
    queries,
    kv_pool,
    page_table,
    ctx_lens,
    w_out,
    residual,
    moe_gain,
    expert_ids,
    route_weights,
    w_gate,
    w_up,
    w_down,
    final_gain,
):
    experts = lax.axis_size("expert")
    depth = experts // 4
    me = lax.axis_index("expert")
    x = lax.axis_index("dp")
    c = me % 2
    first = x == 0
    feats = residual.shape[1]
    block = residual.shape[0]
    units = w_gate.shape[2]
    units_here = w_down.shape[1]
    width = -(-units_here // 256) * 256

    def own_part(weights):
        return jnp.where(first, weights[:, :width], weights[:, units - width :])

    def sent_part(weights):
        return jnp.where(first, weights[:, units - width :], weights[:, :width])

    deep = w_gate.shape[1] * 5 // 8
    gate_sent = [sent_part(w_gate[0, :deep]), sent_part(w_gate[0, deep:])]
    gate_own = own_part(w_gate[0])
    gate_far = [flip_x(piece) for piece in gate_sent]

    near = [w_out] + [shift_z(w_out, depth, s) for s in range(1, depth)]
    across_own = flip_y(w_out, depth)

    queries, gate_sent[0], gate_sent[1], gate_own = lax.optimization_barrier(
        (queries, gate_sent[0], gate_sent[1], gate_own)
    )
    context = attend(queries, kv_pool, page_table, ctx_lens)
    near[1:], across_own, gate_far[0], context, w_up, w_down, route_weights, gate_own = (
        lax.optimization_barrier(
            (
                near[1:],
                across_own,
                gate_far[0],
                context,
                w_up,
                w_down,
                route_weights,
                gate_own,
            )
        )
    )
    across = [across_own] + [flip_y(piece, depth) for piece in near[1:]]
    across[1], across[2], across[3], gate_far[1] = lax.optimization_barrier(
        (across[1], across[2], across[3], gate_far[1])
    )
    columns = near + across
    columns = columns + [flip_core(piece, depth) for piece in columns]

    deep = w_up.shape[1] // 2
    up_sent = [sent_part(w_up[0, :deep]), sent_part(w_up[0, deep:])]
    up_own = own_part(w_up[0])
    down_own = w_down[0]
    here_core = [flip_core(array, depth) for array in (gate_own, up_own, down_own)]

    named = expert_ids[:, :, None] == jnp.arange(experts, dtype=jnp.int32)[None, None, :]
    share = jnp.sum(jnp.where(named, route_weights[:, :, None], 0.0), axis=1)
    both = jnp.stack([me, me + 1 - 2 * c])
    pick = both[:, None] == jnp.arange(experts, dtype=jnp.int32)[None, :]
    share_l = jnp.stack([share] + [shift_z(share, depth, s) for s in range(1, depth)])
    share_x = flip_x(share_l)
    share_y = flip_y(share_l, depth)
    share_d = flip_y(share_x, depth)
    shares = jnp.stack([share_l, share_x, share_y, share_d])
    shares = jnp.stack(
        [jnp.sum(jnp.where(pick[i], shares, 0.0), axis=-1) for i in range(2)], axis=-1
    )

    own, sent = project(context, columns, depth)
    own, sent, shares, here_core[0], here_core[1], here_core[2] = lax.optimization_barrier(
        (own, sent, shares, here_core[0], here_core[1], here_core[2])
    )
    received, up_sent[0], up_sent[1] = lax.optimization_barrier(
        (flip_x(sent), up_sent[0], up_sent[1])
    )
    up_far = [flip_x(piece) for piece in up_sent]
    gate_far_core = [flip_core(piece, depth) for piece in gate_far]
    hidden_state = residual.astype(jnp.float32) + (own + received.astype(jnp.float32))
    moe_input = normalize(hidden_state, moe_gain).astype(jnp.bfloat16)

    mid_z = depth // 2
    ready = []
    at = 0
    arrived = [moe_input] + [shift_z(moe_input, depth, s) for s in range(1, depth)]
    for rows in (block // 2, block // 2):
        line = jnp.stack([piece[at : at + rows] for piece in arrived])
        line_x = flip_x(line)
        line_y = flip_y(line, depth)
        low = flip_y(line_x[:mid_z], depth)
        high = flip_x(line_y[mid_z:])
        share = shares[:, :, at : at + rows].reshape(4 * depth * rows, 2)
        ready.append(([line, line_x, line_y, low, high], share))
        at += rows

    ready[0][0][1], up_far[0] = lax.optimization_barrier((ready[0][0][1], up_far[0]))
    ready[0][0][3], ready[0][0][4], up_far[1] = lax.optimization_barrier(
        (ready[0][0][3], ready[0][0][4], up_far[1])
    )
    up_far_core = [flip_core(piece, depth) for piece in up_far]
    weights = [
        ([gate_own] + gate_far, [up_own] + up_far, down_own),
        ([here_core[0]] + gate_far_core, [here_core[1]] + up_far_core, here_core[2]),
    ]

    moe = []
    for pieces, share in ready:
        out_l, out_x, out_y, out_low, out_high = run_experts(
            [piece.reshape(-1, feats) for piece in pieces],
            (jnp.float32, jnp.float32, jnp.float32, jnp.bfloat16, jnp.bfloat16),
            share,
            weights,
        )
        out_l = out_l.reshape(pieces[0].shape)
        out_x = out_x.reshape(pieces[0].shape)
        out_y = out_y.reshape(pieces[0].shape)
        back_low = flip_y(out_low, depth).reshape(pieces[3].shape).astype(jnp.float32)
        back_high = flip_x(out_high).reshape(pieces[4].shape).astype(jnp.float32)
        sum_x = jnp.concatenate([out_x[:mid_z] + back_low, out_x[mid_z:]], axis=0)
        sum_y = jnp.concatenate([out_y[:mid_z], out_y[mid_z:] + back_high], axis=0)
        back_x = flip_x(sum_x.astype(jnp.bfloat16)).astype(jnp.float32)
        back_y = flip_y(sum_y.astype(jnp.bfloat16), depth).astype(jnp.float32)
        full = out_l + back_x + back_y
        total = full[0]
        for s in range(1, depth):
            total = total + shift_z(full[s].astype(jnp.bfloat16), depth, depth - s).astype(
                jnp.float32
            )
        moe.append(total)
    combined = hidden_state + jnp.concatenate(moe, axis=0)
    return normalize(combined, final_gain).astype(jnp.bfloat16)


def solution(mesh):
    few = mesh.shape["dp"] == 2 and mesh.shape["expert"] == 16
    return jax.shard_map(
        gathered if few else dispatched,
        mesh=mesh,
        in_specs=(
            P("expert", "dp"),
            P(None, "expert", None, "dp"),
            P("expert", None),
            P("expert"),
            P("dp", "expert"),
            P(("expert", "dp"), None),
            P(),
            P(("expert", "dp"), None),
            P(("expert", "dp"), None),
            P("expert", "dp", None),
            P("expert", "dp", None),
            P("expert", "dp", None),
            P(),
        ),
        out_specs=P(("expert", "dp"), None),
        check_vma=False,
    )
```

```python
import functools
import math

import jax
import jax.numpy as jnp
from jax import lax
from jax.experimental import pallas as pl
from jax.experimental.pallas import tpu as pltpu
from jax.sharding import PartitionSpec as P

HD = 128
TOP = 6
CTX = 256
MIB = 1024 * 1024


def normalize(values, gain):
    mean_sq = jnp.mean(values * values, axis=-1, keepdims=True)
    return values * lax.rsqrt(mean_sq + 1e-06) * gain


def attend(queries, kv_pool, page_table, ctx_lens):
    scale = 1.0 / math.sqrt(HD)
    group_rows = queries.shape[0]
    local_feats = queries.shape[1]
    local_heads = local_feats // HD
    seq_count = page_table.shape[0]
    seq_rows = group_rows // seq_count
    pool_here = kv_pool.shape[1]
    local_pages = page_table - lax.axis_index("expert") * pool_here
    keys = kv_pool[0][local_pages].reshape(seq_count, CTX, local_heads, HD)
    values = kv_pool[1][local_pages].reshape(seq_count, CTX, local_heads, HD)
    asked = queries.reshape(seq_count, seq_rows, local_heads, HD)
    scores = jnp.einsum("sqhd,skhd->shqk", asked, keys, preferred_element_type=jnp.float32) * scale
    lengths = ctx_lens.reshape(seq_count, seq_rows)
    visible = (jnp.arange(CTX, dtype=jnp.int32)[None, None, :] < lengths[:, :, None])[:, None]
    scores = jnp.where(visible, scores, -1e30)
    top_score = jnp.max(scores, axis=-1, keepdims=True)
    expo = jnp.where(visible, jnp.exp(scores - top_score), 0.0)
    probs = (expo / jnp.sum(expo, axis=-1, keepdims=True)).astype(jnp.bfloat16)
    mixed = jnp.einsum("shqk,skhd->sqhd", probs, values, preferred_element_type=jnp.float32)
    return mixed.astype(jnp.bfloat16).reshape(group_rows, local_feats)


def dispatched(
    queries,
    kv_pool,
    page_table,
    ctx_lens,
    w_out,
    residual,
    moe_gain,
    expert_ids,
    route_weights,
    w_gate,
    w_up,
    w_down,
    final_gain,
):
    context = attend(queries, kv_pool, page_table, ctx_lens)
    columns = lax.all_gather(w_out, "expert", axis=1, tiled=True)
    projected = lax.psum_scatter(
        jnp.dot(context, columns, preferred_element_type=jnp.float32).astype(jnp.bfloat16),
        "dp",
        scatter_dimension=0,
        tiled=True,
    ).astype(jnp.float32)
    hidden_state = residual.astype(jnp.float32) + projected
    moe_input = normalize(hidden_state, moe_gain).astype(jnp.bfloat16)
    rows_here = moe_input.shape[0]
    experts = lax.axis_size("expert")
    slots = max(2, min(rows_here, 2 * rows_here * TOP // experts))
    flat_ids = expert_ids.reshape(-1)
    marks = (flat_ids[:, None] == jnp.arange(experts, dtype=jnp.int32)[None, :]).astype(jnp.int32)
    before = jnp.sum((jnp.cumsum(marks, axis=0) - 1) * marks, axis=1)
    target = (flat_ids * slots + before).reshape(rows_here, TOP)
    placing = jnp.any(
        jnp.arange(experts * slots, dtype=jnp.int32)[:, None, None] == target[None], axis=-1
    )
    outbound = jnp.dot(placing.astype(jnp.bfloat16), moe_input, preferred_element_type=jnp.float32)
    outbound = outbound.astype(jnp.bfloat16).reshape(experts, slots, moe_input.shape[1])
    gate_full = lax.all_gather(w_gate, "dp", axis=1, tiled=True)
    up_full = lax.all_gather(w_up, "dp", axis=1, tiled=True)
    down_full = lax.all_gather(w_down, "dp", axis=1, tiled=True)
    arrived = lax.all_to_all(outbound, "expert", split_axis=0, concat_axis=0, tiled=True)
    flat = arrived.reshape(-1, arrived.shape[2])
    gate = jnp.dot(flat, gate_full[0], preferred_element_type=jnp.float32)
    up_part = jnp.dot(flat, up_full[0], preferred_element_type=jnp.float32)
    expert_mid = (jax.nn.silu(gate) * up_part).astype(jnp.bfloat16)
    done = jnp.dot(expert_mid, down_full[0], preferred_element_type=jnp.float32).astype(
        jnp.bfloat16
    )
    done = done.reshape(arrived.shape[0], arrived.shape[1], arrived.shape[2])
    returned = lax.all_to_all(done, "expert", split_axis=0, concat_axis=0, tiled=True)
    answers = returned.reshape(experts * slots, returned.shape[2])[target]
    moe = jnp.sum(route_weights[:, :, None] * answers.astype(jnp.float32), axis=1)
    combined = hidden_state + moe
    return normalize(combined, final_gain).astype(jnp.bfloat16)


def place(z, y, c):
    return (z * 2 + y) * 2 + c


def shift_z(values, depth, step):
    pairs = [
        (place((z + step) % depth, y, c), place(z, y, c))
        for z in range(depth)
        for y in range(2)
        for c in range(2)
    ]
    return lax.ppermute(values, "expert", pairs)


def flip_y(values, depth):
    pairs = [
        (place(z, 1 - y, c), place(z, y, c))
        for z in range(depth)
        for y in range(2)
        for c in range(2)
    ]
    return lax.ppermute(values, "expert", pairs)


def flip_core(values, depth):
    pairs = [
        (place(z, y, 1 - c), place(z, y, c))
        for z in range(depth)
        for y in range(2)
        for c in range(2)
    ]
    return lax.ppermute(values, "expert", pairs)


def flip_x(values):
    return lax.ppermute(values, "dp", [(0, 1), (1, 0)])


def attend_kernel(pages_ref, lens_ref, q_ref, kv_ref, out_ref):
    scale = 1.0 / math.sqrt(HD)
    seqs, slots = pages_ref.shape
    rows, feats = q_ref.shape
    each = rows // seqs
    page = kv_ref.shape[2]
    first_page = lax.axis_index("expert") * kv_ref.shape[1]
    place_in = lax.broadcasted_iota(jnp.int32, (each, slots * page), 1)
    for s in range(seqs):
        here = slice(s * each, (s + 1) * each)
        pages = [pages_ref[s, p] - first_page for p in range(slots)]
        keys = jnp.concatenate([kv_ref[0, p] for p in pages], axis=0)
        values = jnp.concatenate([kv_ref[1, p] for p in pages], axis=0)
        visible = place_in < lens_ref[here, :]
        for h in range(feats // HD):
            lanes = slice(h * HD, (h + 1) * HD)
            scores = lax.dot_general(
                q_ref[here, lanes],
                keys[:, lanes],
                (((1,), (1,)), ((), ())),
                preferred_element_type=jnp.float32,
            )
            scores = jnp.where(visible, scores * scale, -1e30)
            top_score = jnp.max(scores, axis=-1, keepdims=True)
            expo = jnp.where(visible, jnp.exp(scores - top_score), 0.0)
            probs = (expo / jnp.sum(expo, axis=-1, keepdims=True)).astype(jnp.bfloat16)
            mixed = jnp.dot(probs, values[:, lanes], preferred_element_type=jnp.float32)
            out_ref[here, lanes] = mixed.astype(out_ref.dtype)


def attend_here(queries, kv_pool, page_table, ctx_lens):
    vmem_spec = pl.BlockSpec(memory_space=pltpu.VMEM)
    return pl.pallas_call(
        attend_kernel,
        out_shape=jax.ShapeDtypeStruct(queries.shape, jnp.bfloat16),
        in_specs=[pl.BlockSpec(memory_space=pltpu.SMEM)] + [vmem_spec] * 3,
        out_specs=vmem_spec,
        compiler_params=pltpu.CompilerParams(vmem_limit_bytes=16 * MIB),
        cost_estimate=pl.CostEstimate(
            flops=4 * queries.size * CTX,
            bytes_accessed=2 * kv_pool.size + 4 * queries.size,
            transcendentals=queries.size * CTX // HD,
        ),
        name="attend",
    )(page_table, ctx_lens[:, None], queries, kv_pool)


def project_kernel(depth, ctx_ref, other_ref, *refs):
    pieces, (kept_ref, sent_ref) = refs[:-2], refs[-2:]
    half = ctx_ref.shape[0] // 2
    width = pieces[0].shape[1]
    me = lax.axis_index("expert")
    x = lax.axis_index("dp")
    y = lax.rem(lax.div(me, 2), 2)
    z = lax.div(me, 4)
    mine = pl.ds(pl.multiple_of(x * half, half), half)
    theirs = pl.ds(pl.multiple_of((1 - x) * half, half), half)
    rows = jnp.concatenate(
        [ctx_ref[mine, :], other_ref[mine, :], ctx_ref[theirs, :], other_ref[theirs, :]], axis=0
    )
    for flip in range(2):
        at_y = y if flip == 0 else 1 - y
        for r in range(depth):
            total = jnp.dot(rows, pieces[flip * depth + r][...], preferred_element_type=jnp.float32)
            index = lax.rem(z + r, depth) * 2 + at_y
            columns = pl.ds(pl.multiple_of(index * width, width), width)
            kept_ref[:, columns] = total[: 2 * half]
            sent_ref[:, columns] = total[2 * half :].astype(sent_ref.dtype)


def project(context, other, pieces, depth):
    rows, feats = context.shape
    columns = pieces[0].shape[1] * 2 * depth
    return pl.pallas_call(
        functools.partial(project_kernel, depth),
        out_shape=(
            jax.ShapeDtypeStruct((rows, columns), jnp.float32),
            jax.ShapeDtypeStruct((rows, columns), jnp.bfloat16),
        ),
        compiler_params=pltpu.CompilerParams(vmem_limit_bytes=16 * MIB),
        cost_estimate=pl.CostEstimate(
            flops=4 * rows * feats * columns,
            bytes_accessed=2 * feats * columns + 6 * rows * columns,
            transcendentals=0,
        ),
        name="project",
    )(context, other, *pieces)


def join_kernel(width, mine_ref, other_ref, residual_ref, gain_ref, share_ref, hidden_ref, out_ref):
    c = lax.rem(lax.axis_index("expert"), 2)
    feats = residual_ref.shape[1]
    for i in range(feats // (2 * width)):
        source = slice(i * width, (i + 1) * width)
        for own, ref in ((True, mine_ref), (False, other_ref)):
            index = 2 * i + (c if own else 1 - c)
            columns = pl.ds(pl.multiple_of(index * width, width), width)
            hidden_ref[:, columns] = ref[:, source]
    hidden = residual_ref[...].astype(jnp.float32) + hidden_ref[...]
    hidden_ref[...] = hidden
    mean_sq = jnp.mean(hidden * hidden, axis=-1, keepdims=True)
    out_ref[:, :feats] = (hidden * lax.rsqrt(mean_sq + 1e-06) * gain_ref[...]).astype(
        out_ref.dtype
    )
    out_ref[:, feats:] = share_ref[...]


def join(mine, other, residual, gain, share, width):
    rows, feats = residual.shape
    return pl.pallas_call(
        functools.partial(join_kernel, width),
        out_shape=(
            jax.ShapeDtypeStruct((rows, feats), jnp.float32),
            jax.ShapeDtypeStruct((rows, feats + share.shape[1]), jnp.bfloat16),
        ),
        compiler_params=pltpu.CompilerParams(vmem_limit_bytes=16 * MIB),
        cost_estimate=pl.CostEstimate(
            flops=6 * rows * feats, bytes_accessed=12 * rows * feats, transcendentals=rows
        ),
        name="join",
    )(mine, other, residual, gain[None, :], share)


def cut_kernel(width, w_ref, *refs):
    outs, sems = refs[:-1], refs[-1]
    x = lax.axis_index("dp")
    units = w_ref.shape[2]
    low = x * (units - width)
    high = (1 - x) * (units - width)
    copies = []
    at = 0
    for i, out in enumerate(outs):
        start = pl.multiple_of(high if i > 0 else low, 128)
        source_at = 0 if i == 0 else at
        copy = pltpu.make_async_copy(
            w_ref.at[0, pl.ds(source_at, out.shape[0]), pl.ds(start, width)], out, sems.at[i]
        )
        copy.start()
        copies.append(copy)
        if i > 0:
            at += out.shape[0]
    for copy in copies:
        copy.wait()


def cut(weights, width, parts):
    depth = weights.shape[1]
    shapes = [depth] + list(parts)
    any_spec = pl.BlockSpec(memory_space=pl.ANY)
    return pl.pallas_call(
        functools.partial(cut_kernel, width),
        out_shape=tuple(jax.ShapeDtypeStruct((n, width), weights.dtype) for n in shapes),
        in_specs=[any_spec],
        out_specs=(pl.BlockSpec(memory_space=pltpu.VMEM),) * len(shapes),
        scratch_shapes=[pltpu.SemaphoreType.DMA((len(shapes),))],
        cost_estimate=pl.CostEstimate(
            flops=0, bytes_accessed=8 * depth * width, transcendentals=0
        ),
        compiler_params=pltpu.CompilerParams(vmem_limit_bytes=16 * MIB),
        name="cut",
    )(weights)


SLOTS = 3


def experts_kernel(tile, out_tile, first_row, count, n_gate, n_up, *refs):
    per_expert = n_gate + n_up + 1
    pieces, refs = refs[:count], refs[count:]
    weights, refs = refs[: 2 * per_expert], refs[2 * per_expert :]
    outs, refs = refs[:count], refs[count:]
    rows, share, gate, up, down, mid, row_sem, weight_sem, down_sem = refs
    x = lax.axis_index("dp")
    me = lax.axis_index("expert")
    feats = rows.shape[2]
    blocks, each = rows.shape[0], rows.shape[1]
    half = feats // 2
    width = down.shape[0] // 2
    tiles = width // tile
    near = pl.ds(pl.multiple_of(x * half, half), half)
    far = pl.ds(pl.multiple_of((1 - x) * half, half), half)
    taken = pl.ds(first_row, each)

    row_copies = []
    spans = []
    at = 0
    for i, piece in enumerate(pieces):
        part = piece.shape[0]
        spans.append((at * each, part * each))
        here = pl.ds(at, part)
        for s, (source, target) in enumerate(
            (
                (piece.at[:, taken, near], rows.at[here, :, pl.ds(0, half)]),
                (piece.at[:, taken, far], rows.at[here, :, pl.ds(half, half)]),
                (piece.at[:, taken, pl.ds(feats, 128)], share.at[here]),
            )
        ):
            copy = pltpu.make_async_copy(source, target, row_sem.at[3 * i + s])
            copy.start()
            row_copies.append(copy)
        at += part

    def fetch(t):
        e, j = t // tiles, t % tiles
        mine = weights[e * per_expert : (e + 1) * per_expert]
        group = []
        sem = (n_gate + n_up) * (t % SLOTS)
        for sources, target in ((mine[:n_gate], gate), (mine[n_gate:-1], up)):
            depth_at = 0
            for source in sources:
                copy = pltpu.make_async_copy(
                    source.at[:, pl.ds(j * tile, tile)],
                    target.at[t % SLOTS, pl.ds(depth_at, source.shape[0]), :],
                    weight_sem.at[sem],
                )
                copy.start()
                group.append(copy)
                depth_at += source.shape[0]
                sem += 1
        return group

    weight_copies = [fetch(t) for t in range(SLOTS)]
    units = weights[-1].shape[0]
    spare = width - units
    down_copies = []
    for e in range(2):
        start = pl.multiple_of(e * width + x * spare, 16)
        copy = pltpu.make_async_copy(
            weights[(e + 1) * per_expert - 1], down.at[pl.ds(start, units), :], down_sem.at[e]
        )
        copy.start()
        down_copies.append(copy)
        if spare:
            blank = pl.multiple_of(e * width + (1 - x) * units, 16)
            down[pl.ds(blank, spare), :] = jnp.zeros((spare, feats), down.dtype)

    for copy in row_copies:
        copy.wait()
    total_rows = blocks * each
    shares = share[...].reshape(total_rows, 128).astype(jnp.float32)
    lane = lax.broadcasted_iota(jnp.int32, (total_rows, 128), 1)
    experts = lax.axis_size("expert")
    for t in range(2 * tiles):
        e, j = t // tiles, t % tiles
        if j == 0:
            chosen = me if e == 0 else me + 1 - 2 * lax.rem(me, 2)
            hit = (lane == chosen) | (lane == chosen + experts)
            scale = jnp.sum(jnp.where(hit, shares, 0.0), axis=1, keepdims=True)
        for copy in weight_copies[t]:
            copy.wait()
        values = rows[...].reshape(total_rows, feats)
        g = jnp.dot(values, gate[t % SLOTS], preferred_element_type=jnp.float32)
        u = jnp.dot(values, up[t % SLOTS], preferred_element_type=jnp.float32)
        h = g / (1.0 + jnp.exp(-g)) * u * scale
        mid[:, pl.ds(t * tile, tile)] = h.astype(mid.dtype)
        if t + SLOTS < 2 * tiles:
            weight_copies.append(fetch(t + SLOTS))
    for copy in down_copies:
        copy.wait()
    for n in range(feats // out_tile):
        lanes = pl.ds(n * out_tile, out_tile)
        total = jnp.dot(mid[...], down[:, lanes], preferred_element_type=jnp.float32)
        for (first, part), out in zip(spans, outs):
            out[:, lanes] = total[first : first + part].astype(out.dtype)


def run_experts(pieces, kinds, first_row, each, experts_weights):
    feats = experts_weights[0][2].shape[1]
    width = experts_weights[0][0][0].shape[1]
    n_gate, n_up = len(experts_weights[0][0]), len(experts_weights[0][1])
    weights = [
        array for gate, up, down in experts_weights for array in list(gate) + list(up) + [down]
    ]
    count = len(pieces)
    blocks = sum(piece.shape[0] for piece in pieces)
    total = blocks * each
    tile = 256
    any_spec = pl.BlockSpec(memory_space=pl.ANY)
    vmem_spec = pl.BlockSpec(memory_space=pltpu.VMEM)
    return pl.pallas_call(
        functools.partial(experts_kernel, tile, 512, first_row, count, n_gate, n_up),
        out_shape=tuple(
            jax.ShapeDtypeStruct((piece.shape[0] * each, feats), kind)
            for piece, kind in zip(pieces, kinds)
        ),
        in_specs=[any_spec] * (count + len(weights)),
        out_specs=(vmem_spec,) * count,
        scratch_shapes=[
            pltpu.VMEM((blocks, each, feats), jnp.bfloat16),
            pltpu.VMEM((blocks, each, 128), jnp.bfloat16),
            pltpu.VMEM((SLOTS, feats, tile), jnp.bfloat16),
            pltpu.VMEM((SLOTS, feats, tile), jnp.bfloat16),
            pltpu.VMEM((2 * width, feats), jnp.bfloat16),
            pltpu.VMEM((total, 2 * width), jnp.bfloat16),
            pltpu.SemaphoreType.DMA((3 * count,)),
            pltpu.SemaphoreType.DMA((SLOTS * (n_gate + n_up),)),
            pltpu.SemaphoreType.DMA((2,)),
        ],
        compiler_params=pltpu.CompilerParams(vmem_limit_bytes=30 * MIB),
        cost_estimate=pl.CostEstimate(
            flops=2 * total * feats * width * 6,
            bytes_accessed=12 * feats * width + 12 * total * feats,
            transcendentals=total * width * 2,
        ),
        name="experts",
    )(*pieces, *weights)


def send_sides(out_l, out_x, out_y, far, k, depth):
    if k % 2 == 0:
        out_x = out_x + far.astype(jnp.float32)
    else:
        out_y = out_y + far.astype(jnp.float32)
    return (
        out_l,
        flip_x(out_x.astype(jnp.bfloat16)),
        flip_y(out_y.astype(jnp.bfloat16), depth),
    )


def send_line(out_l, back_x, back_y, depth):
    full = out_l + back_x.astype(jnp.float32) + back_y.astype(jnp.float32)
    full = full.reshape(depth, -1, full.shape[1])
    total = full[0]
    for s in range(1, depth):
        back = shift_z(full[s].astype(jnp.bfloat16), depth, depth - s)
        total = total + back.astype(jnp.float32)
    return total


def gathered(
    queries,
    kv_pool,
    page_table,
    ctx_lens,
    w_out,
    residual,
    moe_gain,
    expert_ids,
    route_weights,
    w_gate,
    w_up,
    w_down,
    final_gain,
):
    experts = lax.axis_size("expert")
    depth = experts // 4
    feats = residual.shape[1]
    block = residual.shape[0]
    units_here = w_down.shape[1]
    width = -(-units_here // 256) * 256
    barrier = lax.optimization_barrier

    near = [w_out] + [shift_z(w_out, depth, s) for s in range(1, depth)]
    across_own = flip_y(w_out, depth)

    feats_here = w_gate.shape[1]
    early = feats_here * 7 // 16
    gate_own, *gate_sent = cut(w_gate, width, (early, feats_here - early))
    gate_far = [flip_x(piece) for piece in gate_sent]
    queries, gate_sent = barrier((queries, gate_sent))
    context = attend_here(queries, kv_pool, page_table, ctx_lens)
    near[1:], across_own, gate_far[0], gate_sent[1], w_up, w_down, gate_own, context = barrier(
        (near[1:], across_own, gate_far[0], gate_sent[1], w_up, w_down, gate_own, context)
    )
    other = flip_core(context, depth)
    gate_far[1] = flip_x(gate_sent[1])
    across = [across_own] + [flip_y(piece, depth) for piece in near[1:]]
    early = feats_here // 4
    up_own, *up_sent = cut(w_up, width, (early, feats_here - early))
    up_early = flip_x(up_sent[0])
    down_own = w_down[0]
    here_core = [flip_core(array, depth) for array in (gate_own, up_own, down_own)]

    named = expert_ids[:, :, None] == jnp.arange(experts, dtype=jnp.int32)[None, None, :]
    share = jnp.sum(jnp.where(named, route_weights[:, :, None], 0.0), axis=1)
    share_high = share.astype(jnp.bfloat16)
    share_low = (share - share_high.astype(jnp.float32)).astype(jnp.bfloat16)
    share = jnp.concatenate(
        [share_high, share_low, jnp.zeros((block, 128 - 2 * experts), jnp.bfloat16)], axis=1
    )

    across, share, here_core = barrier((across, share, here_core))
    kept, sent = project(context, other, near + across, depth)
    kept, sent, gate_far[1] = barrier((kept, sent, gate_far[1]))
    received, up_sent[1], up_early = barrier((flip_x(sent), up_sent[1], up_early))
    up_far = [up_early, flip_x(up_sent[1])]
    gate_far_core = [flip_core(piece, depth) for piece in gate_far]
    total = kept + received.astype(jnp.float32)
    back = flip_core(total[block:], depth)
    hidden_state, message = join(total[:block], back, residual, moe_gain, share, w_out.shape[1])

    line = jnp.stack([message] + [shift_z(message, depth, s) for s in range(1, depth)])
    line_x, up_far[1] = barrier((flip_x(line), up_far[1]))
    line_y = flip_y(line, depth)
    mid_z = depth // 2
    low = flip_y(line_x[:mid_z], depth)
    high = flip_x(line_y[mid_z:])
    up_far_core = [flip_core(piece, depth) for piece in up_far]
    weights = [
        ([gate_own] + gate_far, [up_own] + up_far, down_own),
        ([here_core[0]] + gate_far_core, [here_core[1]] + up_far_core, here_core[2]),
    ]

    moe = []
    diagonal = []
    sides = []
    at = 0
    quarter = block // 4
    for k, each in enumerate((quarter, 2 * quarter, quarter)):
        outs = run_experts(
            [line, line_x, line_y, low, high],
            (jnp.float32, jnp.float32, jnp.float32, jnp.bfloat16, jnp.bfloat16),
            at,
            each,
            weights,
        )
        at += each
        if k > 0:
            outs, diagonal[k - 1] = barrier((outs, diagonal[k - 1]))
            sides.append(send_sides(*diagonal[k - 1], k - 1, depth))
        if k > 1:
            outs, sides[k - 2] = barrier((outs, sides[k - 2]))
            moe.append(send_line(*sides[k - 2], depth))
        line, outs = barrier((line, outs))
        out_l, out_x, out_y, out_low, out_high = outs
        far = jnp.concatenate([out_low, out_high], axis=0)
        far = flip_y(far, depth) if k % 2 == 0 else flip_x(far)
        diagonal.append((out_l, out_x, out_y, far))
    sides.append(send_sides(*diagonal[-1], len(diagonal) - 1, depth))
    for side in sides[-2:]:
        moe.append(send_line(*side, depth))
    combined = hidden_state + jnp.concatenate(moe, axis=0)
    return normalize(combined, final_gain).astype(jnp.bfloat16)


def solution(mesh):
    few = mesh.shape["dp"] == 2 and mesh.shape["expert"] == 16
    return jax.shard_map(
        gathered if few else dispatched,
        mesh=mesh,
        in_specs=(
            P("expert", "dp"),
            P(None, "expert", None, "dp"),
            P("expert", None),
            P("expert"),
            P("dp", "expert"),
            P(("expert", "dp"), None),
            P(),
            P(("expert", "dp"), None),
            P(("expert", "dp"), None),
            P("expert", "dp", None),
            P("expert", "dp", None),
            P("expert", "dp", None),
            P(),
        ),
        out_specs=P(("expert", "dp"), None),
        check_vma=False,
    )
```

```python
import functools
import math

import jax
import jax.numpy as jnp
from jax import lax
from jax.experimental import pallas as pl
from jax.experimental.pallas import tpu as pltpu
from jax.sharding import PartitionSpec as P

HD = 128
TOP = 6
CTX = 256
MIB = 1024 * 1024


def normalize(values, gain):
    mean_sq = jnp.mean(values * values, axis=-1, keepdims=True)
    return values * lax.rsqrt(mean_sq + 1e-06) * gain


def attend(queries, kv_pool, page_table, ctx_lens):
    scale = 1.0 / math.sqrt(HD)
    group_rows = queries.shape[0]
    local_feats = queries.shape[1]
    local_heads = local_feats // HD
    seq_count = page_table.shape[0]
    seq_rows = group_rows // seq_count
    pool_here = kv_pool.shape[1]
    local_pages = page_table - lax.axis_index("expert") * pool_here
    keys = kv_pool[0][local_pages].reshape(seq_count, CTX, local_heads, HD)
    values = kv_pool[1][local_pages].reshape(seq_count, CTX, local_heads, HD)
    asked = queries.reshape(seq_count, seq_rows, local_heads, HD)
    scores = jnp.einsum("sqhd,skhd->shqk", asked, keys, preferred_element_type=jnp.float32) * scale
    lengths = ctx_lens.reshape(seq_count, seq_rows)
    visible = (jnp.arange(CTX, dtype=jnp.int32)[None, None, :] < lengths[:, :, None])[:, None]
    scores = jnp.where(visible, scores, -1e30)
    top_score = jnp.max(scores, axis=-1, keepdims=True)
    expo = jnp.where(visible, jnp.exp(scores - top_score), 0.0)
    probs = (expo / jnp.sum(expo, axis=-1, keepdims=True)).astype(jnp.bfloat16)
    mixed = jnp.einsum("shqk,skhd->sqhd", probs, values, preferred_element_type=jnp.float32)
    return mixed.astype(jnp.bfloat16).reshape(group_rows, local_feats)


def dispatched(
    queries,
    kv_pool,
    page_table,
    ctx_lens,
    w_out,
    residual,
    moe_gain,
    expert_ids,
    route_weights,
    w_gate,
    w_up,
    w_down,
    final_gain,
):
    context = attend(queries, kv_pool, page_table, ctx_lens)
    columns = lax.all_gather(w_out, "expert", axis=1, tiled=True)
    projected = lax.psum_scatter(
        jnp.dot(context, columns, preferred_element_type=jnp.float32).astype(jnp.bfloat16),
        "dp",
        scatter_dimension=0,
        tiled=True,
    ).astype(jnp.float32)
    hidden_state = residual.astype(jnp.float32) + projected
    moe_input = normalize(hidden_state, moe_gain).astype(jnp.bfloat16)
    rows_here = moe_input.shape[0]
    experts = lax.axis_size("expert")
    slots = max(2, min(rows_here, 2 * rows_here * TOP // experts))
    flat_ids = expert_ids.reshape(-1)
    marks = (flat_ids[:, None] == jnp.arange(experts, dtype=jnp.int32)[None, :]).astype(jnp.int32)
    before = jnp.sum((jnp.cumsum(marks, axis=0) - 1) * marks, axis=1)
    target = (flat_ids * slots + before).reshape(rows_here, TOP)
    placing = jnp.any(
        jnp.arange(experts * slots, dtype=jnp.int32)[:, None, None] == target[None], axis=-1
    )
    outbound = jnp.dot(placing.astype(jnp.bfloat16), moe_input, preferred_element_type=jnp.float32)
    outbound = outbound.astype(jnp.bfloat16).reshape(experts, slots, moe_input.shape[1])
    gate_full = lax.all_gather(w_gate, "dp", axis=1, tiled=True)
    up_full = lax.all_gather(w_up, "dp", axis=1, tiled=True)
    down_full = lax.all_gather(w_down, "dp", axis=1, tiled=True)
    arrived = lax.all_to_all(outbound, "expert", split_axis=0, concat_axis=0, tiled=True)
    flat = arrived.reshape(-1, arrived.shape[2])
    gate = jnp.dot(flat, gate_full[0], preferred_element_type=jnp.float32)
    up_part = jnp.dot(flat, up_full[0], preferred_element_type=jnp.float32)
    expert_mid = (jax.nn.silu(gate) * up_part).astype(jnp.bfloat16)
    done = jnp.dot(expert_mid, down_full[0], preferred_element_type=jnp.float32).astype(
        jnp.bfloat16
    )
    done = done.reshape(arrived.shape[0], arrived.shape[1], arrived.shape[2])
    returned = lax.all_to_all(done, "expert", split_axis=0, concat_axis=0, tiled=True)
    answers = returned.reshape(experts * slots, returned.shape[2])[target]
    moe = jnp.sum(route_weights[:, :, None] * answers.astype(jnp.float32), axis=1)
    combined = hidden_state + moe
    return normalize(combined, final_gain).astype(jnp.bfloat16)


def place(z, y, c):
    return (z * 2 + y) * 2 + c


def shift_z(values, depth, step):
    pairs = [
        (place((z + step) % depth, y, c), place(z, y, c))
        for z in range(depth)
        for y in range(2)
        for c in range(2)
    ]
    return lax.ppermute(values, "expert", pairs)


def flip_y(values, depth):
    pairs = [
        (place(z, 1 - y, c), place(z, y, c))
        for z in range(depth)
        for y in range(2)
        for c in range(2)
    ]
    return lax.ppermute(values, "expert", pairs)


def flip_core(values, depth):
    pairs = [
        (place(z, y, 1 - c), place(z, y, c))
        for z in range(depth)
        for y in range(2)
        for c in range(2)
    ]
    return lax.ppermute(values, "expert", pairs)


def flip_x(values):
    return lax.ppermute(values, "dp", [(0, 1), (1, 0)])


def flip_xy(values, depth):
    pairs = [
        ((1 - x) * 4 * depth + place(z, 1 - y, c), x * 4 * depth + place(z, y, c))
        for x in range(2)
        for z in range(depth)
        for y in range(2)
        for c in range(2)
    ]
    return lax.ppermute(values, ("dp", "expert"), pairs)


def attend_kernel(pages_ref, lens_ref, q_ref, kv_ref, out_ref):
    scale = 1.0 / math.sqrt(HD)
    seqs, slots = pages_ref.shape
    rows, feats = q_ref.shape
    each = rows // seqs
    page = kv_ref.shape[2]
    first_page = lax.axis_index("expert") * kv_ref.shape[1]
    place_in = lax.broadcasted_iota(jnp.int32, (each, slots * page), 1)
    for s in range(seqs):
        here = slice(s * each, (s + 1) * each)
        pages = [pages_ref[s, p] - first_page for p in range(slots)]
        keys = jnp.concatenate([kv_ref[0, p] for p in pages], axis=0)
        values = jnp.concatenate([kv_ref[1, p] for p in pages], axis=0)
        visible = place_in < lens_ref[here, :]
        for h in range(feats // HD):
            lanes = slice(h * HD, (h + 1) * HD)
            scores = lax.dot_general(
                q_ref[here, lanes],
                keys[:, lanes],
                (((1,), (1,)), ((), ())),
                preferred_element_type=jnp.float32,
            )
            scores = jnp.where(visible, scores * scale, -1e30)
            top_score = jnp.max(scores, axis=-1, keepdims=True)
            expo = jnp.where(visible, jnp.exp(scores - top_score), 0.0)
            probs = (expo / jnp.sum(expo, axis=-1, keepdims=True)).astype(jnp.bfloat16)
            mixed = jnp.dot(probs, values[:, lanes], preferred_element_type=jnp.float32)
            out_ref[here, lanes] = mixed.astype(out_ref.dtype)


def attend_here(queries, kv_pool, page_table, ctx_lens):
    vmem_spec = pl.BlockSpec(memory_space=pltpu.VMEM)
    return pl.pallas_call(
        attend_kernel,
        out_shape=jax.ShapeDtypeStruct(queries.shape, jnp.bfloat16),
        in_specs=[pl.BlockSpec(memory_space=pltpu.SMEM)] + [vmem_spec] * 3,
        out_specs=vmem_spec,
        compiler_params=pltpu.CompilerParams(vmem_limit_bytes=16 * MIB),
        cost_estimate=pl.CostEstimate(
            flops=4 * queries.size * CTX,
            bytes_accessed=2 * kv_pool.size + 4 * queries.size,
            transcendentals=queries.size * CTX // HD,
        ),
        name="attend",
    )(page_table, ctx_lens[:, None], queries, kv_pool)


def project_kernel(depth, ctx_ref, other_ref, *refs):
    pieces, (kept_ref, sent_ref) = refs[:-2], refs[-2:]
    half = ctx_ref.shape[0] // 2
    feats, width = pieces[0].shape
    me = lax.axis_index("expert")
    x = lax.axis_index("dp")
    y = lax.rem(lax.div(me, 2), 2)
    z = lax.div(me, 4)
    mine = pl.ds(pl.multiple_of(x * half, half), half)
    theirs = pl.ds(pl.multiple_of((1 - x) * half, half), half)
    rows = jnp.concatenate(
        [ctx_ref[mine, :], other_ref[mine, :], ctx_ref[theirs, :], other_ref[theirs, :]], axis=0
    )
    for flip in range(2):
        at_y = y if flip == 0 else 1 - y
        for r in range(depth):
            if r == 0:
                piece = pieces[2 * flip][...]
            else:
                piece = pieces[2 * flip + 1][(r - 1) * feats : r * feats, :]
            total = jnp.dot(rows, piece, preferred_element_type=jnp.float32)
            index = lax.rem(z + r, depth) * 2 + at_y
            columns = pl.ds(pl.multiple_of(index * width, width), width)
            kept_ref[:, columns] = total[: 2 * half]
            sent_ref[:, columns] = total[2 * half :].astype(sent_ref.dtype)


def project(context, other, pieces, depth):
    rows, feats = context.shape
    columns = pieces[0].shape[1] * 2 * depth
    return pl.pallas_call(
        functools.partial(project_kernel, depth),
        out_shape=(
            jax.ShapeDtypeStruct((rows, columns), jnp.float32),
            jax.ShapeDtypeStruct((rows, columns), jnp.bfloat16),
        ),
        compiler_params=pltpu.CompilerParams(vmem_limit_bytes=16 * MIB),
        cost_estimate=pl.CostEstimate(
            flops=4 * rows * feats * columns,
            bytes_accessed=2 * feats * columns + 6 * rows * columns,
            transcendentals=0,
        ),
        name="project",
    )(context, other, *pieces)


def join_kernel(width, mine_ref, other_ref, residual_ref, gain_ref, share_ref, hidden_ref, out_ref):
    c = lax.rem(lax.axis_index("expert"), 2)
    feats = residual_ref.shape[1]
    for i in range(feats // (2 * width)):
        source = slice(i * width, (i + 1) * width)
        for own, ref in ((True, mine_ref), (False, other_ref)):
            index = 2 * i + (c if own else 1 - c)
            columns = pl.ds(pl.multiple_of(index * width, width), width)
            hidden_ref[:, columns] = ref[:, source]
    hidden = residual_ref[...].astype(jnp.float32) + hidden_ref[...]
    hidden_ref[...] = hidden
    mean_sq = jnp.mean(hidden * hidden, axis=-1, keepdims=True)
    out_ref[:, :feats] = (hidden * lax.rsqrt(mean_sq + 1e-06) * gain_ref[...]).astype(
        out_ref.dtype
    )
    out_ref[:, feats:] = share_ref[...]


def join(mine, other, residual, gain, share, width):
    rows, feats = residual.shape
    return pl.pallas_call(
        functools.partial(join_kernel, width),
        out_shape=(
            jax.ShapeDtypeStruct((rows, feats), jnp.float32),
            jax.ShapeDtypeStruct((rows, feats + share.shape[1]), jnp.bfloat16),
        ),
        compiler_params=pltpu.CompilerParams(vmem_limit_bytes=16 * MIB),
        cost_estimate=pl.CostEstimate(
            flops=6 * rows * feats, bytes_accessed=12 * rows * feats, transcendentals=rows
        ),
        name="join",
    )(mine, other, residual, gain[None, :], share)


def cut_kernel(width, w_ref, *refs):
    outs, sems = refs[:-1], refs[-1]
    x = lax.axis_index("dp")
    units = w_ref.shape[2]
    low = x * (units - width)
    high = (1 - x) * (units - width)
    copies = []
    at = 0
    for i, out in enumerate(outs):
        start = pl.multiple_of(high if i > 0 else low, 128)
        source_at = 0 if i == 0 else at
        copy = pltpu.make_async_copy(
            w_ref.at[0, pl.ds(source_at, out.shape[0]), pl.ds(start, width)], out, sems.at[i]
        )
        copy.start()
        copies.append(copy)
        if i > 0:
            at += out.shape[0]
    for copy in copies:
        copy.wait()


def cut(weights, width, parts):
    depth = weights.shape[1]
    shapes = [depth] + list(parts)
    any_spec = pl.BlockSpec(memory_space=pl.ANY)
    return pl.pallas_call(
        functools.partial(cut_kernel, width),
        out_shape=tuple(jax.ShapeDtypeStruct((n, width), weights.dtype) for n in shapes),
        in_specs=[any_spec],
        out_specs=(pl.BlockSpec(memory_space=pltpu.VMEM),) * len(shapes),
        scratch_shapes=[pltpu.SemaphoreType.DMA((len(shapes),))],
        cost_estimate=pl.CostEstimate(
            flops=0, bytes_accessed=8 * depth * width, transcendentals=0
        ),
        compiler_params=pltpu.CompilerParams(vmem_limit_bytes=16 * MIB),
        name="cut",
    )(weights)


SLOTS = 3


def experts_kernel(tile, out_tile, first_row, count, split, *refs):
    per_expert = 6
    pieces, refs = refs[:count], refs[count:]
    weights, refs = refs[: 2 * per_expert], refs[2 * per_expert :]
    outs, refs = refs[:count], refs[count:]
    rows, share, gate, up, down, mid, row_sem, weight_sem, down_sem = refs
    x = lax.axis_index("dp")
    me = lax.axis_index("expert")
    feats = rows.shape[2]
    blocks, each = rows.shape[0], rows.shape[1]
    half = feats // 2
    width = down.shape[0] // 2
    tiles = width // tile
    near = pl.ds(pl.multiple_of(x * half, half), half)
    far = pl.ds(pl.multiple_of((1 - x) * half, half), half)
    taken = pl.ds(first_row, each)

    row_copies = []
    spans = []
    at = 0
    for i, piece in enumerate(pieces):
        part = piece.shape[0]
        spans.append((at * each, part * each))
        here = pl.ds(at, part)
        for s, (source, target) in enumerate(
            (
                (piece.at[:, taken, near], rows.at[here, :, pl.ds(0, half)]),
                (piece.at[:, taken, far], rows.at[here, :, pl.ds(half, half)]),
                (piece.at[:, taken, pl.ds(feats, 128)], share.at[here]),
            )
        ):
            copy = pltpu.make_async_copy(source, target, row_sem.at[3 * i + s])
            copy.start()
            row_copies.append(copy)
        at += part

    def fetch(t):
        e, j = t // tiles, t % tiles
        gate_own, gate_far, mixed, up_own, up_far, _ = weights[
            e * per_expert : (e + 1) * per_expert
        ]
        group = []
        sem = 6 * (t % SLOTS)
        gates = ((gate_own, 0), (gate_far, 0), (mixed, 0))
        ups = ((up_own, 0), (mixed, split), (up_far, 0))
        for sources, target in ((gates, gate), (ups, up)):
            depth_at = 0
            for source, start in sources:
                end = split if source is mixed and start == 0 else source.shape[0]
                copy = pltpu.make_async_copy(
                    source.at[pl.ds(start, end - start), pl.ds(j * tile, tile)],
                    target.at[t % SLOTS, pl.ds(depth_at, end - start), :],
                    weight_sem.at[sem],
                )
                copy.start()
                group.append(copy)
                depth_at += end - start
                sem += 1
        return group

    weight_copies = [fetch(t) for t in range(SLOTS)]
    units = weights[-1].shape[0]
    spare = width - units
    down_copies = []
    for e in range(2):
        start = pl.multiple_of(e * width + x * spare, 16)
        copy = pltpu.make_async_copy(
            weights[(e + 1) * per_expert - 1], down.at[pl.ds(start, units), :], down_sem.at[e]
        )
        copy.start()
        down_copies.append(copy)
        if spare:
            blank = pl.multiple_of(e * width + (1 - x) * units, 16)
            down[pl.ds(blank, spare), :] = jnp.zeros((spare, feats), down.dtype)

    for copy in row_copies:
        copy.wait()
    total_rows = blocks * each
    shares = share[...].reshape(total_rows, 128).astype(jnp.float32)
    lane = lax.broadcasted_iota(jnp.int32, (total_rows, 128), 1)
    experts = lax.axis_size("expert")
    for t in range(2 * tiles):
        e, j = t // tiles, t % tiles
        if j == 0:
            chosen = me if e == 0 else me + 1 - 2 * lax.rem(me, 2)
            hit = (lane == chosen) | (lane == chosen + experts)
            scale = jnp.sum(jnp.where(hit, shares, 0.0), axis=1, keepdims=True)
        for copy in weight_copies[t]:
            copy.wait()
        values = rows[...].reshape(total_rows, feats)
        g = jnp.dot(values, gate[t % SLOTS], preferred_element_type=jnp.float32)
        u = jnp.dot(values, up[t % SLOTS], preferred_element_type=jnp.float32)
        h = g / (1.0 + jnp.exp(-g)) * u * scale
        mid[:, pl.ds(t * tile, tile)] = h.astype(mid.dtype)
        if t + SLOTS < 2 * tiles:
            weight_copies.append(fetch(t + SLOTS))
    for copy in down_copies:
        copy.wait()
    for n in range(feats // out_tile):
        lanes = pl.ds(n * out_tile, out_tile)
        total = jnp.dot(mid[...], down[:, lanes], preferred_element_type=jnp.float32)
        for (first, part), out in zip(spans, outs):
            out[:, lanes] = total[first : first + part].astype(out.dtype)


def run_experts(pieces, kinds, first_row, each, weights, split):
    feats = weights[-1].shape[1]
    width = weights[0].shape[1]
    count = len(pieces)
    blocks = sum(piece.shape[0] for piece in pieces)
    total = blocks * each
    tile = 256
    any_spec = pl.BlockSpec(memory_space=pl.ANY)
    vmem_spec = pl.BlockSpec(memory_space=pltpu.VMEM)
    return pl.pallas_call(
        functools.partial(experts_kernel, tile, 512, first_row, count, split),
        out_shape=tuple(
            jax.ShapeDtypeStruct((piece.shape[0] * each, feats), kind)
            for piece, kind in zip(pieces, kinds)
        ),
        in_specs=[any_spec] * (count + len(weights)),
        out_specs=(vmem_spec,) * count,
        scratch_shapes=[
            pltpu.VMEM((blocks, each, feats), jnp.bfloat16),
            pltpu.VMEM((blocks, each, 128), jnp.bfloat16),
            pltpu.VMEM((SLOTS, feats, tile), jnp.bfloat16),
            pltpu.VMEM((SLOTS, feats, tile), jnp.bfloat16),
            pltpu.VMEM((2 * width, feats), jnp.bfloat16),
            pltpu.VMEM((total, 2 * width), jnp.bfloat16),
            pltpu.SemaphoreType.DMA((3 * count,)),
            pltpu.SemaphoreType.DMA((SLOTS * 6,)),
            pltpu.SemaphoreType.DMA((2,)),
        ],
        compiler_params=pltpu.CompilerParams(vmem_limit_bytes=30 * MIB),
        cost_estimate=pl.CostEstimate(
            flops=2 * total * feats * width * 6,
            bytes_accessed=12 * feats * width + 12 * total * feats,
            transcendentals=total * width * 2,
        ),
        name="experts",
    )(*pieces, *weights)


def diagonal(line_x, line_y, depth):
    half = depth // 2
    return flip_y(line_x[:half], depth), flip_x(line_y[half:])


def send_line(full, depth):
    full = full.reshape(depth, -1, full.shape[1])
    total = full[0]
    for s in range(1, depth):
        back = shift_z(full[s].astype(jnp.bfloat16), depth, depth - s)
        total = total + back.astype(jnp.float32)
    return total


def gathered(
    queries,
    kv_pool,
    page_table,
    ctx_lens,
    w_out,
    residual,
    moe_gain,
    expert_ids,
    route_weights,
    w_gate,
    w_up,
    w_down,
    final_gain,
):
    experts = lax.axis_size("expert")
    depth = experts // 4
    feats = residual.shape[1]
    block = residual.shape[0]
    units_here = w_down.shape[1]
    width = -(-units_here // 256) * 256
    barrier = lax.optimization_barrier

    shifted = [shift_z(w_out, depth, s) for s in range(1, depth)]
    across_own = flip_y(w_out, depth)

    feats_here = w_gate.shape[1]
    early = feats_here * 7 // 8
    gate_own, *gate_sent = cut(w_gate, width, (early, feats_here - early))
    gate_far = flip_x(gate_sent[0])
    split = feats_here - early
    queries, gate_sent[1], gate_own = barrier((queries, gate_sent[1], gate_own))
    context = attend_here(queries, kv_pool, page_table, ctx_lens)
    context, w_up, w_down = barrier((context, w_up, w_down))
    early = feats_here * 27 // 64
    up_own, *up_sent = cut(w_up, width, (early, feats_here - early))
    mixed_sent = jnp.concatenate([gate_sent[1], up_sent[0]], axis=0)
    shifted, across_own, gate_far, mixed_sent, up_sent[1], gate_own, up_own, w_down, context = (
        barrier(
            (
                shifted,
                across_own,
                gate_far,
                mixed_sent,
                up_sent[1],
                gate_own,
                up_own,
                w_down,
                context,
            )
        )
    )
    shifted = jnp.concatenate(shifted, axis=0)
    across = flip_y(shifted, depth)
    mixed_far = flip_x(mixed_sent)
    other = flip_core(context, depth)
    down_own = w_down[0]
    here_core = [flip_core(array, depth) for array in (gate_own, up_own, down_own)]

    named = expert_ids[:, :, None] == jnp.arange(experts, dtype=jnp.int32)[None, None, :]
    share = jnp.sum(jnp.where(named, route_weights[:, :, None], 0.0), axis=1)
    share_high = share.astype(jnp.bfloat16)
    share_low = (share - share_high.astype(jnp.float32)).astype(jnp.bfloat16)
    share = jnp.concatenate(
        [share_high, share_low, jnp.zeros((block, 128 - 2 * experts), jnp.bfloat16)], axis=1
    )

    across, share, here_core, mixed_far = barrier((across, share, here_core, mixed_far))
    kept, sent = project(context, other, [w_out, shifted, across_own, across], depth)
    gate_far_core = flip_core(gate_far, depth)
    mixed_far_core = flip_core(mixed_far, depth)
    received, up_late = barrier((flip_x(sent), up_sent[1]))
    up_far = flip_x(up_late)
    total = kept + received.astype(jnp.float32)
    back = flip_core(total[block:], depth)
    hidden_state, message = join(total[:block], back, residual, moe_gain, share, w_out.shape[1])

    rows = block // 2
    arrived = [message] + [shift_z(message, depth, s) for s in range(1, depth)]
    ready = []
    for k in range(2):
        line = jnp.stack([piece[rows * k : rows * (k + 1)] for piece in arrived])
        if k > 0:
            line, ready[0][3], ready[0][4] = barrier((line, ready[0][3], ready[0][4]))
        line_x = flip_x(line)
        line_y = flip_y(line, depth)
        if k == 0:
            line_x, line_y, up_far = barrier((line_x, line_y, up_far))
            ready.append([line, line_x, line_y, *diagonal(line_x, line_y, depth)])
        else:
            ready.append([line, line_x, line_y])

    weights = [gate_own, gate_far, mixed_far, up_own, up_far, down_own]
    weights += [
        here_core[0],
        gate_far_core,
        mixed_far_core,
        here_core[1],
        flip_core(up_far, depth),
        here_core[2],
    ]

    backs = []
    last = None
    for chunk, at, each in ((0, 0, rows), (1, 0, rows // 2), (1, rows // 2, rows // 2)):
        pieces = ready[chunk]
        if len(pieces) == 3:
            pieces[1], pieces[2], last = barrier((pieces[1], pieces[2], last))
            pieces += diagonal(pieces[1], pieces[2], depth)
        elif last is not None:
            pieces[0], last = barrier((pieces[0], last))
        out_l, out_x, out_y, out_low, out_high = run_experts(
            pieces,
            (jnp.float32, jnp.bfloat16, jnp.bfloat16, jnp.bfloat16, jnp.bfloat16),
            at,
            each,
            weights,
            split,
        )
        last = out_low
        far = jnp.concatenate([out_low, out_high], axis=0)
        backs.append((out_l, flip_x(out_x), flip_y(out_y, depth), flip_xy(far, depth)))
    moe = []
    full = None
    for back in backs:
        if full is not None:
            back, full = barrier((back, full))
            moe.append(send_line(full, depth))
        full = back[0]
        for part in back[1:]:
            full = full + part.astype(jnp.float32)
    moe.append(send_line(full, depth))
    combined = hidden_state + jnp.concatenate(moe, axis=0)
    return normalize(combined, final_gain).astype(jnp.bfloat16)


def solution(mesh):
    few = mesh.shape["dp"] == 2 and mesh.shape["expert"] == 16
    return jax.shard_map(
        gathered if few else dispatched,
        mesh=mesh,
        in_specs=(
            P("expert", "dp"),
            P(None, "expert", None, "dp"),
            P("expert", None),
            P("expert"),
            P("dp", "expert"),
            P(("expert", "dp"), None),
            P(),
            P(("expert", "dp"), None),
            P(("expert", "dp"), None),
            P("expert", "dp", None),
            P("expert", "dp", None),
            P("expert", "dp", None),
            P(),
        ),
        out_specs=P(("expert", "dp"), None),
        check_vma=False,
    )
```

```python
import functools
import math

import jax
import jax.numpy as jnp
from jax import lax
from jax.experimental import pallas as pl
from jax.experimental.pallas import tpu as pltpu
from jax.sharding import PartitionSpec as P

HD = 128
TOP = 6
CTX = 256
MIB = 1024 * 1024


def normalize(values, gain):
    mean_sq = jnp.mean(values * values, axis=-1, keepdims=True)
    return values * lax.rsqrt(mean_sq + 1e-06) * gain


def attend(queries, kv_pool, page_table, ctx_lens):
    scale = 1.0 / math.sqrt(HD)
    group_rows = queries.shape[0]
    local_feats = queries.shape[1]
    local_heads = local_feats // HD
    seq_count = page_table.shape[0]
    seq_rows = group_rows // seq_count
    pool_here = kv_pool.shape[1]
    local_pages = page_table - lax.axis_index("expert") * pool_here
    keys = kv_pool[0][local_pages].reshape(seq_count, CTX, local_heads, HD)
    values = kv_pool[1][local_pages].reshape(seq_count, CTX, local_heads, HD)
    asked = queries.reshape(seq_count, seq_rows, local_heads, HD)
    scores = jnp.einsum("sqhd,skhd->shqk", asked, keys, preferred_element_type=jnp.float32) * scale
    lengths = ctx_lens.reshape(seq_count, seq_rows)
    visible = (jnp.arange(CTX, dtype=jnp.int32)[None, None, :] < lengths[:, :, None])[:, None]
    scores = jnp.where(visible, scores, -1e30)
    top_score = jnp.max(scores, axis=-1, keepdims=True)
    expo = jnp.where(visible, jnp.exp(scores - top_score), 0.0)
    probs = (expo / jnp.sum(expo, axis=-1, keepdims=True)).astype(jnp.bfloat16)
    mixed = jnp.einsum("shqk,skhd->sqhd", probs, values, preferred_element_type=jnp.float32)
    return mixed.astype(jnp.bfloat16).reshape(group_rows, local_feats)


def dispatched(
    queries,
    kv_pool,
    page_table,
    ctx_lens,
    w_out,
    residual,
    moe_gain,
    expert_ids,
    route_weights,
    w_gate,
    w_up,
    w_down,
    final_gain,
):
    context = attend(queries, kv_pool, page_table, ctx_lens)
    columns = lax.all_gather(w_out, "expert", axis=1, tiled=True)
    projected = lax.psum_scatter(
        jnp.dot(context, columns, preferred_element_type=jnp.float32).astype(jnp.bfloat16),
        "dp",
        scatter_dimension=0,
        tiled=True,
    ).astype(jnp.float32)
    hidden_state = residual.astype(jnp.float32) + projected
    moe_input = normalize(hidden_state, moe_gain).astype(jnp.bfloat16)
    rows_here = moe_input.shape[0]
    experts = lax.axis_size("expert")
    slots = max(2, min(rows_here, 2 * rows_here * TOP // experts))
    flat_ids = expert_ids.reshape(-1)
    marks = (flat_ids[:, None] == jnp.arange(experts, dtype=jnp.int32)[None, :]).astype(jnp.int32)
    before = jnp.sum((jnp.cumsum(marks, axis=0) - 1) * marks, axis=1)
    target = (flat_ids * slots + before).reshape(rows_here, TOP)
    placing = jnp.any(
        jnp.arange(experts * slots, dtype=jnp.int32)[:, None, None] == target[None], axis=-1
    )
    outbound = jnp.dot(placing.astype(jnp.bfloat16), moe_input, preferred_element_type=jnp.float32)
    outbound = outbound.astype(jnp.bfloat16).reshape(experts, slots, moe_input.shape[1])
    gate_full = lax.all_gather(w_gate, "dp", axis=1, tiled=True)
    up_full = lax.all_gather(w_up, "dp", axis=1, tiled=True)
    down_full = lax.all_gather(w_down, "dp", axis=1, tiled=True)
    arrived = lax.all_to_all(outbound, "expert", split_axis=0, concat_axis=0, tiled=True)
    flat = arrived.reshape(-1, arrived.shape[2])
    gate = jnp.dot(flat, gate_full[0], preferred_element_type=jnp.float32)
    up_part = jnp.dot(flat, up_full[0], preferred_element_type=jnp.float32)
    expert_mid = (jax.nn.silu(gate) * up_part).astype(jnp.bfloat16)
    done = jnp.dot(expert_mid, down_full[0], preferred_element_type=jnp.float32).astype(
        jnp.bfloat16
    )
    done = done.reshape(arrived.shape[0], arrived.shape[1], arrived.shape[2])
    returned = lax.all_to_all(done, "expert", split_axis=0, concat_axis=0, tiled=True)
    answers = returned.reshape(experts * slots, returned.shape[2])[target]
    moe = jnp.sum(route_weights[:, :, None] * answers.astype(jnp.float32), axis=1)
    combined = hidden_state + moe
    return normalize(combined, final_gain).astype(jnp.bfloat16)


def place(z, y, c):
    return (z * 2 + y) * 2 + c


def shift_z(values, depth, step):
    pairs = [
        (place((z + step) % depth, y, c), place(z, y, c))
        for z in range(depth)
        for y in range(2)
        for c in range(2)
    ]
    return lax.ppermute(values, "expert", pairs)


def flip_y(values, depth):
    pairs = [
        (place(z, 1 - y, c), place(z, y, c))
        for z in range(depth)
        for y in range(2)
        for c in range(2)
    ]
    return lax.ppermute(values, "expert", pairs)


def flip_core(values, depth):
    pairs = [
        (place(z, y, 1 - c), place(z, y, c))
        for z in range(depth)
        for y in range(2)
        for c in range(2)
    ]
    return lax.ppermute(values, "expert", pairs)


def flip_x(values):
    return lax.ppermute(values, "dp", [(0, 1), (1, 0)])


def flip_xy(values, depth):
    pairs = [
        ((1 - x) * 4 * depth + place(z, 1 - y, c), x * 4 * depth + place(z, y, c))
        for x in range(2)
        for z in range(depth)
        for y in range(2)
        for c in range(2)
    ]
    return lax.ppermute(values, ("dp", "expert"), pairs)


def attend_kernel(pages_ref, lens_ref, q_ref, kv_ref, out_ref):
    scale = 1.0 / math.sqrt(HD)
    seqs, slots = pages_ref.shape
    rows, feats = q_ref.shape
    each = rows // seqs
    page = kv_ref.shape[2]
    first_page = lax.axis_index("expert") * kv_ref.shape[1]
    place_in = lax.broadcasted_iota(jnp.int32, (each, slots * page), 1)
    for s in range(seqs):
        here = slice(s * each, (s + 1) * each)
        pages = [pages_ref[s, p] - first_page for p in range(slots)]
        keys = jnp.concatenate([kv_ref[0, p] for p in pages], axis=0)
        values = jnp.concatenate([kv_ref[1, p] for p in pages], axis=0)
        visible = place_in < lens_ref[here, :]
        for h in range(feats // HD):
            lanes = slice(h * HD, (h + 1) * HD)
            scores = lax.dot_general(
                q_ref[here, lanes],
                keys[:, lanes],
                (((1,), (1,)), ((), ())),
                preferred_element_type=jnp.float32,
            )
            scores = jnp.where(visible, scores * scale, -1e30)
            top_score = jnp.max(scores, axis=-1, keepdims=True)
            expo = jnp.where(visible, jnp.exp(scores - top_score), 0.0)
            probs = (expo / jnp.sum(expo, axis=-1, keepdims=True)).astype(jnp.bfloat16)
            mixed = jnp.dot(probs, values[:, lanes], preferred_element_type=jnp.float32)
            out_ref[here, lanes] = mixed.astype(out_ref.dtype)


def attend_here(queries, kv_pool, page_table, ctx_lens):
    vmem_spec = pl.BlockSpec(memory_space=pltpu.VMEM)
    return pl.pallas_call(
        attend_kernel,
        out_shape=jax.ShapeDtypeStruct(queries.shape, jnp.bfloat16),
        in_specs=[pl.BlockSpec(memory_space=pltpu.SMEM)] + [vmem_spec] * 3,
        out_specs=vmem_spec,
        compiler_params=pltpu.CompilerParams(vmem_limit_bytes=16 * MIB),
        cost_estimate=pl.CostEstimate(
            flops=4 * queries.size * CTX,
            bytes_accessed=2 * kv_pool.size + 4 * queries.size,
            transcendentals=queries.size * CTX // HD,
        ),
        name="attend",
    )(page_table, ctx_lens[:, None], queries, kv_pool)


def project_kernel(depth, ctx_ref, other_ref, *refs):
    pieces, (kept_ref, sent_ref) = refs[:-2], refs[-2:]
    half = ctx_ref.shape[0] // 2
    width = pieces[0].shape[1]
    me = lax.axis_index("expert")
    x = lax.axis_index("dp")
    y = lax.rem(lax.div(me, 2), 2)
    z = lax.div(me, 4)
    mine = pl.ds(pl.multiple_of(x * half, half), half)
    theirs = pl.ds(pl.multiple_of((1 - x) * half, half), half)
    rows = jnp.concatenate(
        [ctx_ref[mine, :], other_ref[mine, :], ctx_ref[theirs, :], other_ref[theirs, :]], axis=0
    )
    for flip in range(2):
        at_y = y if flip == 0 else 1 - y
        for r in range(depth):
            piece = pieces[flip * depth + r][...]
            total = jnp.dot(rows, piece, preferred_element_type=jnp.float32)
            index = lax.rem(z + r, depth) * 2 + at_y
            columns = pl.ds(pl.multiple_of(index * width, width), width)
            kept_ref[:, columns] = total[: 2 * half]
            sent_ref[:, columns] = total[2 * half :].astype(sent_ref.dtype)


def project(context, other, pieces, depth):
    rows, feats = context.shape
    columns = pieces[0].shape[1] * 2 * depth
    return pl.pallas_call(
        functools.partial(project_kernel, depth),
        out_shape=(
            jax.ShapeDtypeStruct((rows, columns), jnp.float32),
            jax.ShapeDtypeStruct((rows, columns), jnp.bfloat16),
        ),
        compiler_params=pltpu.CompilerParams(vmem_limit_bytes=16 * MIB),
        cost_estimate=pl.CostEstimate(
            flops=4 * rows * feats * columns,
            bytes_accessed=2 * feats * columns + 6 * rows * columns,
            transcendentals=0,
        ),
        name="project",
    )(context, other, *pieces)


def join_kernel(width, mine_ref, other_ref, residual_ref, gain_ref, share_ref, hidden_ref, out_ref):
    c = lax.rem(lax.axis_index("expert"), 2)
    feats = residual_ref.shape[1]
    for i in range(feats // (2 * width)):
        source = slice(i * width, (i + 1) * width)
        for own, ref in ((True, mine_ref), (False, other_ref)):
            index = 2 * i + (c if own else 1 - c)
            columns = pl.ds(pl.multiple_of(index * width, width), width)
            hidden_ref[:, columns] = ref[:, source]
    hidden = residual_ref[...].astype(jnp.float32) + hidden_ref[...]
    hidden_ref[...] = hidden
    mean_sq = jnp.mean(hidden * hidden, axis=-1, keepdims=True)
    out_ref[:, :feats] = (hidden * lax.rsqrt(mean_sq + 1e-06) * gain_ref[...]).astype(
        out_ref.dtype
    )
    out_ref[:, feats:] = share_ref[...]


def join(mine, other, residual, gain, share, width):
    rows, feats = residual.shape
    return pl.pallas_call(
        functools.partial(join_kernel, width),
        out_shape=(
            jax.ShapeDtypeStruct((rows, feats), jnp.float32),
            jax.ShapeDtypeStruct((rows, feats + share.shape[1]), jnp.bfloat16),
        ),
        compiler_params=pltpu.CompilerParams(vmem_limit_bytes=16 * MIB),
        cost_estimate=pl.CostEstimate(
            flops=6 * rows * feats, bytes_accessed=12 * rows * feats, transcendentals=rows
        ),
        name="join",
    )(mine, other, residual, gain[None, :], share)


def cut_kernel(width, w_ref, *refs):
    outs, sems = refs[:-1], refs[-1]
    x = lax.axis_index("dp")
    units = w_ref.shape[2]
    low = x * (units - width)
    high = (1 - x) * (units - width)
    copies = []
    at = 0
    for i, out in enumerate(outs):
        start = pl.multiple_of(high if i > 0 else low, 128)
        source_at = 0 if i == 0 else at
        copy = pltpu.make_async_copy(
            w_ref.at[0, pl.ds(source_at, out.shape[0]), pl.ds(start, width)], out, sems.at[i]
        )
        copy.start()
        copies.append(copy)
        if i > 0:
            at += out.shape[0]
    for copy in copies:
        copy.wait()


def cut(weights, width, parts):
    depth = weights.shape[1]
    shapes = [depth] + list(parts)
    any_spec = pl.BlockSpec(memory_space=pl.ANY)
    return pl.pallas_call(
        functools.partial(cut_kernel, width),
        out_shape=tuple(jax.ShapeDtypeStruct((n, width), weights.dtype) for n in shapes),
        in_specs=[pl.BlockSpec(memory_space=pltpu.HBM)],
        out_specs=(pl.BlockSpec(memory_space=pltpu.VMEM),) * len(shapes),
        scratch_shapes=[pltpu.SemaphoreType.DMA((len(shapes),))],
        cost_estimate=pl.CostEstimate(
            flops=0, bytes_accessed=8 * depth * width, transcendentals=0
        ),
        compiler_params=pltpu.CompilerParams(vmem_limit_bytes=16 * MIB),
        name="cut",
    )(weights)


SLOTS = 3


def experts_kernel(tile, out_tile, first_row, count, split, *refs):
    per_expert = 6
    pieces, refs = refs[:count], refs[count:]
    weights, refs = refs[: 2 * per_expert], refs[2 * per_expert :]
    outs, refs = refs[:count], refs[count:]
    rows, share, gate, up, down, mid, row_sem, weight_sem, down_sem = refs
    x = lax.axis_index("dp")
    me = lax.axis_index("expert")
    feats = rows.shape[2]
    blocks, each = rows.shape[0], rows.shape[1]
    half = feats // 2
    width = down.shape[0] // 2
    tiles = width // tile
    near = pl.ds(pl.multiple_of(x * half, half), half)
    far = pl.ds(pl.multiple_of((1 - x) * half, half), half)
    taken = pl.ds(first_row, each)

    row_copies = []
    spans = []
    at = 0
    for i, piece in enumerate(pieces):
        part = piece.shape[0]
        spans.append((at * each, part * each))
        here = pl.ds(at, part)
        for s, (source, target) in enumerate(
            (
                (piece.at[:, taken, near], rows.at[here, :, pl.ds(0, half)]),
                (piece.at[:, taken, far], rows.at[here, :, pl.ds(half, half)]),
                (piece.at[:, taken, pl.ds(feats, 128)], share.at[here]),
            )
        ):
            copy = pltpu.make_async_copy(source, target, row_sem.at[3 * i + s])
            copy.start()
            row_copies.append(copy)
        at += part

    def fetch(t):
        e, j = t // tiles, t % tiles
        gate_own, gate_far, mixed, up_own, up_far, _ = weights[
            e * per_expert : (e + 1) * per_expert
        ]
        group = []
        sem = 6 * (t % SLOTS)
        gates = ((gate_own, 0), (gate_far, 0), (mixed, 0))
        ups = ((up_own, 0), (mixed, split), (up_far, 0))
        for sources, target in ((gates, gate), (ups, up)):
            depth_at = 0
            for source, start in sources:
                end = split if source is mixed and start == 0 else source.shape[0]
                copy = pltpu.make_async_copy(
                    source.at[pl.ds(start, end - start), pl.ds(j * tile, tile)],
                    target.at[t % SLOTS, pl.ds(depth_at, end - start), :],
                    weight_sem.at[sem],
                )
                copy.start()
                group.append(copy)
                depth_at += end - start
                sem += 1
        return group

    weight_copies = [fetch(t) for t in range(SLOTS)]
    units = weights[-1].shape[0]
    spare = width - units
    down_copies = []
    for e in range(2):
        start = pl.multiple_of(e * width + x * spare, 16)
        copy = pltpu.make_async_copy(
            weights[(e + 1) * per_expert - 1], down.at[pl.ds(start, units), :], down_sem.at[e]
        )
        copy.start()
        down_copies.append(copy)
        if spare:
            blank = pl.multiple_of(e * width + (1 - x) * units, 16)
            down[pl.ds(blank, spare), :] = jnp.zeros((spare, feats), down.dtype)

    for copy in row_copies:
        copy.wait()
    total_rows = blocks * each
    shares = share[...].reshape(total_rows, 128).astype(jnp.float32)
    lane = lax.broadcasted_iota(jnp.int32, (total_rows, 128), 1)
    experts = lax.axis_size("expert")
    for t in range(2 * tiles):
        e, j = t // tiles, t % tiles
        if j == 0:
            chosen = me if e == 0 else me + 1 - 2 * lax.rem(me, 2)
            hit = (lane == chosen) | (lane == chosen + experts)
            scale = jnp.sum(jnp.where(hit, shares, 0.0), axis=1, keepdims=True)
        for copy in weight_copies[t]:
            copy.wait()
        values = rows[...].reshape(total_rows, feats)
        g = jnp.dot(values, gate[t % SLOTS], preferred_element_type=jnp.float32)
        u = jnp.dot(values, up[t % SLOTS], preferred_element_type=jnp.float32)
        h = g / (1.0 + jnp.exp(-g)) * u * scale
        mid[:, pl.ds(t * tile, tile)] = h.astype(mid.dtype)
        if t + SLOTS < 2 * tiles:
            weight_copies.append(fetch(t + SLOTS))
    for copy in down_copies:
        copy.wait()
    for n in range(feats // out_tile):
        lanes = pl.ds(n * out_tile, out_tile)
        total = jnp.dot(mid[...], down[:, lanes], preferred_element_type=jnp.float32)
        for (first, part), out in zip(spans, outs):
            out[:, lanes] = total[first : first + part].astype(out.dtype)


def run_experts(pieces, kinds, first_row, each, weights, split):
    feats = weights[-1].shape[1]
    width = weights[0].shape[1]
    count = len(pieces)
    blocks = sum(piece.shape[0] for piece in pieces)
    total = blocks * each
    tile = 256
    any_spec = pl.BlockSpec(memory_space=pl.ANY)
    vmem_spec = pl.BlockSpec(memory_space=pltpu.VMEM)
    return pl.pallas_call(
        functools.partial(experts_kernel, tile, 512, first_row, count, split),
        out_shape=tuple(
            jax.ShapeDtypeStruct((piece.shape[0] * each, feats), kind)
            for piece, kind in zip(pieces, kinds)
        ),
        in_specs=[any_spec] * (count + len(weights)),
        out_specs=(vmem_spec,) * count,
        scratch_shapes=[
            pltpu.VMEM((blocks, each, feats), jnp.bfloat16),
            pltpu.VMEM((blocks, each, 128), jnp.bfloat16),
            pltpu.VMEM((SLOTS, feats, tile), jnp.bfloat16),
            pltpu.VMEM((SLOTS, feats, tile), jnp.bfloat16),
            pltpu.VMEM((2 * width, feats), jnp.bfloat16),
            pltpu.VMEM((total, 2 * width), jnp.bfloat16),
            pltpu.SemaphoreType.DMA((3 * count,)),
            pltpu.SemaphoreType.DMA((SLOTS * 6,)),
            pltpu.SemaphoreType.DMA((2,)),
        ],
        compiler_params=pltpu.CompilerParams(vmem_limit_bytes=30 * MIB),
        cost_estimate=pl.CostEstimate(
            flops=2 * total * feats * width * 6,
            bytes_accessed=12 * feats * width + 12 * total * feats,
            transcendentals=total * width * 2,
        ),
        name="experts",
    )(*pieces, *weights)


def diagonal(line_x, line_y, depth):
    half = depth // 2
    return flip_y(line_x[:half], depth), flip_x(line_y[half:])


def send_line(full, depth):
    full = full.reshape(depth, -1, full.shape[1])
    total = full[0]
    for s in range(1, depth):
        back = shift_z(full[s].astype(jnp.bfloat16), depth, depth - s)
        total = total + back.astype(jnp.float32)
    return total


def gathered(
    queries,
    kv_pool,
    page_table,
    ctx_lens,
    w_out,
    residual,
    moe_gain,
    expert_ids,
    route_weights,
    w_gate,
    w_up,
    w_down,
    final_gain,
):
    experts = lax.axis_size("expert")
    depth = experts // 4
    feats = residual.shape[1]
    block = residual.shape[0]
    units_here = w_down.shape[1]
    width = -(-units_here // 256) * 256
    barrier = lax.optimization_barrier

    shifted = [shift_z(w_out, depth, s) for s in range(1, depth)]
    across = [flip_y(w_out, depth), flip_y(shifted[0], depth)]

    feats_here = w_gate.shape[1]
    early = feats_here * 3 // 4
    gate_own, *gate_sent = cut(w_gate, width, (early, feats_here - early))
    gate_far = flip_x(gate_sent[0])
    split = feats_here - early
    queries, gate_sent[1], gate_own = barrier((queries, gate_sent[1], gate_own))
    context = attend_here(queries, kv_pool, page_table, ctx_lens)
    context, w_up, w_down = barrier((context, w_up, w_down))
    early = feats_here * 3 // 32
    up_own, *up_sent = cut(w_up, width, (early, feats_here - early))
    mixed_sent = jnp.concatenate([gate_sent[1], up_sent[0]], axis=0)
    shifted, across, gate_far, mixed_sent, up_sent[1], gate_own, up_own, w_down, context = (
        barrier(
            (
                shifted,
                across,
                gate_far,
                mixed_sent,
                up_sent[1],
                gate_own,
                up_own,
                w_down,
                context,
            )
        )
    )
    across += [flip_y(piece, depth) for piece in shifted[1:]]
    mixed_far = flip_x(mixed_sent)
    other = flip_core(context, depth)
    down_own = w_down[0]
    here_core = [flip_core(array, depth) for array in (gate_own, up_own, down_own)]

    named = expert_ids[:, :, None] == jnp.arange(experts, dtype=jnp.int32)[None, None, :]
    share = jnp.sum(jnp.where(named, route_weights[:, :, None], 0.0), axis=1)
    share_high = share.astype(jnp.bfloat16)
    share_low = (share - share_high.astype(jnp.float32)).astype(jnp.bfloat16)
    share = jnp.concatenate(
        [share_high, share_low, jnp.zeros((block, 128 - 2 * experts), jnp.bfloat16)], axis=1
    )

    across, share, here_core, mixed_far = barrier((across, share, here_core, mixed_far))
    kept, sent = project(context, other, [w_out] + shifted + across, depth)
    gate_far_core = flip_core(gate_far, depth)
    mixed_far_core = flip_core(mixed_far, depth)
    received, up_late = barrier((flip_x(sent), up_sent[1]))
    up_far = flip_x(up_late)
    total = kept + received.astype(jnp.float32)
    back = flip_core(total[block:], depth)
    hidden_state, message = join(total[:block], back, residual, moe_gain, share, w_out.shape[1])

    rows = block // 2
    lines = []
    for k in range(2):
        mine = message[rows * k : rows * (k + 1)]
        lines.append([mine] + [shift_z(mine, depth, s) for s in range(1, depth)])
    ready = []
    for k in range(2):
        line = jnp.stack(lines[k])
        if k > 0:
            line, ready[0][3], ready[0][4] = barrier((line, ready[0][3], ready[0][4]))
        line_x = flip_x(line)
        line_y = flip_y(line, depth)
        if k == 0:
            line_x, line_y, lines[1], up_far = barrier((line_x, line_y, lines[1], up_far))
            ready.append([line, line_x, line_y, *diagonal(line_x, line_y, depth)])
        else:
            ready.append([line, line_x, line_y])

    weights = [gate_own, gate_far, mixed_far, up_own, up_far, down_own]
    weights += [
        here_core[0],
        gate_far_core,
        mixed_far_core,
        here_core[1],
        flip_core(up_far, depth),
        here_core[2],
    ]

    kinds = (jnp.float32, jnp.bfloat16, jnp.bfloat16, jnp.bfloat16, jnp.bfloat16)
    outs = run_experts(ready[0], kinds, 0, rows, weights, split)
    ready[1][1], ready[1][2], outs = barrier((ready[1][1], ready[1][2], outs))
    ready[1] += diagonal(ready[1][1], ready[1][2], depth)
    ready[1], outs = barrier((ready[1], outs))
    out_l, out_x, out_y, out_low, out_high = outs
    far = jnp.concatenate([out_low, out_high], axis=0)
    backs = [flip_x(out_x), flip_y(out_y, depth), flip_xy(far, depth)]

    kinds = (jnp.float32, jnp.float32, jnp.float32, jnp.bfloat16, jnp.bfloat16)
    last_l, last_x, last_y, last_low, last_high = run_experts(
        ready[1], kinds, 0, rows, weights, split
    )
    back_low, back_high = flip_y(last_low, depth), flip_x(last_high)
    full = out_l
    for back in backs:
        full = full + back.astype(jnp.float32)
    full, back_low, back_high = barrier((full, back_low, back_high))
    first_rows = send_line(full, depth)
    half = last_x.shape[0] // 2
    sum_x = jnp.concatenate([last_x[:half] + back_low.astype(jnp.float32), last_x[half:]], axis=0)
    sum_y = jnp.concatenate([last_y[:half], last_y[half:] + back_high.astype(jnp.float32)], axis=0)
    back_x = flip_x(sum_x.astype(jnp.bfloat16))
    back_y = flip_y(sum_y.astype(jnp.bfloat16), depth)
    first_rows, back_x, back_y = barrier((first_rows, back_x, back_y))
    full = last_l + back_x.astype(jnp.float32) + back_y.astype(jnp.float32)
    moe = [first_rows, send_line(full, depth)]
    combined = hidden_state + jnp.concatenate(moe, axis=0)
    return normalize(combined, final_gain).astype(jnp.bfloat16)


def solution(mesh):
    few = mesh.shape["dp"] == 2 and mesh.shape["expert"] == 16
    return jax.shard_map(
        gathered if few else dispatched,
        mesh=mesh,
        in_specs=(
            P("expert", "dp"),
            P(None, "expert", None, "dp"),
            P("expert", None),
            P("expert"),
            P("dp", "expert"),
            P(("expert", "dp"), None),
            P(),
            P(("expert", "dp"), None),
            P(("expert", "dp"), None),
            P("expert", "dp", None),
            P("expert", "dp", None),
            P("expert", "dp", None),
            P(),
        ),
        out_specs=P(("expert", "dp"), None),
        check_vma=False,
    )
```

```python
import functools
import math

import jax
import jax.numpy as jnp
from jax import lax
from jax.experimental import pallas as pl
from jax.experimental.pallas import tpu as pltpu
from jax.sharding import PartitionSpec as P

HD = 128
TOP = 6
CTX = 256
MIB = 1024 * 1024


def normalize(values, gain):
    mean_sq = jnp.mean(values * values, axis=-1, keepdims=True)
    return values * lax.rsqrt(mean_sq + 1e-06) * gain


def attend(queries, kv_pool, page_table, ctx_lens):
    scale = 1.0 / math.sqrt(HD)
    group_rows = queries.shape[0]
    local_feats = queries.shape[1]
    local_heads = local_feats // HD
    seq_count = page_table.shape[0]
    seq_rows = group_rows // seq_count
    pool_here = kv_pool.shape[1]
    local_pages = page_table - lax.axis_index("expert") * pool_here
    keys = kv_pool[0][local_pages].reshape(seq_count, CTX, local_heads, HD)
    values = kv_pool[1][local_pages].reshape(seq_count, CTX, local_heads, HD)
    asked = queries.reshape(seq_count, seq_rows, local_heads, HD)
    scores = jnp.einsum("sqhd,skhd->shqk", asked, keys, preferred_element_type=jnp.float32) * scale
    lengths = ctx_lens.reshape(seq_count, seq_rows)
    visible = (jnp.arange(CTX, dtype=jnp.int32)[None, None, :] < lengths[:, :, None])[:, None]
    scores = jnp.where(visible, scores, -1e30)
    top_score = jnp.max(scores, axis=-1, keepdims=True)
    expo = jnp.where(visible, jnp.exp(scores - top_score), 0.0)
    probs = (expo / jnp.sum(expo, axis=-1, keepdims=True)).astype(jnp.bfloat16)
    mixed = jnp.einsum("shqk,skhd->sqhd", probs, values, preferred_element_type=jnp.float32)
    return mixed.astype(jnp.bfloat16).reshape(group_rows, local_feats)


def dispatched(
    queries,
    kv_pool,
    page_table,
    ctx_lens,
    w_out,
    residual,
    moe_gain,
    expert_ids,
    route_weights,
    w_gate,
    w_up,
    w_down,
    final_gain,
):
    context = attend(queries, kv_pool, page_table, ctx_lens)
    columns = lax.all_gather(w_out, "expert", axis=1, tiled=True)
    projected = lax.psum_scatter(
        jnp.dot(context, columns, preferred_element_type=jnp.float32).astype(jnp.bfloat16),
        "dp",
        scatter_dimension=0,
        tiled=True,
    ).astype(jnp.float32)
    hidden_state = residual.astype(jnp.float32) + projected
    moe_input = normalize(hidden_state, moe_gain).astype(jnp.bfloat16)
    rows_here = moe_input.shape[0]
    experts = lax.axis_size("expert")
    slots = max(2, min(rows_here, 2 * rows_here * TOP // experts))
    flat_ids = expert_ids.reshape(-1)
    marks = (flat_ids[:, None] == jnp.arange(experts, dtype=jnp.int32)[None, :]).astype(jnp.int32)
    before = jnp.sum((jnp.cumsum(marks, axis=0) - 1) * marks, axis=1)
    target = (flat_ids * slots + before).reshape(rows_here, TOP)
    placing = jnp.any(
        jnp.arange(experts * slots, dtype=jnp.int32)[:, None, None] == target[None], axis=-1
    )
    outbound = jnp.dot(placing.astype(jnp.bfloat16), moe_input, preferred_element_type=jnp.float32)
    outbound = outbound.astype(jnp.bfloat16).reshape(experts, slots, moe_input.shape[1])
    gate_full = lax.all_gather(w_gate, "dp", axis=1, tiled=True)
    up_full = lax.all_gather(w_up, "dp", axis=1, tiled=True)
    down_full = lax.all_gather(w_down, "dp", axis=1, tiled=True)
    arrived = lax.all_to_all(outbound, "expert", split_axis=0, concat_axis=0, tiled=True)
    flat = arrived.reshape(-1, arrived.shape[2])
    gate = jnp.dot(flat, gate_full[0], preferred_element_type=jnp.float32)
    up_part = jnp.dot(flat, up_full[0], preferred_element_type=jnp.float32)
    expert_mid = (jax.nn.silu(gate) * up_part).astype(jnp.bfloat16)
    done = jnp.dot(expert_mid, down_full[0], preferred_element_type=jnp.float32).astype(
        jnp.bfloat16
    )
    done = done.reshape(arrived.shape[0], arrived.shape[1], arrived.shape[2])
    returned = lax.all_to_all(done, "expert", split_axis=0, concat_axis=0, tiled=True)
    answers = returned.reshape(experts * slots, returned.shape[2])[target]
    moe = jnp.sum(route_weights[:, :, None] * answers.astype(jnp.float32), axis=1)
    combined = hidden_state + moe
    return normalize(combined, final_gain).astype(jnp.bfloat16)


def place(z, y, c):
    return (z * 2 + y) * 2 + c


def shift_z(values, depth, step):
    pairs = [
        (place((z + step) % depth, y, c), place(z, y, c))
        for z in range(depth)
        for y in range(2)
        for c in range(2)
    ]
    return lax.ppermute(values, "expert", pairs)


def flip_y(values, depth):
    pairs = [
        (place(z, 1 - y, c), place(z, y, c))
        for z in range(depth)
        for y in range(2)
        for c in range(2)
    ]
    return lax.ppermute(values, "expert", pairs)


def flip_core(values, depth):
    pairs = [
        (place(z, y, 1 - c), place(z, y, c))
        for z in range(depth)
        for y in range(2)
        for c in range(2)
    ]
    return lax.ppermute(values, "expert", pairs)


def flip_x(values):
    return lax.ppermute(values, "dp", [(0, 1), (1, 0)])


def flip_xy(values, depth):
    pairs = [
        ((1 - x) * 4 * depth + place(z, 1 - y, c), x * 4 * depth + place(z, y, c))
        for x in range(2)
        for z in range(depth)
        for y in range(2)
        for c in range(2)
    ]
    return lax.ppermute(values, ("dp", "expert"), pairs)


def attend_kernel(pages_ref, lens_ref, q_ref, kv_ref, out_ref):
    scale = 1.0 / math.sqrt(HD)
    seqs, slots = pages_ref.shape
    rows, feats = q_ref.shape
    each = rows // seqs
    page = kv_ref.shape[2]
    first_page = lax.axis_index("expert") * kv_ref.shape[1]
    place_in = lax.broadcasted_iota(jnp.int32, (each, slots * page), 1)
    for s in range(seqs):
        here = slice(s * each, (s + 1) * each)
        pages = [pages_ref[s, p] - first_page for p in range(slots)]
        keys = jnp.concatenate([kv_ref[0, p] for p in pages], axis=0)
        values = jnp.concatenate([kv_ref[1, p] for p in pages], axis=0)
        visible = place_in < lens_ref[here, :]
        for h in range(feats // HD):
            lanes = slice(h * HD, (h + 1) * HD)
            scores = lax.dot_general(
                q_ref[here, lanes],
                keys[:, lanes],
                (((1,), (1,)), ((), ())),
                preferred_element_type=jnp.float32,
            )
            scores = jnp.where(visible, scores * scale, -1e30)
            top_score = jnp.max(scores, axis=-1, keepdims=True)
            expo = jnp.where(visible, jnp.exp(scores - top_score), 0.0)
            probs = (expo / jnp.sum(expo, axis=-1, keepdims=True)).astype(jnp.bfloat16)
            mixed = jnp.dot(probs, values[:, lanes], preferred_element_type=jnp.float32)
            out_ref[here, lanes] = mixed.astype(out_ref.dtype)


def attend_here(queries, kv_pool, page_table, ctx_lens):
    vmem_spec = pl.BlockSpec(memory_space=pltpu.VMEM)
    return pl.pallas_call(
        attend_kernel,
        out_shape=jax.ShapeDtypeStruct(queries.shape, jnp.bfloat16),
        in_specs=[pl.BlockSpec(memory_space=pltpu.SMEM)] + [vmem_spec] * 3,
        out_specs=vmem_spec,
        compiler_params=pltpu.CompilerParams(vmem_limit_bytes=16 * MIB),
        cost_estimate=pl.CostEstimate(
            flops=4 * queries.size * CTX,
            bytes_accessed=2 * kv_pool.size + 4 * queries.size,
            transcendentals=queries.size * CTX // HD,
        ),
        name="attend",
    )(page_table, ctx_lens[:, None], queries, kv_pool)


def project_kernel(depth, ctx_ref, other_ref, *refs):
    pieces, (kept_ref, sent_ref) = refs[:-2], refs[-2:]
    half = ctx_ref.shape[0] // 2
    width = pieces[0].shape[1]
    me = lax.axis_index("expert")
    x = lax.axis_index("dp")
    y = lax.rem(lax.div(me, 2), 2)
    z = lax.div(me, 4)
    mine = pl.ds(pl.multiple_of(x * half, half), half)
    theirs = pl.ds(pl.multiple_of((1 - x) * half, half), half)
    rows = jnp.concatenate(
        [ctx_ref[mine, :], other_ref[mine, :], ctx_ref[theirs, :], other_ref[theirs, :]], axis=0
    )
    for flip in range(2):
        at_y = y if flip == 0 else 1 - y
        for r in range(depth):
            piece = pieces[flip * depth + r][...]
            total = jnp.dot(rows, piece, preferred_element_type=jnp.float32)
            index = lax.rem(z + r, depth) * 2 + at_y
            columns = pl.ds(pl.multiple_of(index * width, width), width)
            kept_ref[:, columns] = total[: 2 * half]
            sent_ref[:, columns] = total[2 * half :].astype(sent_ref.dtype)


def project(context, other, pieces, depth):
    rows, feats = context.shape
    columns = pieces[0].shape[1] * 2 * depth
    return pl.pallas_call(
        functools.partial(project_kernel, depth),
        out_shape=(
            jax.ShapeDtypeStruct((rows, columns), jnp.float32),
            jax.ShapeDtypeStruct((rows, columns), jnp.bfloat16),
        ),
        compiler_params=pltpu.CompilerParams(vmem_limit_bytes=16 * MIB),
        cost_estimate=pl.CostEstimate(
            flops=4 * rows * feats * columns,
            bytes_accessed=2 * feats * columns + 6 * rows * columns,
            transcendentals=0,
        ),
        name="project",
    )(context, other, *pieces)


def join_kernel(width, mine_ref, other_ref, residual_ref, gain_ref, share_ref, hidden_ref, out_ref):
    c = lax.rem(lax.axis_index("expert"), 2)
    feats = residual_ref.shape[1]
    for i in range(feats // (2 * width)):
        source = slice(i * width, (i + 1) * width)
        for own, ref in ((True, mine_ref), (False, other_ref)):
            index = 2 * i + (c if own else 1 - c)
            columns = pl.ds(pl.multiple_of(index * width, width), width)
            hidden_ref[:, columns] = ref[:, source]
    hidden = residual_ref[...].astype(jnp.float32) + hidden_ref[...]
    hidden_ref[...] = hidden
    mean_sq = jnp.mean(hidden * hidden, axis=-1, keepdims=True)
    out_ref[:, :feats] = (hidden * lax.rsqrt(mean_sq + 1e-06) * gain_ref[...]).astype(
        out_ref.dtype
    )
    out_ref[:, feats:] = share_ref[...]


def join(mine, other, residual, gain, share, width):
    rows, feats = residual.shape
    return pl.pallas_call(
        functools.partial(join_kernel, width),
        out_shape=(
            jax.ShapeDtypeStruct((rows, feats), jnp.float32),
            jax.ShapeDtypeStruct((rows, feats + share.shape[1]), jnp.bfloat16),
        ),
        compiler_params=pltpu.CompilerParams(vmem_limit_bytes=16 * MIB),
        cost_estimate=pl.CostEstimate(
            flops=6 * rows * feats, bytes_accessed=12 * rows * feats, transcendentals=rows
        ),
        name="join",
    )(mine, other, residual, gain[None, :], share)


def cut_kernel(width, w_ref, *refs):
    outs, sems = refs[:-1], refs[-1]
    x = lax.axis_index("dp")
    units = w_ref.shape[2]
    low = x * (units - width)
    high = (1 - x) * (units - width)
    copies = []
    at = 0
    for i, out in enumerate(outs):
        start = pl.multiple_of(high if i > 0 else low, 128)
        source_at = 0 if i == 0 else at
        copy = pltpu.make_async_copy(
            w_ref.at[0, pl.ds(source_at, out.shape[0]), pl.ds(start, width)], out, sems.at[i]
        )
        copy.start()
        copies.append(copy)
        if i > 0:
            at += out.shape[0]
    for copy in copies:
        copy.wait()


def cut(weights, width, parts):
    depth = weights.shape[1]
    shapes = [depth] + list(parts)
    any_spec = pl.BlockSpec(memory_space=pl.ANY)
    return pl.pallas_call(
        functools.partial(cut_kernel, width),
        out_shape=tuple(jax.ShapeDtypeStruct((n, width), weights.dtype) for n in shapes),
        in_specs=[pl.BlockSpec(memory_space=pltpu.HBM)],
        out_specs=(pl.BlockSpec(memory_space=pltpu.VMEM),) * len(shapes),
        scratch_shapes=[pltpu.SemaphoreType.DMA((len(shapes),))],
        cost_estimate=pl.CostEstimate(
            flops=0, bytes_accessed=8 * depth * width, transcendentals=0
        ),
        compiler_params=pltpu.CompilerParams(vmem_limit_bytes=16 * MIB),
        name="cut",
    )(weights)


SLOTS = 3


def experts_kernel(tile, out_tile, first_row, count, split, *refs):
    per_expert = 6
    pieces, refs = refs[:count], refs[count:]
    weights, refs = refs[: 2 * per_expert], refs[2 * per_expert :]
    outs, refs = refs[:count], refs[count:]
    rows, share, gate, up, down, mid, row_sem, weight_sem, down_sem = refs
    x = lax.axis_index("dp")
    me = lax.axis_index("expert")
    feats = rows.shape[2]
    blocks, each = rows.shape[0], rows.shape[1]
    half = feats // 2
    width = down.shape[0] // 2
    tiles = width // tile
    near = pl.ds(pl.multiple_of(x * half, half), half)
    far = pl.ds(pl.multiple_of((1 - x) * half, half), half)
    taken = pl.ds(first_row, each)

    row_copies = []
    spans = []
    at = 0
    for i, piece in enumerate(pieces):
        part = piece.shape[0]
        spans.append((at * each, part * each))
        here = pl.ds(at, part)
        for s, (source, target) in enumerate(
            (
                (piece.at[:, taken, near], rows.at[here, :, pl.ds(0, half)]),
                (piece.at[:, taken, far], rows.at[here, :, pl.ds(half, half)]),
                (piece.at[:, taken, pl.ds(feats, 128)], share.at[here]),
            )
        ):
            copy = pltpu.make_async_copy(source, target, row_sem.at[3 * i + s])
            copy.start()
            row_copies.append(copy)
        at += part

    def fetch(t):
        e, j = t // tiles, t % tiles
        gate_own, gate_far, mixed, up_own, up_far, _ = weights[
            e * per_expert : (e + 1) * per_expert
        ]
        group = []
        sem = 6 * (t % SLOTS)
        gates = ((gate_own, 0), (gate_far, 0), (mixed, 0))
        ups = ((up_own, 0), (mixed, split), (up_far, 0))
        for sources, target in ((gates, gate), (ups, up)):
            depth_at = 0
            for source, start in sources:
                end = split if source is mixed and start == 0 else source.shape[0]
                copy = pltpu.make_async_copy(
                    source.at[pl.ds(start, end - start), pl.ds(j * tile, tile)],
                    target.at[t % SLOTS, pl.ds(depth_at, end - start), :],
                    weight_sem.at[sem],
                )
                copy.start()
                group.append(copy)
                depth_at += end - start
                sem += 1
        return group

    weight_copies = [fetch(t) for t in range(SLOTS)]
    units = weights[-1].shape[0]
    spare = width - units
    down_copies = []
    for e in range(2):
        start = pl.multiple_of(e * width + x * spare, 16)
        copy = pltpu.make_async_copy(
            weights[(e + 1) * per_expert - 1], down.at[pl.ds(start, units), :], down_sem.at[e]
        )
        copy.start()
        down_copies.append(copy)
        if spare:
            blank = pl.multiple_of(e * width + (1 - x) * units, 16)
            down[pl.ds(blank, spare), :] = jnp.zeros((spare, feats), down.dtype)

    for copy in row_copies:
        copy.wait()
    total_rows = blocks * each
    shares = share[...].reshape(total_rows, 128).astype(jnp.float32)
    lane = lax.broadcasted_iota(jnp.int32, (total_rows, 128), 1)
    experts = lax.axis_size("expert")

    def activate(t, g, u, scale):
        h = g / (1.0 + jnp.exp(-g)) * u * scale
        mid[:, pl.ds(t * tile, tile)] = h.astype(mid.dtype)

    pending = None
    for t in range(2 * tiles):
        e, j = t // tiles, t % tiles
        if j == 0:
            chosen = me if e == 0 else me + 1 - 2 * lax.rem(me, 2)
            hit = (lane == chosen) | (lane == chosen + experts)
            scale = jnp.sum(jnp.where(hit, shares, 0.0), axis=1, keepdims=True)
        for copy in weight_copies[t]:
            copy.wait()
        values = rows[...].reshape(total_rows, feats)
        g = jnp.dot(values, gate[t % SLOTS], preferred_element_type=jnp.float32)
        u = jnp.dot(values, up[t % SLOTS], preferred_element_type=jnp.float32)
        if pending is not None:
            activate(*pending)
        pending = (t, g, u, scale)
        if t + SLOTS < 2 * tiles:
            weight_copies.append(fetch(t + SLOTS))
    activate(*pending)
    for copy in down_copies:
        copy.wait()
    for n in range(feats // out_tile):
        lanes = pl.ds(n * out_tile, out_tile)
        total = jnp.dot(mid[...], down[:, lanes], preferred_element_type=jnp.float32)
        for (first, part), out in zip(spans, outs):
            out[:, lanes] = total[first : first + part].astype(out.dtype)


def run_experts(pieces, kinds, first_row, each, weights, split):
    feats = weights[-1].shape[1]
    width = weights[0].shape[1]
    count = len(pieces)
    blocks = sum(piece.shape[0] for piece in pieces)
    total = blocks * each
    tile = 256
    any_spec = pl.BlockSpec(memory_space=pl.ANY)
    vmem_spec = pl.BlockSpec(memory_space=pltpu.VMEM)
    return pl.pallas_call(
        functools.partial(experts_kernel, tile, 512, first_row, count, split),
        out_shape=tuple(
            jax.ShapeDtypeStruct((piece.shape[0] * each, feats), kind)
            for piece, kind in zip(pieces, kinds)
        ),
        in_specs=[any_spec] * (count + len(weights)),
        out_specs=(vmem_spec,) * count,
        scratch_shapes=[
            pltpu.VMEM((blocks, each, feats), jnp.bfloat16),
            pltpu.VMEM((blocks, each, 128), jnp.bfloat16),
            pltpu.VMEM((SLOTS, feats, tile), jnp.bfloat16),
            pltpu.VMEM((SLOTS, feats, tile), jnp.bfloat16),
            pltpu.VMEM((2 * width, feats), jnp.bfloat16),
            pltpu.VMEM((total, 2 * width), jnp.bfloat16),
            pltpu.SemaphoreType.DMA((3 * count,)),
            pltpu.SemaphoreType.DMA((SLOTS * 6,)),
            pltpu.SemaphoreType.DMA((2,)),
        ],
        compiler_params=pltpu.CompilerParams(vmem_limit_bytes=30 * MIB),
        cost_estimate=pl.CostEstimate(
            flops=2 * total * feats * width * 6,
            bytes_accessed=12 * feats * width + 12 * total * feats,
            transcendentals=total * width * 2,
        ),
        name="experts",
    )(*pieces, *weights)


def diagonal(line_x, line_y, depth):
    half = depth // 2
    return flip_y(line_x[:half], depth), flip_x(line_y[half:])


def send_line(full, depth):
    full = full.reshape(depth, -1, full.shape[1])
    total = full[0]
    for s in range(1, depth):
        back = shift_z(full[s].astype(jnp.bfloat16), depth, depth - s)
        total = total + back.astype(jnp.float32)
    return total


def gathered(
    queries,
    kv_pool,
    page_table,
    ctx_lens,
    w_out,
    residual,
    moe_gain,
    expert_ids,
    route_weights,
    w_gate,
    w_up,
    w_down,
    final_gain,
):
    experts = lax.axis_size("expert")
    depth = experts // 4
    feats = residual.shape[1]
    block = residual.shape[0]
    units_here = w_down.shape[1]
    width = -(-units_here // 256) * 256
    barrier = lax.optimization_barrier

    shifted = [shift_z(w_out, depth, s) for s in range(1, depth)]
    across = [flip_y(w_out, depth), flip_y(shifted[0], depth)]

    feats_here = w_gate.shape[1]
    early = feats_here * 3 // 4
    gate_own, *gate_sent = cut(w_gate, width, (early, feats_here - early))
    gate_far = flip_x(gate_sent[0])
    split = feats_here - early
    queries, gate_sent[1], gate_own = barrier((queries, gate_sent[1], gate_own))
    context = attend_here(queries, kv_pool, page_table, ctx_lens)
    context, w_up, w_down = barrier((context, w_up, w_down))
    early = feats_here * 7 // 32
    up_own, *up_sent = cut(w_up, width, (early, feats_here - early))
    mixed_sent = jnp.concatenate([gate_sent[1], up_sent[0]], axis=0)
    shifted, across, gate_far, mixed_sent, up_sent[1], gate_own, up_own, w_down, context = (
        barrier(
            (
                shifted,
                across,
                gate_far,
                mixed_sent,
                up_sent[1],
                gate_own,
                up_own,
                w_down,
                context,
            )
        )
    )
    across += [flip_y(piece, depth) for piece in shifted[1:]]
    mixed_far = flip_x(mixed_sent)
    other = flip_core(context, depth)
    down_own = w_down[0]
    here_core = [flip_core(array, depth) for array in (gate_own, up_own, down_own)]

    named = expert_ids[:, :, None] == jnp.arange(experts, dtype=jnp.int32)[None, None, :]
    share = jnp.sum(jnp.where(named, route_weights[:, :, None], 0.0), axis=1)
    share_high = share.astype(jnp.bfloat16)
    share_low = (share - share_high.astype(jnp.float32)).astype(jnp.bfloat16)
    share = jnp.concatenate(
        [share_high, share_low, jnp.zeros((block, 128 - 2 * experts), jnp.bfloat16)], axis=1
    )

    across, share, here_core, mixed_far = barrier((across, share, here_core, mixed_far))
    kept, sent = project(context, other, [w_out] + shifted + across, depth)
    gate_far_core = flip_core(gate_far, depth)
    mixed_far_core = flip_core(mixed_far, depth)
    received, up_late = barrier((flip_x(sent), up_sent[1]))
    up_far = flip_x(up_late)
    total = kept + received.astype(jnp.float32)
    back = flip_core(total[block:], depth)
    hidden_state, message = join(total[:block], back, residual, moe_gain, share, w_out.shape[1])

    rows = block // 2
    arrived = [message] + [shift_z(message, depth, s) for s in range(1, depth)]
    ready = []
    for k in range(2):
        line = jnp.stack([piece[rows * k : rows * (k + 1)] for piece in arrived])
        if k > 0:
            line, ready[0][3], ready[0][4] = barrier((line, ready[0][3], ready[0][4]))
        line_x = flip_x(line)
        line_y = flip_y(line, depth)
        if k == 0:
            line_x, line_y, up_far = barrier((line_x, line_y, up_far))
            ready.append([line, line_x, line_y, *diagonal(line_x, line_y, depth)])
        else:
            ready.append([line, line_x, line_y])

    weights = [gate_own, gate_far, mixed_far, up_own, up_far, down_own]
    weights += [
        here_core[0],
        gate_far_core,
        mixed_far_core,
        here_core[1],
        flip_core(up_far, depth),
        here_core[2],
    ]

    kinds = (jnp.float32, jnp.bfloat16, jnp.bfloat16, jnp.bfloat16, jnp.bfloat16)
    outs = run_experts(ready[0], kinds, 0, rows, weights, split)
    ready[1][1], ready[1][2], outs = barrier((ready[1][1], ready[1][2], outs))
    ready[1] += diagonal(ready[1][1], ready[1][2], depth)
    ready[1], outs = barrier((ready[1], outs))
    out_l, out_x, out_y, out_low, out_high = outs
    far = jnp.concatenate([out_low, out_high], axis=0)
    backs = [flip_x(out_x), flip_y(out_y, depth), flip_xy(far, depth)]

    kinds = (jnp.float32, jnp.float32, jnp.float32, jnp.bfloat16, jnp.bfloat16)
    last_l, last_x, last_y, last_low, last_high = run_experts(
        ready[1], kinds, 0, rows, weights, split
    )
    half = last_x.shape[0] // 2
    back_low, back_high = flip_y(last_low, depth), flip_x(last_high)
    plain_x = flip_x(last_x[half:].astype(jnp.bfloat16))
    plain_y = flip_y(last_y[:half].astype(jnp.bfloat16), depth)
    full = out_l
    for back in backs:
        full = full + back.astype(jnp.float32)
    first_rows = send_line(full, depth)
    back_low, back_high, plain_x, plain_y, _ = barrier(
        (back_low, back_high, plain_x, plain_y, full)
    )
    sum_x = last_x[:half] + back_low.astype(jnp.float32)
    sum_y = last_y[half:] + back_high.astype(jnp.float32)
    sum_x = flip_x(sum_x.astype(jnp.bfloat16))
    sum_y = flip_y(sum_y.astype(jnp.bfloat16), depth)
    full = (
        last_l
        + jnp.concatenate([sum_x, plain_x], axis=0).astype(jnp.float32)
        + jnp.concatenate([plain_y, sum_y], axis=0).astype(jnp.float32)
    )
    full, first_rows = barrier((full, first_rows))
    moe = [first_rows, send_line(full, depth)]
    combined = hidden_state + jnp.concatenate(moe, axis=0)
    return normalize(combined, final_gain).astype(jnp.bfloat16)


def solution(mesh):
    few = mesh.shape["dp"] == 2 and mesh.shape["expert"] == 16
    return jax.shard_map(
        gathered if few else dispatched,
        mesh=mesh,
        in_specs=(
            P("expert", "dp"),
            P(None, "expert", None, "dp"),
            P("expert", None),
            P("expert"),
            P("dp", "expert"),
            P(("expert", "dp"), None),
            P(),
            P(("expert", "dp"), None),
            P(("expert", "dp"), None),
            P("expert", "dp", None),
            P("expert", "dp", None),
            P("expert", "dp", None),
            P(),
        ),
        out_specs=P(("expert", "dp"), None),
        check_vma=False,
    )
```

```python
import functools
import math

import jax
import jax.numpy as jnp
from jax import lax
from jax.experimental import pallas as pl
from jax.experimental.pallas import tpu as pltpu
from jax.sharding import PartitionSpec as P

HD = 128
TOP = 6
CTX = 256
MIB = 1024 * 1024


def normalize(values, gain):
    mean_sq = jnp.mean(values * values, axis=-1, keepdims=True)
    return values * lax.rsqrt(mean_sq + 1e-06) * gain


def attend(queries, kv_pool, page_table, ctx_lens):
    scale = 1.0 / math.sqrt(HD)
    group_rows = queries.shape[0]
    local_feats = queries.shape[1]
    local_heads = local_feats // HD
    seq_count = page_table.shape[0]
    seq_rows = group_rows // seq_count
    pool_here = kv_pool.shape[1]
    local_pages = page_table - lax.axis_index("expert") * pool_here
    keys = kv_pool[0][local_pages].reshape(seq_count, CTX, local_heads, HD)
    values = kv_pool[1][local_pages].reshape(seq_count, CTX, local_heads, HD)
    asked = queries.reshape(seq_count, seq_rows, local_heads, HD)
    scores = jnp.einsum("sqhd,skhd->shqk", asked, keys, preferred_element_type=jnp.float32) * scale
    lengths = ctx_lens.reshape(seq_count, seq_rows)
    visible = (jnp.arange(CTX, dtype=jnp.int32)[None, None, :] < lengths[:, :, None])[:, None]
    scores = jnp.where(visible, scores, -1e30)
    top_score = jnp.max(scores, axis=-1, keepdims=True)
    expo = jnp.where(visible, jnp.exp(scores - top_score), 0.0)
    probs = (expo / jnp.sum(expo, axis=-1, keepdims=True)).astype(jnp.bfloat16)
    mixed = jnp.einsum("shqk,skhd->sqhd", probs, values, preferred_element_type=jnp.float32)
    return mixed.astype(jnp.bfloat16).reshape(group_rows, local_feats)


def dispatched(
    queries,
    kv_pool,
    page_table,
    ctx_lens,
    w_out,
    residual,
    moe_gain,
    expert_ids,
    route_weights,
    w_gate,
    w_up,
    w_down,
    final_gain,
):
    context = attend(queries, kv_pool, page_table, ctx_lens)
    columns = lax.all_gather(w_out, "expert", axis=1, tiled=True)
    projected = lax.psum_scatter(
        jnp.dot(context, columns, preferred_element_type=jnp.float32).astype(jnp.bfloat16),
        "dp",
        scatter_dimension=0,
        tiled=True,
    ).astype(jnp.float32)
    hidden_state = residual.astype(jnp.float32) + projected
    moe_input = normalize(hidden_state, moe_gain).astype(jnp.bfloat16)
    rows_here = moe_input.shape[0]
    experts = lax.axis_size("expert")
    slots = max(2, min(rows_here, 2 * rows_here * TOP // experts))
    flat_ids = expert_ids.reshape(-1)
    marks = (flat_ids[:, None] == jnp.arange(experts, dtype=jnp.int32)[None, :]).astype(jnp.int32)
    before = jnp.sum((jnp.cumsum(marks, axis=0) - 1) * marks, axis=1)
    target = (flat_ids * slots + before).reshape(rows_here, TOP)
    placing = jnp.any(
        jnp.arange(experts * slots, dtype=jnp.int32)[:, None, None] == target[None], axis=-1
    )
    outbound = jnp.dot(placing.astype(jnp.bfloat16), moe_input, preferred_element_type=jnp.float32)
    outbound = outbound.astype(jnp.bfloat16).reshape(experts, slots, moe_input.shape[1])
    gate_full = lax.all_gather(w_gate, "dp", axis=1, tiled=True)
    up_full = lax.all_gather(w_up, "dp", axis=1, tiled=True)
    down_full = lax.all_gather(w_down, "dp", axis=1, tiled=True)
    arrived = lax.all_to_all(outbound, "expert", split_axis=0, concat_axis=0, tiled=True)
    flat = arrived.reshape(-1, arrived.shape[2])
    gate = jnp.dot(flat, gate_full[0], preferred_element_type=jnp.float32)
    up_part = jnp.dot(flat, up_full[0], preferred_element_type=jnp.float32)
    expert_mid = (jax.nn.silu(gate) * up_part).astype(jnp.bfloat16)
    done = jnp.dot(expert_mid, down_full[0], preferred_element_type=jnp.float32).astype(
        jnp.bfloat16
    )
    done = done.reshape(arrived.shape[0], arrived.shape[1], arrived.shape[2])
    returned = lax.all_to_all(done, "expert", split_axis=0, concat_axis=0, tiled=True)
    answers = returned.reshape(experts * slots, returned.shape[2])[target]
    moe = jnp.sum(route_weights[:, :, None] * answers.astype(jnp.float32), axis=1)
    combined = hidden_state + moe
    return normalize(combined, final_gain).astype(jnp.bfloat16)


def place(z, y, c):
    return (z * 2 + y) * 2 + c


def shift_z(values, depth, step):
    pairs = [
        (place((z + step) % depth, y, c), place(z, y, c))
        for z in range(depth)
        for y in range(2)
        for c in range(2)
    ]
    return lax.ppermute(values, "expert", pairs)


def flip_y(values, depth):
    pairs = [
        (place(z, 1 - y, c), place(z, y, c))
        for z in range(depth)
        for y in range(2)
        for c in range(2)
    ]
    return lax.ppermute(values, "expert", pairs)


def flip_core(values, depth):
    pairs = [
        (place(z, y, 1 - c), place(z, y, c))
        for z in range(depth)
        for y in range(2)
        for c in range(2)
    ]
    return lax.ppermute(values, "expert", pairs)


def flip_x(values):
    return lax.ppermute(values, "dp", [(0, 1), (1, 0)])


def flip_xy(values, depth):
    pairs = [
        ((1 - x) * 4 * depth + place(z, 1 - y, c), x * 4 * depth + place(z, y, c))
        for x in range(2)
        for z in range(depth)
        for y in range(2)
        for c in range(2)
    ]
    return lax.ppermute(values, ("dp", "expert"), pairs)


def attend_kernel(pages_ref, lens_ref, q_ref, kv_ref, out_ref):
    scale = 1.0 / math.sqrt(HD)
    seqs, slots = pages_ref.shape
    rows, feats = q_ref.shape
    each = rows // seqs
    page = kv_ref.shape[2]
    first_page = lax.axis_index("expert") * kv_ref.shape[1]
    place_in = lax.broadcasted_iota(jnp.int32, (each, slots * page), 1)
    for s in range(seqs):
        here = slice(s * each, (s + 1) * each)
        pages = [pages_ref[s, p] - first_page for p in range(slots)]
        keys = jnp.concatenate([kv_ref[0, p] for p in pages], axis=0)
        values = jnp.concatenate([kv_ref[1, p] for p in pages], axis=0)
        visible = place_in < lens_ref[here, :]
        for h in range(feats // HD):
            lanes = slice(h * HD, (h + 1) * HD)
            scores = lax.dot_general(
                q_ref[here, lanes],
                keys[:, lanes],
                (((1,), (1,)), ((), ())),
                preferred_element_type=jnp.float32,
            )
            scores = jnp.where(visible, scores * scale, -1e30)
            top_score = jnp.max(scores, axis=-1, keepdims=True)
            expo = jnp.where(visible, jnp.exp(scores - top_score), 0.0)
            probs = (expo / jnp.sum(expo, axis=-1, keepdims=True)).astype(jnp.bfloat16)
            mixed = jnp.dot(probs, values[:, lanes], preferred_element_type=jnp.float32)
            out_ref[here, lanes] = mixed.astype(out_ref.dtype)


def attend_here(queries, kv_pool, page_table, ctx_lens):
    vmem_spec = pl.BlockSpec(memory_space=pltpu.VMEM)
    return pl.pallas_call(
        attend_kernel,
        out_shape=jax.ShapeDtypeStruct(queries.shape, jnp.bfloat16),
        in_specs=[pl.BlockSpec(memory_space=pltpu.SMEM)] + [vmem_spec] * 3,
        out_specs=vmem_spec,
        compiler_params=pltpu.CompilerParams(vmem_limit_bytes=16 * MIB),
        cost_estimate=pl.CostEstimate(
            flops=4 * queries.size * CTX,
            bytes_accessed=2 * kv_pool.size + 4 * queries.size,
            transcendentals=queries.size * CTX // HD,
        ),
        name="attend",
    )(page_table, ctx_lens[:, None], queries, kv_pool)


def project_kernel(depth, ctx_ref, other_ref, *refs):
    pieces, (kept_ref, sent_ref) = refs[:-2], refs[-2:]
    half = ctx_ref.shape[0] // 2
    width = pieces[0].shape[1]
    me = lax.axis_index("expert")
    x = lax.axis_index("dp")
    y = lax.rem(lax.div(me, 2), 2)
    z = lax.div(me, 4)
    mine = pl.ds(pl.multiple_of(x * half, half), half)
    theirs = pl.ds(pl.multiple_of((1 - x) * half, half), half)
    rows = jnp.concatenate(
        [ctx_ref[mine, :], other_ref[mine, :], ctx_ref[theirs, :], other_ref[theirs, :]], axis=0
    )
    for flip in range(2):
        at_y = y if flip == 0 else 1 - y
        for r in range(depth):
            piece = pieces[flip * depth + r][...]
            total = jnp.dot(rows, piece, preferred_element_type=jnp.float32)
            index = lax.rem(z + r, depth) * 2 + at_y
            columns = pl.ds(pl.multiple_of(index * width, width), width)
            kept_ref[:, columns] = total[: 2 * half]
            sent_ref[:, columns] = total[2 * half :].astype(sent_ref.dtype)


def project(context, other, pieces, depth):
    rows, feats = context.shape
    columns = pieces[0].shape[1] * 2 * depth
    return pl.pallas_call(
        functools.partial(project_kernel, depth),
        out_shape=(
            jax.ShapeDtypeStruct((rows, columns), jnp.float32),
            jax.ShapeDtypeStruct((rows, columns), jnp.bfloat16),
        ),
        compiler_params=pltpu.CompilerParams(vmem_limit_bytes=16 * MIB),
        cost_estimate=pl.CostEstimate(
            flops=4 * rows * feats * columns,
            bytes_accessed=2 * feats * columns + 6 * rows * columns,
            transcendentals=0,
        ),
        name="project",
    )(context, other, *pieces)


def join_kernel(width, mine_ref, other_ref, residual_ref, gain_ref, share_ref, hidden_ref, out_ref):
    c = lax.rem(lax.axis_index("expert"), 2)
    feats = residual_ref.shape[1]
    for i in range(feats // (2 * width)):
        source = slice(i * width, (i + 1) * width)
        for own, ref in ((True, mine_ref), (False, other_ref)):
            index = 2 * i + (c if own else 1 - c)
            columns = pl.ds(pl.multiple_of(index * width, width), width)
            hidden_ref[:, columns] = ref[:, source]
    hidden = residual_ref[...].astype(jnp.float32) + hidden_ref[...]
    hidden_ref[...] = hidden
    mean_sq = jnp.mean(hidden * hidden, axis=-1, keepdims=True)
    out_ref[:, :feats] = (hidden * lax.rsqrt(mean_sq + 1e-06) * gain_ref[...]).astype(
        out_ref.dtype
    )
    out_ref[:, feats:] = share_ref[...]


def join(mine, other, residual, gain, share, width):
    rows, feats = residual.shape
    return pl.pallas_call(
        functools.partial(join_kernel, width),
        out_shape=(
            jax.ShapeDtypeStruct((rows, feats), jnp.float32),
            jax.ShapeDtypeStruct((rows, feats + share.shape[1]), jnp.bfloat16),
        ),
        compiler_params=pltpu.CompilerParams(vmem_limit_bytes=16 * MIB),
        cost_estimate=pl.CostEstimate(
            flops=6 * rows * feats, bytes_accessed=12 * rows * feats, transcendentals=rows
        ),
        name="join",
    )(mine, other, residual, gain[None, :], share)


def cut_kernel(width, w_ref, *refs):
    outs, sems = refs[:-1], refs[-1]
    x = lax.axis_index("dp")
    units = w_ref.shape[2]
    low = x * (units - width)
    high = (1 - x) * (units - width)
    copies = []
    at = 0
    for i, out in enumerate(outs):
        start = pl.multiple_of(high if i > 0 else low, 128)
        source_at = 0 if i == 0 else at
        copy = pltpu.make_async_copy(
            w_ref.at[0, pl.ds(source_at, out.shape[0]), pl.ds(start, width)], out, sems.at[i]
        )
        copy.start()
        copies.append(copy)
        if i > 0:
            at += out.shape[0]
    for copy in copies:
        copy.wait()


def cut(weights, width, parts):
    depth = weights.shape[1]
    shapes = [depth] + list(parts)
    any_spec = pl.BlockSpec(memory_space=pl.ANY)
    return pl.pallas_call(
        functools.partial(cut_kernel, width),
        out_shape=tuple(jax.ShapeDtypeStruct((n, width), weights.dtype) for n in shapes),
        in_specs=[pl.BlockSpec(memory_space=pltpu.HBM)],
        out_specs=(pl.BlockSpec(memory_space=pltpu.VMEM),) * len(shapes),
        scratch_shapes=[pltpu.SemaphoreType.DMA((len(shapes),))],
        cost_estimate=pl.CostEstimate(
            flops=0, bytes_accessed=8 * depth * width, transcendentals=0
        ),
        compiler_params=pltpu.CompilerParams(vmem_limit_bytes=16 * MIB),
        name="cut",
    )(weights)


SLOTS = 3


def experts_kernel(tile, out_tile, first_row, count, split, *refs):
    per_expert = 6
    pieces, refs = refs[:count], refs[count:]
    weights, refs = refs[: 2 * per_expert], refs[2 * per_expert :]
    outs, refs = refs[:count], refs[count:]
    rows, share, gate, up, down, mid, row_sem, weight_sem, down_sem = refs
    x = lax.axis_index("dp")
    me = lax.axis_index("expert")
    feats = rows.shape[2]
    blocks, each = rows.shape[0], rows.shape[1]
    half = feats // 2
    width = down.shape[0] // 2
    tiles = width // tile
    near = pl.ds(pl.multiple_of(x * half, half), half)
    far = pl.ds(pl.multiple_of((1 - x) * half, half), half)
    taken = pl.ds(first_row, each)

    row_copies = []
    spans = []
    at = 0
    for i, piece in enumerate(pieces):
        part = piece.shape[0]
        spans.append((at * each, part * each))
        here = pl.ds(at, part)
        for s, (source, target) in enumerate(
            (
                (piece.at[:, taken, near], rows.at[here, :, pl.ds(0, half)]),
                (piece.at[:, taken, far], rows.at[here, :, pl.ds(half, half)]),
                (piece.at[:, taken, pl.ds(feats, 128)], share.at[here]),
            )
        ):
            copy = pltpu.make_async_copy(source, target, row_sem.at[3 * i + s])
            copy.start()
            row_copies.append(copy)
        at += part

    def fetch(t):
        e, j = t // tiles, t % tiles
        gate_own, gate_far, mixed, up_own, up_far, _ = weights[
            e * per_expert : (e + 1) * per_expert
        ]
        group = []
        sem = 6 * (t % SLOTS)
        gates = ((gate_own, 0), (gate_far, 0), (mixed, 0))
        ups = ((up_own, 0), (mixed, split), (up_far, 0))
        for sources, target in ((gates, gate), (ups, up)):
            depth_at = 0
            for source, start in sources:
                end = split if source is mixed and start == 0 else source.shape[0]
                copy = pltpu.make_async_copy(
                    source.at[pl.ds(start, end - start), pl.ds(j * tile, tile)],
                    target.at[t % SLOTS, pl.ds(depth_at, end - start), :],
                    weight_sem.at[sem],
                )
                copy.start()
                group.append(copy)
                depth_at += end - start
                sem += 1
        return group

    weight_copies = [fetch(t) for t in range(SLOTS)]
    units = weights[-1].shape[0]
    spare = width - units
    down_copies = []
    for e in range(2):
        start = pl.multiple_of(e * width + x * spare, 16)
        copy = pltpu.make_async_copy(
            weights[(e + 1) * per_expert - 1], down.at[pl.ds(start, units), :], down_sem.at[e]
        )
        copy.start()
        down_copies.append(copy)
        if spare:
            blank = pl.multiple_of(e * width + (1 - x) * units, 16)
            down[pl.ds(blank, spare), :] = jnp.zeros((spare, feats), down.dtype)

    for copy in row_copies:
        copy.wait()
    total_rows = blocks * each
    shares = share[...].reshape(total_rows, 128).astype(jnp.float32)
    lane = lax.broadcasted_iota(jnp.int32, (total_rows, 128), 1)
    experts = lax.axis_size("expert")
    for t in range(2 * tiles):
        e, j = t // tiles, t % tiles
        if j == 0:
            chosen = me if e == 0 else me + 1 - 2 * lax.rem(me, 2)
            hit = (lane == chosen) | (lane == chosen + experts)
            scale = jnp.sum(jnp.where(hit, shares, 0.0), axis=1, keepdims=True)
        for copy in weight_copies[t]:
            copy.wait()
        values = rows[...].reshape(total_rows, feats)
        g = jnp.dot(values, gate[t % SLOTS], preferred_element_type=jnp.float32)
        u = jnp.dot(values, up[t % SLOTS], preferred_element_type=jnp.float32)
        h = g / (1.0 + jnp.exp(-g)) * u * scale
        mid[:, pl.ds(t * tile, tile)] = h.astype(mid.dtype)
        if t + SLOTS < 2 * tiles:
            weight_copies.append(fetch(t + SLOTS))
    for copy in down_copies:
        copy.wait()
    for n in range(feats // out_tile):
        lanes = pl.ds(n * out_tile, out_tile)
        total = jnp.dot(mid[...], down[:, lanes], preferred_element_type=jnp.float32)
        for (first, part), out in zip(spans, outs):
            out[:, lanes] = total[first : first + part].astype(out.dtype)


def run_experts(pieces, kinds, first_row, each, weights, split):
    feats = weights[-1].shape[1]
    width = weights[0].shape[1]
    count = len(pieces)
    blocks = sum(piece.shape[0] for piece in pieces)
    total = blocks * each
    tile = 256
    any_spec = pl.BlockSpec(memory_space=pl.ANY)
    vmem_spec = pl.BlockSpec(memory_space=pltpu.VMEM)
    return pl.pallas_call(
        functools.partial(experts_kernel, tile, 512, first_row, count, split),
        out_shape=tuple(
            jax.ShapeDtypeStruct((piece.shape[0] * each, feats), kind)
            for piece, kind in zip(pieces, kinds)
        ),
        in_specs=[any_spec] * (count + len(weights)),
        out_specs=(vmem_spec,) * count,
        scratch_shapes=[
            pltpu.VMEM((blocks, each, feats), jnp.bfloat16),
            pltpu.VMEM((blocks, each, 128), jnp.bfloat16),
            pltpu.VMEM((SLOTS, feats, tile), jnp.bfloat16),
            pltpu.VMEM((SLOTS, feats, tile), jnp.bfloat16),
            pltpu.VMEM((2 * width, feats), jnp.bfloat16),
            pltpu.VMEM((total, 2 * width), jnp.bfloat16),
            pltpu.SemaphoreType.DMA((3 * count,)),
            pltpu.SemaphoreType.DMA((SLOTS * 6,)),
            pltpu.SemaphoreType.DMA((2,)),
        ],
        compiler_params=pltpu.CompilerParams(vmem_limit_bytes=30 * MIB),
        cost_estimate=pl.CostEstimate(
            flops=2 * total * feats * width * 6,
            bytes_accessed=12 * feats * width + 12 * total * feats,
            transcendentals=total * width * 2,
        ),
        name="experts",
    )(*pieces, *weights)


def send_line(full, depth):
    full = full.reshape(depth, -1, full.shape[1])
    total = full[0]
    for s in range(1, depth):
        back = shift_z(full[s].astype(jnp.bfloat16), depth, depth - s)
        total = total + back.astype(jnp.float32)
    return total


def gathered(
    queries,
    kv_pool,
    page_table,
    ctx_lens,
    w_out,
    residual,
    moe_gain,
    expert_ids,
    route_weights,
    w_gate,
    w_up,
    w_down,
    final_gain,
):
    experts = lax.axis_size("expert")
    depth = experts // 4
    feats = residual.shape[1]
    block = residual.shape[0]
    units_here = w_down.shape[1]
    width = -(-units_here // 256) * 256
    barrier = lax.optimization_barrier

    shifted = [shift_z(w_out, depth, s) for s in range(1, depth)]
    across = [flip_y(piece, depth) for piece in [w_out] + shifted[:-1]]

    feats_here = w_gate.shape[1]
    early = feats_here * 3 // 4
    gate_own, *gate_sent = cut(w_gate, width, (early, feats_here - early))
    gate_far = flip_x(gate_sent[0])
    split = feats_here - early
    queries, gate_sent[1], gate_own = barrier((queries, gate_sent[1], gate_own))
    context = attend_here(queries, kv_pool, page_table, ctx_lens)
    context, w_up, w_down = barrier((context, w_up, w_down))
    early = feats_here // 32
    up_own, *up_sent = cut(w_up, width, (early, feats_here - early))
    mixed_sent = jnp.concatenate([gate_sent[1], up_sent[0]], axis=0)
    shifted, across, gate_far, mixed_sent, up_sent[1], gate_own, up_own, w_down, context = (
        barrier(
            (
                shifted,
                across,
                gate_far,
                mixed_sent,
                up_sent[1],
                gate_own,
                up_own,
                w_down,
                context,
            )
        )
    )
    across.append(flip_y(shifted[-1], depth))
    mixed_far = flip_x(mixed_sent)
    other = flip_core(context, depth)
    down_own = w_down[0]
    here_core = [flip_core(array, depth) for array in (gate_own, up_own, down_own)]

    named = expert_ids[:, :, None] == jnp.arange(experts, dtype=jnp.int32)[None, None, :]
    share = jnp.sum(jnp.where(named, route_weights[:, :, None], 0.0), axis=1)
    share_high = share.astype(jnp.bfloat16)
    share_low = (share - share_high.astype(jnp.float32)).astype(jnp.bfloat16)
    share = jnp.concatenate(
        [share_high, share_low, jnp.zeros((block, 128 - 2 * experts), jnp.bfloat16)], axis=1
    )

    across, share, here_core, mixed_far = barrier((across, share, here_core, mixed_far))
    kept, sent = project(context, other, [w_out] + shifted + across, depth)
    gate_far_core = flip_core(gate_far, depth)
    mixed_far_core = flip_core(mixed_far, depth)
    received, up_late = barrier((flip_x(sent), up_sent[1]))
    up_far = flip_x(up_late)
    total = kept + received.astype(jnp.float32)
    back = flip_core(total[block:], depth)
    hidden_state, message = join(total[:block], back, residual, moe_gain, share, w_out.shape[1])

    rows = block // 2
    arrived = [message] + [shift_z(message, depth, s) for s in range(1, depth)]
    ready = []
    for k in range(2):
        line = jnp.stack([piece[rows * k : rows * (k + 1)] for piece in arrived])
        if k > 0:
            line, ready[0] = barrier((line, ready[0]))
        pieces = [line, flip_x(line), flip_y(line, depth), flip_xy(line, depth)]
        if k == 0:
            pieces, up_far = barrier((pieces, up_far))
        ready.append(pieces)

    weights = [gate_own, gate_far, mixed_far, up_own, up_far, down_own]
    weights += [
        here_core[0],
        gate_far_core,
        mixed_far_core,
        here_core[1],
        flip_core(up_far, depth),
        here_core[2],
    ]

    kinds = (jnp.float32, jnp.bfloat16, jnp.bfloat16, jnp.bfloat16)
    outs = run_experts(ready[0], kinds, 0, rows, weights, split)
    ready[1], outs = barrier((ready[1], outs))
    out_l, out_x, out_y, out_far = outs
    backs = [flip_x(out_x), flip_y(out_y, depth), flip_xy(out_far, depth)]

    kinds = (jnp.float32, jnp.float32, jnp.float32, jnp.bfloat16)
    last_l, last_x, last_y, last_far = run_experts(ready[1], kinds, 0, rows, weights, split)
    half = last_x.shape[0] // 2
    back_low, back_high = flip_y(last_far[:half], depth), flip_x(last_far[half:])
    plain_x = flip_x(last_x[half:].astype(jnp.bfloat16))
    plain_y = flip_y(last_y[:half].astype(jnp.bfloat16), depth)
    full = out_l
    for back in backs:
        full = full + back.astype(jnp.float32)
    first_rows = send_line(full, depth)
    back_low, back_high, plain_x, plain_y, _ = barrier(
        (back_low, back_high, plain_x, plain_y, full)
    )
    sum_x = last_x[:half] + back_low.astype(jnp.float32)
    sum_y = last_y[half:] + back_high.astype(jnp.float32)
    sum_x = flip_x(sum_x.astype(jnp.bfloat16))
    sum_y = flip_y(sum_y.astype(jnp.bfloat16), depth)
    full = (
        last_l
        + jnp.concatenate([sum_x, plain_x], axis=0).astype(jnp.float32)
        + jnp.concatenate([plain_y, sum_y], axis=0).astype(jnp.float32)
    )
    full, first_rows = barrier((full, first_rows))
    moe = [first_rows, send_line(full, depth)]
    combined = hidden_state + jnp.concatenate(moe, axis=0)
    return normalize(combined, final_gain).astype(jnp.bfloat16)


def solution(mesh):
    few = mesh.shape["dp"] == 2 and mesh.shape["expert"] == 16
    return jax.shard_map(
        gathered if few else dispatched,
        mesh=mesh,
        in_specs=(
            P("expert", "dp"),
            P(None, "expert", None, "dp"),
            P("expert", None),
            P("expert"),
            P("dp", "expert"),
            P(("expert", "dp"), None),
            P(),
            P(("expert", "dp"), None),
            P(("expert", "dp"), None),
            P("expert", "dp", None),
            P("expert", "dp", None),
            P("expert", "dp", None),
            P(),
        ),
        out_specs=P(("expert", "dp"), None),
        check_vma=False,
    )
```

```python
import functools
import math

import jax
import jax.numpy as jnp
from jax import lax
from jax.experimental import pallas as pl
from jax.experimental.pallas import tpu as pltpu
from jax.sharding import PartitionSpec as P

HD = 128
TOP = 6
CTX = 256
MIB = 1024 * 1024


def normalize(values, gain):
    mean_sq = jnp.mean(values * values, axis=-1, keepdims=True)
    return values * lax.rsqrt(mean_sq + 1e-06) * gain


def attend(queries, kv_pool, page_table, ctx_lens):
    scale = 1.0 / math.sqrt(HD)
    group_rows = queries.shape[0]
    local_feats = queries.shape[1]
    local_heads = local_feats // HD
    seq_count = page_table.shape[0]
    seq_rows = group_rows // seq_count
    pool_here = kv_pool.shape[1]
    local_pages = page_table - lax.axis_index("expert") * pool_here
    keys = kv_pool[0][local_pages].reshape(seq_count, CTX, local_heads, HD)
    values = kv_pool[1][local_pages].reshape(seq_count, CTX, local_heads, HD)
    asked = queries.reshape(seq_count, seq_rows, local_heads, HD)
    scores = jnp.einsum("sqhd,skhd->shqk", asked, keys, preferred_element_type=jnp.float32) * scale
    lengths = ctx_lens.reshape(seq_count, seq_rows)
    visible = (jnp.arange(CTX, dtype=jnp.int32)[None, None, :] < lengths[:, :, None])[:, None]
    scores = jnp.where(visible, scores, -1e30)
    top_score = jnp.max(scores, axis=-1, keepdims=True)
    expo = jnp.where(visible, jnp.exp(scores - top_score), 0.0)
    probs = (expo / jnp.sum(expo, axis=-1, keepdims=True)).astype(jnp.bfloat16)
    mixed = jnp.einsum("shqk,skhd->sqhd", probs, values, preferred_element_type=jnp.float32)
    return mixed.astype(jnp.bfloat16).reshape(group_rows, local_feats)


def dispatched(
    queries,
    kv_pool,
    page_table,
    ctx_lens,
    w_out,
    residual,
    moe_gain,
    expert_ids,
    route_weights,
    w_gate,
    w_up,
    w_down,
    final_gain,
):
    context = attend(queries, kv_pool, page_table, ctx_lens)
    columns = lax.all_gather(w_out, "expert", axis=1, tiled=True)
    projected = lax.psum_scatter(
        jnp.dot(context, columns, preferred_element_type=jnp.float32).astype(jnp.bfloat16),
        "dp",
        scatter_dimension=0,
        tiled=True,
    ).astype(jnp.float32)
    hidden_state = residual.astype(jnp.float32) + projected
    moe_input = normalize(hidden_state, moe_gain).astype(jnp.bfloat16)
    rows_here = moe_input.shape[0]
    experts = lax.axis_size("expert")
    slots = max(2, min(rows_here, 2 * rows_here * TOP // experts))
    flat_ids = expert_ids.reshape(-1)
    marks = (flat_ids[:, None] == jnp.arange(experts, dtype=jnp.int32)[None, :]).astype(jnp.int32)
    before = jnp.sum((jnp.cumsum(marks, axis=0) - 1) * marks, axis=1)
    target = (flat_ids * slots + before).reshape(rows_here, TOP)
    placing = jnp.any(
        jnp.arange(experts * slots, dtype=jnp.int32)[:, None, None] == target[None], axis=-1
    )
    outbound = jnp.dot(placing.astype(jnp.bfloat16), moe_input, preferred_element_type=jnp.float32)
    outbound = outbound.astype(jnp.bfloat16).reshape(experts, slots, moe_input.shape[1])
    gate_full = lax.all_gather(w_gate, "dp", axis=1, tiled=True)
    up_full = lax.all_gather(w_up, "dp", axis=1, tiled=True)
    down_full = lax.all_gather(w_down, "dp", axis=1, tiled=True)
    arrived = lax.all_to_all(outbound, "expert", split_axis=0, concat_axis=0, tiled=True)
    flat = arrived.reshape(-1, arrived.shape[2])
    gate = jnp.dot(flat, gate_full[0], preferred_element_type=jnp.float32)
    up_part = jnp.dot(flat, up_full[0], preferred_element_type=jnp.float32)
    expert_mid = (jax.nn.silu(gate) * up_part).astype(jnp.bfloat16)
    done = jnp.dot(expert_mid, down_full[0], preferred_element_type=jnp.float32).astype(
        jnp.bfloat16
    )
    done = done.reshape(arrived.shape[0], arrived.shape[1], arrived.shape[2])
    returned = lax.all_to_all(done, "expert", split_axis=0, concat_axis=0, tiled=True)
    answers = returned.reshape(experts * slots, returned.shape[2])[target]
    moe = jnp.sum(route_weights[:, :, None] * answers.astype(jnp.float32), axis=1)
    combined = hidden_state + moe
    return normalize(combined, final_gain).astype(jnp.bfloat16)


def place(z, y, c):
    return (z * 2 + y) * 2 + c


def shift_z(values, depth, step):
    pairs = [
        (place((z + step) % depth, y, c), place(z, y, c))
        for z in range(depth)
        for y in range(2)
        for c in range(2)
    ]
    return lax.ppermute(values, "expert", pairs)


def flip_y(values, depth):
    pairs = [
        (place(z, 1 - y, c), place(z, y, c))
        for z in range(depth)
        for y in range(2)
        for c in range(2)
    ]
    return lax.ppermute(values, "expert", pairs)


def flip_core(values, depth):
    pairs = [
        (place(z, y, 1 - c), place(z, y, c))
        for z in range(depth)
        for y in range(2)
        for c in range(2)
    ]
    return lax.ppermute(values, "expert", pairs)


def flip_x(values):
    return lax.ppermute(values, "dp", [(0, 1), (1, 0)])


def flip_xy(values, depth):
    pairs = [
        ((1 - x) * 4 * depth + place(z, 1 - y, c), x * 4 * depth + place(z, y, c))
        for x in range(2)
        for z in range(depth)
        for y in range(2)
        for c in range(2)
    ]
    return lax.ppermute(values, ("dp", "expert"), pairs)


def attend_kernel(pages_ref, lens_ref, q_ref, kv_ref, out_ref):
    scale = 1.0 / math.sqrt(HD)
    seqs, slots = pages_ref.shape
    rows, feats = q_ref.shape
    each = rows // seqs
    page = kv_ref.shape[2]
    first_page = lax.axis_index("expert") * kv_ref.shape[1]
    place_in = lax.broadcasted_iota(jnp.int32, (each, slots * page), 1)
    for s in range(seqs):
        here = slice(s * each, (s + 1) * each)
        pages = [pages_ref[s, p] - first_page for p in range(slots)]
        keys = jnp.concatenate([kv_ref[0, p] for p in pages], axis=0)
        values = jnp.concatenate([kv_ref[1, p] for p in pages], axis=0)
        visible = place_in < lens_ref[here, :]
        for h in range(feats // HD):
            lanes = slice(h * HD, (h + 1) * HD)
            scores = lax.dot_general(
                q_ref[here, lanes],
                keys[:, lanes],
                (((1,), (1,)), ((), ())),
                preferred_element_type=jnp.float32,
            )
            scores = jnp.where(visible, scores * scale, -1e30)
            top_score = jnp.max(scores, axis=-1, keepdims=True)
            expo = jnp.where(visible, jnp.exp(scores - top_score), 0.0)
            probs = (expo / jnp.sum(expo, axis=-1, keepdims=True)).astype(jnp.bfloat16)
            mixed = jnp.dot(probs, values[:, lanes], preferred_element_type=jnp.float32)
            out_ref[here, lanes] = mixed.astype(out_ref.dtype)


def attend_here(queries, kv_pool, page_table, ctx_lens):
    vmem_spec = pl.BlockSpec(memory_space=pltpu.VMEM)
    return pl.pallas_call(
        attend_kernel,
        out_shape=jax.ShapeDtypeStruct(queries.shape, jnp.bfloat16),
        in_specs=[pl.BlockSpec(memory_space=pltpu.SMEM)] + [vmem_spec] * 3,
        out_specs=vmem_spec,
        compiler_params=pltpu.CompilerParams(vmem_limit_bytes=16 * MIB),
        cost_estimate=pl.CostEstimate(
            flops=4 * queries.size * CTX,
            bytes_accessed=2 * kv_pool.size + 4 * queries.size,
            transcendentals=queries.size * CTX // HD,
        ),
        name="attend",
    )(page_table, ctx_lens[:, None], queries, kv_pool)


def project_kernel(depth, ctx_ref, other_ref, *refs):
    pieces, (kept_ref, sent_ref) = refs[:-2], refs[-2:]
    half = ctx_ref.shape[0] // 2
    width = pieces[0].shape[1]
    me = lax.axis_index("expert")
    x = lax.axis_index("dp")
    y = lax.rem(lax.div(me, 2), 2)
    z = lax.div(me, 4)
    mine = pl.ds(pl.multiple_of(x * half, half), half)
    theirs = pl.ds(pl.multiple_of((1 - x) * half, half), half)
    rows = jnp.concatenate(
        [ctx_ref[mine, :], other_ref[mine, :], ctx_ref[theirs, :], other_ref[theirs, :]], axis=0
    )
    for flip in range(2):
        at_y = y if flip == 0 else 1 - y
        for r in range(depth):
            piece = pieces[flip * depth + r][...]
            total = jnp.dot(rows, piece, preferred_element_type=jnp.float32)
            index = lax.rem(z + r, depth) * 2 + at_y
            columns = pl.ds(pl.multiple_of(index * width, width), width)
            kept_ref[:, columns] = total[: 2 * half]
            sent_ref[:, columns] = total[2 * half :].astype(sent_ref.dtype)


def project(context, other, pieces, depth):
    rows, feats = context.shape
    columns = pieces[0].shape[1] * 2 * depth
    return pl.pallas_call(
        functools.partial(project_kernel, depth),
        out_shape=(
            jax.ShapeDtypeStruct((rows, columns), jnp.float32),
            jax.ShapeDtypeStruct((rows, columns), jnp.bfloat16),
        ),
        compiler_params=pltpu.CompilerParams(vmem_limit_bytes=16 * MIB),
        cost_estimate=pl.CostEstimate(
            flops=4 * rows * feats * columns,
            bytes_accessed=2 * feats * columns + 6 * rows * columns,
            transcendentals=0,
        ),
        name="project",
    )(context, other, *pieces)


def join_kernel(width, mine_ref, other_ref, residual_ref, gain_ref, share_ref, hidden_ref, out_ref):
    c = lax.rem(lax.axis_index("expert"), 2)
    feats = residual_ref.shape[1]
    for i in range(feats // (2 * width)):
        source = slice(i * width, (i + 1) * width)
        for own, ref in ((True, mine_ref), (False, other_ref)):
            index = 2 * i + (c if own else 1 - c)
            columns = pl.ds(pl.multiple_of(index * width, width), width)
            hidden_ref[:, columns] = ref[:, source]
    hidden = residual_ref[...].astype(jnp.float32) + hidden_ref[...]
    hidden_ref[...] = hidden
    mean_sq = jnp.mean(hidden * hidden, axis=-1, keepdims=True)
    out_ref[:, :feats] = (hidden * lax.rsqrt(mean_sq + 1e-06) * gain_ref[...]).astype(
        out_ref.dtype
    )
    out_ref[:, feats:] = share_ref[...]


def join(mine, other, residual, gain, share, width):
    rows, feats = residual.shape
    return pl.pallas_call(
        functools.partial(join_kernel, width),
        out_shape=(
            jax.ShapeDtypeStruct((rows, feats), jnp.float32),
            jax.ShapeDtypeStruct((rows, feats + share.shape[1]), jnp.bfloat16),
        ),
        compiler_params=pltpu.CompilerParams(vmem_limit_bytes=16 * MIB),
        cost_estimate=pl.CostEstimate(
            flops=6 * rows * feats, bytes_accessed=12 * rows * feats, transcendentals=rows
        ),
        name="join",
    )(mine, other, residual, gain[None, :], share)


def cut_kernel(width, w_ref, *refs):
    outs, sems = refs[:-1], refs[-1]
    x = lax.axis_index("dp")
    units = w_ref.shape[2]
    low = x * (units - width)
    high = (1 - x) * (units - width)
    copies = []
    at = 0
    for i, out in enumerate(outs):
        start = pl.multiple_of(high if i > 0 else low, 128)
        source_at = 0 if i == 0 else at
        copy = pltpu.make_async_copy(
            w_ref.at[0, pl.ds(source_at, out.shape[0]), pl.ds(start, width)], out, sems.at[i]
        )
        copy.start()
        copies.append(copy)
        if i > 0:
            at += out.shape[0]
    for copy in copies:
        copy.wait()


def cut(weights, width, parts):
    depth = weights.shape[1]
    shapes = [depth] + list(parts)
    any_spec = pl.BlockSpec(memory_space=pl.ANY)
    return pl.pallas_call(
        functools.partial(cut_kernel, width),
        out_shape=tuple(jax.ShapeDtypeStruct((n, width), weights.dtype) for n in shapes),
        in_specs=[pl.BlockSpec(memory_space=pltpu.HBM)],
        out_specs=(pl.BlockSpec(memory_space=pltpu.VMEM),) * len(shapes),
        scratch_shapes=[pltpu.SemaphoreType.DMA((len(shapes),))],
        cost_estimate=pl.CostEstimate(
            flops=0, bytes_accessed=8 * depth * width, transcendentals=0
        ),
        compiler_params=pltpu.CompilerParams(vmem_limit_bytes=16 * MIB),
        name="cut",
    )(weights)


SLOTS = 3


def experts_kernel(tile, out_tile, first_row, count, split, *refs):
    per_expert = 6
    pieces, refs = refs[:count], refs[count:]
    weights, refs = refs[: 2 * per_expert], refs[2 * per_expert :]
    outs, refs = refs[:count], refs[count:]
    rows, share, gate, up, down, mid, row_sem, weight_sem, down_sem = refs
    x = lax.axis_index("dp")
    me = lax.axis_index("expert")
    feats = rows.shape[2]
    blocks, each = rows.shape[0], rows.shape[1]
    half = feats // 2
    width = down.shape[0] // 2
    tiles = width // tile
    near = pl.ds(pl.multiple_of(x * half, half), half)
    far = pl.ds(pl.multiple_of((1 - x) * half, half), half)
    taken = pl.ds(first_row, each)

    row_copies = []
    spans = []
    at = 0
    for i, piece in enumerate(pieces):
        part = piece.shape[0]
        spans.append((at * each, part * each))
        here = pl.ds(at, part)
        for s, (source, target) in enumerate(
            (
                (piece.at[:, taken, near], rows.at[here, :, pl.ds(0, half)]),
                (piece.at[:, taken, far], rows.at[here, :, pl.ds(half, half)]),
                (piece.at[:, taken, pl.ds(feats, 128)], share.at[here]),
            )
        ):
            copy = pltpu.make_async_copy(source, target, row_sem.at[3 * i + s])
            copy.start()
            row_copies.append(copy)
        at += part

    def fetch(t):
        e, j = t // tiles, t % tiles
        gate_own, gate_far, mixed, up_own, up_far, _ = weights[
            e * per_expert : (e + 1) * per_expert
        ]
        group = []
        sem = 6 * (t % SLOTS)
        gates = ((gate_own, 0), (gate_far, 0), (mixed, 0))
        ups = ((up_own, 0), (mixed, split), (up_far, 0))
        for sources, target in ((gates, gate), (ups, up)):
            depth_at = 0
            for source, start in sources:
                end = split if source is mixed and start == 0 else source.shape[0]
                copy = pltpu.make_async_copy(
                    source.at[pl.ds(start, end - start), pl.ds(j * tile, tile)],
                    target.at[t % SLOTS, pl.ds(depth_at, end - start), :],
                    weight_sem.at[sem],
                )
                copy.start()
                group.append(copy)
                depth_at += end - start
                sem += 1
        return group

    weight_copies = [fetch(t) for t in range(SLOTS)]
    units = weights[-1].shape[0]
    spare = width - units
    down_copies = []
    for e in range(2):
        start = pl.multiple_of(e * width + x * spare, 16)
        copy = pltpu.make_async_copy(
            weights[(e + 1) * per_expert - 1], down.at[pl.ds(start, units), :], down_sem.at[e]
        )
        copy.start()
        down_copies.append(copy)
        if spare:
            blank = pl.multiple_of(e * width + (1 - x) * units, 16)
            down[pl.ds(blank, spare), :] = jnp.zeros((spare, feats), down.dtype)

    for copy in row_copies:
        copy.wait()
    total_rows = blocks * each
    shares = share[...].reshape(total_rows, 128).astype(jnp.float32)
    lane = lax.broadcasted_iota(jnp.int32, (total_rows, 128), 1)
    experts = lax.axis_size("expert")
    for t in range(2 * tiles):
        e, j = t // tiles, t % tiles
        if j == 0:
            chosen = me if e == 0 else me + 1 - 2 * lax.rem(me, 2)
            hit = (lane == chosen) | (lane == chosen + experts)
            scale = jnp.sum(jnp.where(hit, shares, 0.0), axis=1, keepdims=True)
        for copy in weight_copies[t]:
            copy.wait()
        values = rows[...].reshape(total_rows, feats)
        g = jnp.dot(values, gate[t % SLOTS], preferred_element_type=jnp.float32)
        u = jnp.dot(values, up[t % SLOTS], preferred_element_type=jnp.float32)
        h = g / (1.0 + jnp.exp(-g)) * u * scale
        mid[:, pl.ds(t * tile, tile)] = h.astype(mid.dtype)
        if t + SLOTS < 2 * tiles:
            weight_copies.append(fetch(t + SLOTS))
    for copy in down_copies:
        copy.wait()
    for n in range(feats // out_tile):
        lanes = pl.ds(n * out_tile, out_tile)
        total = jnp.dot(mid[...], down[:, lanes], preferred_element_type=jnp.float32)
        for (first, part), out in zip(spans, outs):
            out[:, lanes] = total[first : first + part].astype(out.dtype)


def run_experts(pieces, kinds, first_row, each, weights, split):
    feats = weights[-1].shape[1]
    width = weights[0].shape[1]
    count = len(pieces)
    blocks = sum(piece.shape[0] for piece in pieces)
    total = blocks * each
    tile = 256
    any_spec = pl.BlockSpec(memory_space=pl.ANY)
    vmem_spec = pl.BlockSpec(memory_space=pltpu.VMEM)
    return pl.pallas_call(
        functools.partial(experts_kernel, tile, 512, first_row, count, split),
        out_shape=tuple(
            jax.ShapeDtypeStruct((piece.shape[0] * each, feats), kind)
            for piece, kind in zip(pieces, kinds)
        ),
        in_specs=[any_spec] * (count + len(weights)),
        out_specs=(vmem_spec,) * count,
        scratch_shapes=[
            pltpu.VMEM((blocks, each, feats), jnp.bfloat16),
            pltpu.VMEM((blocks, each, 128), jnp.bfloat16),
            pltpu.VMEM((SLOTS, feats, tile), jnp.bfloat16),
            pltpu.VMEM((SLOTS, feats, tile), jnp.bfloat16),
            pltpu.VMEM((2 * width, feats), jnp.bfloat16),
            pltpu.VMEM((total, 2 * width), jnp.bfloat16),
            pltpu.SemaphoreType.DMA((3 * count,)),
            pltpu.SemaphoreType.DMA((SLOTS * 6,)),
            pltpu.SemaphoreType.DMA((2,)),
        ],
        compiler_params=pltpu.CompilerParams(vmem_limit_bytes=30 * MIB),
        cost_estimate=pl.CostEstimate(
            flops=2 * total * feats * width * 6,
            bytes_accessed=12 * feats * width + 12 * total * feats,
            transcendentals=total * width * 2,
        ),
        name="experts",
    )(*pieces, *weights)


def diagonal(line_x, line_y, depth):
    half = depth // 2
    return flip_y(line_x[:half], depth), flip_x(line_y[half:])


def send_line(full, depth):
    full = full.reshape(depth, -1, full.shape[1])
    total = full[0]
    for s in range(1, depth):
        back = shift_z(full[s].astype(jnp.bfloat16), depth, depth - s)
        total = total + back.astype(jnp.float32)
    return total


def gathered(
    queries,
    kv_pool,
    page_table,
    ctx_lens,
    w_out,
    residual,
    moe_gain,
    expert_ids,
    route_weights,
    w_gate,
    w_up,
    w_down,
    final_gain,
):
    experts = lax.axis_size("expert")
    depth = experts // 4
    feats = residual.shape[1]
    block = residual.shape[0]
    units_here = w_down.shape[1]
    width = -(-units_here // 256) * 256
    barrier = lax.optimization_barrier

    shifted = [shift_z(w_out, depth, s) for s in range(1, depth)]
    across = [flip_y(w_out, depth), flip_y(shifted[0], depth)]

    feats_here = w_gate.shape[1]
    early = feats_here * 3 // 4
    gate_own, *gate_sent = cut(w_gate, width, (early, feats_here - early))
    gate_far = flip_x(gate_sent[0])
    split = feats_here - early
    queries, gate_sent[1], gate_own = barrier((queries, gate_sent[1], gate_own))
    context = attend_here(queries, kv_pool, page_table, ctx_lens)
    context, w_up, w_down = barrier((context, w_up, w_down))
    early = feats_here * 7 // 32
    up_own, *up_sent = cut(w_up, width, (early, feats_here - early))
    mixed_sent = jnp.concatenate([gate_sent[1], up_sent[0]], axis=0)
    shifted, across, gate_far, mixed_sent, up_sent[1], gate_own, up_own, w_down, context = (
        barrier(
            (
                shifted,
                across,
                gate_far,
                mixed_sent,
                up_sent[1],
                gate_own,
                up_own,
                w_down,
                context,
            )
        )
    )
    across += [flip_y(piece, depth) for piece in shifted[1:]]
    mixed_far = flip_x(mixed_sent)
    other = flip_core(context, depth)
    down_own = w_down[0]
    here_core = [flip_core(array, depth) for array in (gate_own, up_own, down_own)]

    named = expert_ids[:, :, None] == jnp.arange(experts, dtype=jnp.int32)[None, None, :]
    share = jnp.sum(jnp.where(named, route_weights[:, :, None], 0.0), axis=1)
    share_high = share.astype(jnp.bfloat16)
    share_low = (share - share_high.astype(jnp.float32)).astype(jnp.bfloat16)
    share = jnp.concatenate(
        [share_high, share_low, jnp.zeros((block, 128 - 2 * experts), jnp.bfloat16)], axis=1
    )

    across, share, here_core, mixed_far = barrier((across, share, here_core, mixed_far))
    kept, sent = project(context, other, [w_out] + shifted + across, depth)
    gate_far_core = flip_core(gate_far, depth)
    mixed_far_core = flip_core(mixed_far, depth)
    received, up_late = barrier((flip_x(sent), up_sent[1]))
    up_far = flip_x(up_late)
    total = kept + received.astype(jnp.float32)
    back = flip_core(total[block:], depth)
    hidden_state, message = join(total[:block], back, residual, moe_gain, share, w_out.shape[1])

    rows = block // 2
    arrived = [message] + [shift_z(message, depth, s) for s in range(1, depth)]
    ready = []
    for k in range(2):
        line = jnp.stack([piece[rows * k : rows * (k + 1)] for piece in arrived])
        if k > 0:
            line, ready[0][3], ready[0][4] = barrier((line, ready[0][3], ready[0][4]))
        line_x = flip_x(line)
        line_y = flip_y(line, depth)
        if k == 0:
            line_x, line_y, up_far = barrier((line_x, line_y, up_far))
            ready.append([line, line_x, line_y, *diagonal(line_x, line_y, depth)])
        else:
            ready.append([line, line_x, line_y])

    weights = [gate_own, gate_far, mixed_far, up_own, up_far, down_own]
    weights += [
        here_core[0],
        gate_far_core,
        mixed_far_core,
        here_core[1],
        flip_core(up_far, depth),
        here_core[2],
    ]

    kinds = (jnp.float32, jnp.bfloat16, jnp.bfloat16, jnp.bfloat16, jnp.bfloat16)
    outs = run_experts(ready[0], kinds, 0, rows, weights, split)
    ready[1][1], ready[1][2], outs = barrier((ready[1][1], ready[1][2], outs))
    ready[1] += diagonal(ready[1][1], ready[1][2], depth)
    ready[1], outs = barrier((ready[1], outs))
    out_l, out_x, out_y, out_low, out_high = outs
    far = jnp.concatenate([out_low, out_high], axis=0)
    backs = [flip_x(out_x), flip_y(out_y, depth), flip_xy(far, depth)]

    kinds = (jnp.float32, jnp.float32, jnp.float32, jnp.bfloat16, jnp.bfloat16)
    last_l, last_x, last_y, last_low, last_high = run_experts(
        ready[1], kinds, 0, rows, weights, split
    )
    half = last_x.shape[0] // 2
    back_low, back_high = flip_y(last_low, depth), flip_x(last_high)
    plain_x = flip_x(last_x[half:].astype(jnp.bfloat16))
    plain_y = flip_y(last_y[:half].astype(jnp.bfloat16), depth)
    full = out_l
    for back in backs:
        full = full + back.astype(jnp.float32)
    first_rows = send_line(full, depth)
    back_low, back_high, plain_x, plain_y, _ = barrier(
        (back_low, back_high, plain_x, plain_y, full)
    )
    sum_x = last_x[:half] + back_low.astype(jnp.float32)
    sum_y = last_y[half:] + back_high.astype(jnp.float32)
    sum_x = flip_x(sum_x.astype(jnp.bfloat16))
    sum_y = flip_y(sum_y.astype(jnp.bfloat16), depth)
    full = (
        last_l
        + jnp.concatenate([sum_x, plain_x], axis=0).astype(jnp.float32)
        + jnp.concatenate([plain_y, sum_y], axis=0).astype(jnp.float32)
    )
    full, first_rows = barrier((full, first_rows))
    moe = [first_rows, send_line(full, depth)]
    combined = hidden_state + jnp.concatenate(moe, axis=0)
    return normalize(combined, final_gain).astype(jnp.bfloat16)


def solution(mesh):
    few = mesh.shape["dp"] == 2 and mesh.shape["expert"] == 16
    return jax.shard_map(
        gathered if few else dispatched,
        mesh=mesh,
        in_specs=(
            P("expert", "dp"),
            P(None, "expert", None, "dp"),
            P("expert", None),
            P("expert"),
            P("dp", "expert"),
            P(("expert", "dp"), None),
            P(),
            P(("expert", "dp"), None),
            P(("expert", "dp"), None),
            P("expert", "dp", None),
            P("expert", "dp", None),
            P("expert", "dp", None),
            P(),
        ),
        out_specs=P(("expert", "dp"), None),
        check_vma=False,
    )
```
